32 devices in a mesh: dp: 8 (over z, y), seq: 4 (over x, core).
Axes of the slice: x: 2, y: 2, z: 4, core: 2. Of those that a mesh axis runs over, the one named last changes fastest.
Arguments:
- layer_input: bfloat16 [8, 1536, 1024], P('dp', 'seq'), may hold values from -6 to 6
- skip_input: bfloat16 [8, 1536, 1024], P('dp', 'seq'), may hold values from -6 to 6
- time_embed: bfloat16 [8, 1536, 1024], P('dp', 'seq'), may hold values from -6 to 6
- segment_ids: int32 [8, 1536], P('dp', 'seq'), may hold values from 0 to 2, as said below
- positions: int32 [8, 1536], P('dp', 'seq'), may hold values from 0 to 1535, as said below
- valid_mask: int32 [8, 1536], P('dp', 'seq'), may hold values from 0 to 1, as said below
- skip_weight: bfloat16 [2048, 1024], P(('dp', 'seq')), may hold values from -0.125 to 0.125
- time_weight: bfloat16 [1024, 5120], P(('dp', 'seq')), may hold values from -0.1875 to 0.1875
- query_weight: bfloat16 [1024, 1024], P(('dp', 'seq')), may hold values from -0.1875 to 0.1875
- key_weight: bfloat16 [1024, 1024], P(('dp', 'seq')), may hold values from -0.1875 to 0.1875
- value_weight: bfloat16 [1024, 1024], P(('dp', 'seq')), may hold values from -0.1875 to 0.1875
- out_weight: bfloat16 [1024, 1024], P(('dp', 'seq')), may hold values from -4 to 4
- up_weight: bfloat16 [1024, 4096], P(('dp', 'seq')), may hold values from -0.1875 to 0.1875
- down_weight: bfloat16 [4096, 1024], P(('dp', 'seq')), may hold values from -0.09375 to 0.09375
- cotangent: bfloat16 [8, 1536, 1024], P('dp', 'seq'), may hold values from -6 to 6
Outputs:
- output: bfloat16 [8, 1536, 1024], P('dp', 'seq')
- input_grad: float32 [8, 1536, 1024], P('dp', 'seq')
- skip_grad: float32 [8, 1536, 1024], P('dp', 'seq')
- time_grad: float32 [8, 1536, 1024], P('dp', 'seq')
- skip_weight_grad: float32 [2048, 1024], P(('dp', 'seq'))
- time_weight_grad: float32 [1024, 5120], P(('dp', 'seq'))
- query_weight_grad: float32 [1024, 1024], P(('dp', 'seq'))
- key_weight_grad: float32 [1024, 1024], P(('dp', 'seq'))
- value_weight_grad: float32 [1024, 1024], P(('dp', 'seq'))
- out_weight_grad: float32 [1024, 1024], P(('dp', 'seq'))
- up_weight_grad: float32 [1024, 4096], P(('dp', 'seq'))
- down_weight_grad: float32 [4096, 1024], P(('dp', 'seq'))
The draws below stay inside these ranges and needn't reach their ends.
Inputs may be any that keep to these rules, and one draw needn't show every extreme that they name: In each row, segment_ids is 0 before a cut among frames 1 to 191, 2 from a second cut onward and 1 between; the second cut lies after 3 * 384 frames, so utterance 1 spans all four shards of its row; padding frames carry 2. positions of real frames count frames from the first frame of their utterance; padding frames carry their index in the row, so the last frame of every row has 1535. valid_mask is 1 except on a tail of 1 to 191 frames of each row, which lies inside utterance 2 and leaves it at least one real frame.
All inputs are finite; a program needn't handle non-finite values.
Results may differ from the reference program's by a relative error of at most 0.02.
Values may be sent and summed in bfloat16 or wider, within the bound.
No kernel may reach another device: no remote copies, remote signals or barrier semaphores. Data moves between devices by JAX's collectives and lax.ppermute only.
A program may use at most 320 MiB of HBM per device.

```python
import jax
import jax.numpy as jnp
from jax import lax

D = 1024
HEADS = 16
HD = 64
FF = 4096
ROW_LEN = 1536
ROWS = 8


def row_cuts(key):
    eighth = max(ROW_LEN // 8, 2)
    key_pad, key_first, key_last = jax.random.split(key, 3)
    padding = jax.random.randint(key_pad, (ROWS, 1), 1, eighth, dtype=jnp.int32)
    valid_len = ROW_LEN - padding
    first_cut = jax.random.randint(key_first, (ROWS, 1), 1, eighth, dtype=jnp.int32)
    last_cut = valid_len - jax.random.randint(key_last, (ROWS, 1), 1, eighth, dtype=jnp.int32)
    frame = jnp.arange(ROW_LEN, dtype=jnp.int32)[None, :]
    after_first = (frame >= first_cut).astype(jnp.int32)
    after_last = (frame >= last_cut).astype(jnp.int32)
    segments = after_first + after_last
    starts = jnp.where(after_last > 0, last_cut, jnp.where(after_first > 0, first_cut, 0))
    real = frame < valid_len
    where = jnp.where(real, frame - starts, frame).astype(jnp.int32)
    valid = real.astype(jnp.int32)
    return (segments, where, valid)


def draw_segment_ids(key, part):
    return row_cuts(key)[0]


def draw_positions(key, part):
    return row_cuts(key)[1]


def draw_valid_mask(key, part):
    return row_cuts(key)[2]


def block_levels(key, shape, pieces, smallest, high):
    level = 1.0
    for position, parts in pieces:
        draws = jax.random.uniform(jax.random.fold_in(jax.random.fold_in(key, 6), position), (parts,), jnp.float32, smallest / len(pieces), high / len(pieces))
        level = level * jnp.repeat(jnp.exp(draws), shape[position] // parts).reshape((-1,) + (1,) * (len(shape) - 1 - position))
    return level


def bell_draw(key, shape, spread, most, shards=(), kind=jnp.bfloat16):
    gain = block_levels(key, shape, shards, -0.22, 0.18) if shards else 1.0
    result = jax.random.normal(key, shape, jnp.float32) * spread * gain
    return jnp.minimum(jnp.maximum(result, -most), most).astype(kind)


def setup_inputs(seed: int = 0) -> dict:
    key_list = jax.random.split(jax.random.key(seed), 16)
    return {
        "layer_input": bell_draw(key_list[0], (ROWS, ROW_LEN, D), 1.0, 6.0, ((0, 8), (1, 4))),
        "skip_input": bell_draw(key_list[1], (ROWS, ROW_LEN, D), 1.0, 6.0, ((0, 8), (1, 4))),
        "time_embed": bell_draw(key_list[2], (ROWS, ROW_LEN, D), 1.0, 6.0, ((0, 8), (1, 4))),
        "segment_ids": draw_segment_ids(jax.random.fold_in(key_list[15], 71), 0),
        "positions": draw_positions(jax.random.fold_in(key_list[15], 71), 0),
        "valid_mask": draw_valid_mask(jax.random.fold_in(key_list[15], 71), 0),
        "skip_weight": bell_draw(key_list[6], (2 * D, D), (2 * D) ** -0.5, 0.125, ((0, 32),)),
        "time_weight": bell_draw(key_list[7], (D, 5 * D), D ** -0.5, 0.1875, ((0, 32),)),
        "query_weight": bell_draw(key_list[8], (D, D), D ** -0.5, 0.1875, ((0, 32),)),
        "key_weight": bell_draw(key_list[9], (D, D), D ** -0.5, 0.1875, ((0, 32),)),
        "value_weight": bell_draw(key_list[10], (D, D), D ** -0.5, 0.1875, ((0, 32),)),
        "out_weight": bell_draw(key_list[11], (D, D), (max(D * 4 // ROW_LEN, 1)) ** -0.5, 4.0, ((0, 32),)),
        "up_weight": bell_draw(key_list[12], (D, FF), D ** -0.5, 0.1875, ((0, 32),)),
        "down_weight": bell_draw(key_list[13], (FF, D), FF ** -0.5, 0.09375, ((0, 32),)),
        "cotangent": bell_draw(key_list[14], (ROWS, ROW_LEN, D), 1.0, 6.0, ((0, 8), (1, 4))),
    }


norm_eps = 1e-06
gelu_coef = 0.7978845608028654
highest = lax.Precision.HIGHEST

@jax.custom_vjp
def low(v):
    return lax.optimization_barrier(v.astype(jnp.bfloat16)).astype(jnp.float32)

@jax.custom_vjp
def low_back(v):
    return v

def low_keep(v):
    return (low(v), None)

def low_pass(kept, grad):
    return (grad,)

def back_keep(v):
    return (v, None)

def back_low(kept, grad):
    return (low(grad),)
low.defvjp(low_keep, low_pass)
low_back.defvjp(back_keep, back_low)

def matmul(left, right):
    return jnp.dot(left, right, precision=highest)

def silu_value(v):
    return v * jax.nn.sigmoid(v)

def gelu_value(u):
    return 0.5 * u * (1.0 + jnp.tanh(gelu_coef * (u + 0.044715 * u * u * u)))

def norm_rows(v):
    mean = lax.optimization_barrier(jnp.mean(v, axis=-1, keepdims=True))
    centred = v - mean
    return centred * lax.rsqrt(lax.optimization_barrier(jnp.mean(centred * centred, axis=-1, keepdims=True)) + norm_eps)

def angle_tables(where, half):
    freq = 10000.0 ** (-jnp.arange(half, dtype=jnp.float32) / half)
    angle = where.astype(jnp.float32)[..., None] * freq
    return (jnp.cos(angle)[..., None, :], jnp.sin(angle)[..., None, :])

def rotate(v, cosine, sine):
    half = v.shape[-1] // 2
    first = v[..., :half]
    second = v[..., half:]
    return jnp.concatenate([first * cosine - second * sine, second * cosine + first * sine], axis=-1)

def attention(query_rot, key_rot, values, seg, valid):
    length = query_rot.shape[0]
    block = min(512, length)
    count = length // block
    scale = HD ** (-0.5)

    def one_block(args):
        query_block, seg_block = args
        scores = low_back(jnp.einsum('qhd,khd->hqk', query_block, key_rot, precision=highest) * scale)
        allowed = (seg_block[:, None] == seg[None, :]) & (valid[None, :] > 0)
        scores = jnp.where(allowed[None], scores, -1e+30)
        top = lax.optimization_barrier(jnp.max(scores, axis=-1, keepdims=True))
        expo = jnp.exp(scores - top)
        probs = expo / lax.optimization_barrier(jnp.sum(expo, axis=-1, keepdims=True))
        return jnp.einsum('hqk,khd->qhd', low(probs), values, precision=highest)
    outs = lax.map(jax.checkpoint(one_block), (query_rot.reshape(count, block, HEADS, HD), seg.reshape(count, block)))
    return outs.reshape(length, HEADS * HD)

def row_forward(params, layer_in, skip_in, time_in, seg, pos, valid):
    skip_w, time_w, query_w, key_w, value_w, out_w, up_w, down_w = params
    length = layer_in.shape[0]
    joined = jnp.concatenate([layer_in, skip_in], axis=1)
    base = low_back(matmul(joined, skip_w))
    time_act = low(silu_value(time_in))
    modul = low_back(matmul(time_act, time_w))
    shift_a, scale_a, shift_b, scale_b, gate_b = jnp.split(modul, 5, axis=1)
    hidden_a = low(norm_rows(base) * (1.0 + scale_a) + shift_a)
    query = low_back(low(matmul(hidden_a, query_w))).reshape(length, HEADS, HD)
    keys = low_back(low(matmul(hidden_a, key_w))).reshape(length, HEADS, HD)
    values = low_back(low(matmul(hidden_a, value_w))).reshape(length, HEADS, HD)
    cosine, sine = angle_tables(pos, HD // 2)
    query_rot = low(rotate(query, cosine, sine))
    key_rot = low(rotate(keys, cosine, sine))
    attended = low_back(low(attention(query_rot, key_rot, values, seg, valid)))
    middle = base + low_back(matmul(attended, out_w))
    hidden_b = low(norm_rows(middle) * (1.0 + scale_b) + shift_b)
    upper = low_back(matmul(hidden_b, up_w))
    acted = low(gelu_value(upper))
    ffn = low_back(matmul(acted, down_w))
    return middle + gate_b * ffn

def reference(layer_input, skip_input, time_embed, segment_ids, positions, valid_mask, skip_weight, time_weight, query_weight, key_weight, value_weight, out_weight, up_weight, down_weight, cotangent):
    weights = (skip_weight.astype(jnp.float32), time_weight.astype(jnp.float32), query_weight.astype(jnp.float32), key_weight.astype(jnp.float32), value_weight.astype(jnp.float32), out_weight.astype(jnp.float32), up_weight.astype(jnp.float32), down_weight.astype(jnp.float32))

    def step(totals, row):
        x_row, skip_row, time_row, seg_row, pos_row, valid_row, cot_row = row

        def forward(params, first, second, third):
            return row_forward(params, first, second, third, seg_row, pos_row, valid_row)
        out_row, pullback = jax.vjp(forward, weights, x_row.astype(jnp.float32), skip_row.astype(jnp.float32), time_row.astype(jnp.float32))
        grad_params, grad_first, grad_second, grad_third = pullback(cot_row.astype(jnp.float32))
        totals = tuple((total + grad for total, grad in zip(totals, grad_params)))
        return (totals, (out_row.astype(jnp.bfloat16), grad_first, grad_second, grad_third))
    zeros = tuple((jnp.zeros(weight.shape, jnp.float32) for weight in weights))
    totals, outs = lax.scan(step, zeros, (layer_input, skip_input, time_embed, segment_ids, positions, valid_mask, cotangent))
    return (outs[0], outs[1], outs[2], outs[3], totals[0], totals[1], totals[2], totals[3], totals[4], totals[5], totals[6], totals[7])
```

```python
import functools

import jax
import jax.numpy as jnp
from jax import lax
from jax.experimental import pallas as pl
from jax.experimental.pallas import tpu as pltpu
from jax.sharding import PartitionSpec as P

HD = 64
NEG = 1e30
norm_eps = 1e-06
gelu_coef = 0.7978845608028654
f32, bf16 = jnp.float32, jnp.bfloat16

RING = (0, 2, 4, 6, 7, 5, 3, 1)
PLACE = tuple(RING.index(d) for d in range(8))


def dot_nt(a, b):
    return lax.dot_general(a, b, (((1,), (1,)), ((), ())), preferred_element_type=f32)


def dot_nn(a, b):
    return lax.dot_general(a, b, (((1,), (0,)), ((), ())), preferred_element_type=f32)


def dot_tn(a, b):
    return lax.dot_general(a, b, (((0,), (0,)), ((), ())), preferred_element_type=f32)


def silu_slope(v):
    sig = jax.nn.sigmoid(v)
    return sig * (1.0 + v * (1.0 - sig))


def gelu_value(u):
    return 0.5 * u * (1.0 + jnp.tanh(gelu_coef * (u + 0.044715 * u * u * u)))


def gelu_slope(u):
    inner = jnp.tanh(gelu_coef * (u + 0.044715 * u * u * u))
    return 0.5 * (1.0 + inner) + 0.5 * u * (1.0 - inner * inner) * gelu_coef * (
        1.0 + 3.0 * 0.044715 * u * u
    )


def norm_rows(v):
    mean = jnp.mean(v, axis=-1, keepdims=True)
    centred = v - mean
    inverse = lax.rsqrt(jnp.mean(centred * centred, axis=-1, keepdims=True) + norm_eps)
    return (centred * inverse, inverse)


def norm_back(grad, normed, inverse):
    return inverse * (
        grad
        - jnp.mean(grad, axis=-1, keepdims=True)
        - normed * jnp.mean(grad * normed, axis=-1, keepdims=True)
    )

def lanes_of(shape):
    return lax.broadcasted_iota(jnp.int32, shape, 1)


def swap_halves(v):
    lane = lanes_of(v.shape)
    return jnp.where(lane % HD < HD // 2, pltpu.roll(v, 128 - HD // 2, 1), pltpu.roll(v, HD // 2, 1))


def three_parts(v):
    hi = v.astype(bf16)
    rest = v - hi.astype(f32)
    mid = rest.astype(bf16)
    low = (rest - mid.astype(f32)).astype(bf16)
    return hi, mid, low


def attend_kernel(pieces, block, scale, *refs):
    qkv = refs[:pieces]
    cos_ref, sin_ref, qext_ref, kext_ref = refs[pieces : pieces + 4]
    att_ref, lse_ref, qrot_ref, krot_ref = refs[pieces + 4 : pieces + 8]
    kx, vx = refs[pieces + 8 :]
    pair, step = pl.program_id(0), pl.program_id(1)
    frames = qkv[0].shape[0]
    per_piece = frames // block

    @pl.when(step == 0)
    def _():
        for j in range(pieces):
            rows = pl.ds(j * frames, frames)
            k = qkv[j][:, pl.ds(pl.multiple_of(256 + pair * 128, 128), 128)].astype(f32)
            k = (k * cos_ref[rows, :] + swap_halves(k) * sin_ref[rows, :]).astype(bf16)
            krot_ref[rows, :] = k
            v = qkv[j][:, pl.ds(pl.multiple_of(512 + pair * 128, 128), 128)]
            ext = kext_ref[rows, :]
            lane = lanes_of(k.shape)
            one = jnp.where(lane % HD == 0, 1.0, 0.0).astype(bf16)
            low_lane = lane < HD
            kx[0, rows, :] = jnp.where(low_lane, k, ext)
            kx[1, rows, :] = jnp.where(low_lane, ext, k)
            vx[0, rows, :] = jnp.where(low_lane, v, one)
            vx[1, rows, :] = jnp.where(low_lane, one, v)

    rows = pl.ds(pl.multiple_of(step * block, block), block)
    for j in range(pieces):

        @pl.when(step // per_piece == j)
        def _(j=j):
            sub = pl.ds(pl.multiple_of((step - j * per_piece) * block, block), block)
            q = qkv[j][sub, pl.ds(pl.multiple_of(pair * 128, 128), 128)].astype(f32)
            q = (q * cos_ref[rows, :] + swap_halves(q) * sin_ref[rows, :]).astype(bf16)
            qrot_ref[...] = (q.astype(f32) * scale).astype(bf16)

    q = qrot_ref[...]
    ext = qext_ref[rows, :]
    low_lane = lanes_of(q.shape) < HD
    outs = []
    for h in range(2):
        qx = jnp.where(low_lane, q, ext) if h == 0 else jnp.where(low_lane, ext, q)
        scores = dot_nt(qx, kx[h])
        top = jnp.max(scores, axis=1, keepdims=True)
        expo = jnp.exp(scores - top)
        mixed = dot_nn(expo.astype(bf16), vx[h])
        total = mixed[:, HD : HD + 1] if h == 0 else mixed[:, 0:1]
        outs.append((mixed / total, top + jnp.log(total)))
    low_out = lanes_of((block, 128)) < HD
    att_ref[...] = jnp.where(low_out, outs[0][0], outs[1][0]).astype(bf16)
    lse_ref[...] = jnp.where(low_out, outs[0][1], outs[1][1])


def attend(qkv, cosine, sine, qext, kext, block=384, scale=HD**-0.5):
    pieces = len(qkv)
    total = pieces * qkv[0].shape[0]
    whole = lambda p, i: (0, 0)
    full = lambda a: pl.BlockSpec(a.shape, whole)
    tile = pl.BlockSpec((block, 128), lambda p, i: (i, p))
    column = pl.BlockSpec((total, 128), lambda p, i: (0, p))
    return pl.pallas_call(
        functools.partial(attend_kernel, pieces, block, scale),
        grid=(2, total // block),
        in_specs=[full(a) for a in (*qkv, cosine, sine, qext, kext)],
        out_specs=[tile, tile, tile, column],
        out_shape=[
            jax.ShapeDtypeStruct((total, 256), bf16),
            jax.ShapeDtypeStruct((total, 256), f32),
            jax.ShapeDtypeStruct((total, 256), bf16),
            jax.ShapeDtypeStruct((total, 256), bf16),
        ],
        scratch_shapes=[pltpu.VMEM((2, total, 128), bf16), pltpu.VMEM((2, total, 128), bf16)],
        compiler_params=pltpu.CompilerParams(vmem_limit_bytes=48 * 2**20),
        cost_estimate=pl.CostEstimate(
            flops=4 * total * total * 512, bytes_accessed=total * 4096, transcendentals=4 * total * total
        ),
        name="attend",
    )(*qkv, cosine, sine, qext, kext)


def attend_back_kernel(pieces, block, scale, *refs):
    grads = refs[:pieces]
    values = refs[pieces : 2 * pieces]
    qrot_ref, krot_ref, att_ref, lse_ref, cos_ref, sin_ref, qext_ref, kext_ref = refs[2 * pieces : 2 * pieces + 8]
    out_ref = refs[2 * pieces + 8]
    qx, gx, qm, gm, dq = refs[2 * pieces + 9 :]
    pair, step = pl.program_id(0), pl.program_id(1)
    last = pl.num_programs(1) - 1
    frames = grads[0].shape[0]
    per_piece = frames // block

    @pl.when(step == 0)
    def _():
        for j in range(pieces):
            rows = pl.ds(j * frames, frames)
            q = qrot_ref[rows, :]
            g = grads[j][:, pl.ds(pl.multiple_of(pair * 128, 128), 128)]
            lane = lanes_of(q.shape)
            low_lane = lane < HD
            spot = lane % HD
            prod = g.astype(f32) * att_ref[rows, :].astype(f32)
            zero = jnp.zeros_like(q)
            lse = lse_ref[rows, :]
            for h in range(2):
                own = low_lane if h == 0 else jnp.logical_not(low_lane)
                lse_h = lse[:, 0:1] if h == 0 else lse[:, HD : HD + 1]
                delta = jnp.sum(jnp.where(own, prod, 0.0), axis=1, keepdims=True)
                a, b, c = (t.astype(f32) for t in three_parts(-lse_h))
                part = jnp.where(spot == 4, a, jnp.where(spot == 5, b, jnp.where(spot == 6, c, qext_ref[rows, :].astype(f32))))
                qx[h, rows, :] = jnp.where(own, q, part.astype(bf16))
                a, b, c = (t.astype(f32) for t in three_parts(-delta))
                part = jnp.where(spot == 0, a, jnp.where(spot == 1, b, jnp.where(spot == 2, c, 0.0)))
                gx[h, rows, :] = jnp.where(own, g, part.astype(bf16))
                qm[h, rows, :] = jnp.where(own, q, zero)
                gm[h, rows, :] = jnp.where(own, g, zero)
        dq[...] = jnp.zeros_like(dq)

    rows = pl.ds(pl.multiple_of(step * block, block), block)
    for j in range(pieces):

        @pl.when(step // per_piece == j)
        def _(j=j):
            sub = pl.ds(pl.multiple_of((step - j * per_piece) * block, block), block)
            k = krot_ref[rows, :]
            v = values[j][sub, pl.ds(pl.multiple_of(512 + pair * 128, 128), 128)]
            ext = kext_ref[rows, :]
            lane = lanes_of(k.shape)
            low_lane = lane < HD
            three = jnp.where(lane % HD < 3, 1.0, 0.0).astype(bf16)
            zero = jnp.zeros_like(k)
            small = k.astype(f32) * scale
            dk = jnp.zeros((block, 128), f32)
            dv = jnp.zeros((block, 128), f32)
            for h in range(2):
                own = low_lane if h == 0 else jnp.logical_not(low_lane)
                kx = jnp.where(own, k, ext)
                vx = jnp.where(own, v, three)
                probs = jnp.exp(dot_nt(kx, qx[h]))
                grad = (probs * dot_nt(vx, gx[h])).astype(bf16)
                dv = dv + dot_nn(probs.astype(bf16), gm[h])
                dk = dk + dot_nn(grad, qm[h])
                turned = jnp.transpose(jnp.where(own, small, 0.0)).astype(bf16)
                dq[...] += dot_nn(turned, grad)
            dk = dk * cos_ref[rows, :] - swap_halves(dk) * sin_ref[rows, :]
            out_ref[rows, pl.ds(pl.multiple_of(256 + pair * 128, 128), 128)] = dk.astype(bf16)
            out_ref[rows, pl.ds(pl.multiple_of(512 + pair * 128, 128), 128)] = dv.astype(bf16)

    @pl.when(step == last)
    def _():
        g = jnp.transpose(dq[...])
        g = g * cos_ref[...] - swap_halves(g) * sin_ref[...]
        out_ref[:, pl.ds(pl.multiple_of(pair * 128, 128), 128)] = g.astype(bf16)


def attend_back(grads, qkv, qrot, krot, att, lse, cosine, sine, qext, kext, block=384, scale=HD**-0.5):
    pieces = len(grads)
    total = pieces * grads[0].shape[0]
    whole = lambda p, i: (0, 0)
    full = lambda a: pl.BlockSpec(a.shape, whole)
    column = pl.BlockSpec((total, 128), lambda p, i: (0, p))
    return pl.pallas_call(
        functools.partial(attend_back_kernel, pieces, block, scale),
        grid=(2, total // block),
        in_specs=[full(a) for a in (*grads, *qkv)] + [column] * 4 + [full(a) for a in (cosine, sine, qext, kext)],
        out_specs=pl.BlockSpec((total, 768), whole),
        out_shape=jax.ShapeDtypeStruct((total, 768), bf16),
        scratch_shapes=[pltpu.VMEM((2, total, 128), bf16)] * 4 + [pltpu.VMEM((128, total), f32)],
        compiler_params=pltpu.CompilerParams(vmem_limit_bytes=56 * 2**20),
        cost_estimate=pl.CostEstimate(
            flops=10 * total * total * 512, bytes_accessed=total * 8192, transcendentals=4 * total * total
        ),
        name="attend_back",
    )(*grads, *qkv, qrot, krot, att, lse, cosine, sine, qext, kext)


def frame_tables(seg, pos, valid):
    half = HD // 2
    freq = 10000.0 ** (-jnp.arange(half, dtype=f32) / half)
    angle = pos.astype(f32)[:, None] * freq
    cosine, sine = jnp.cos(angle), jnp.sin(angle)
    cosine = jnp.concatenate([cosine] * 4, axis=1)
    sine = jnp.concatenate([-sine, sine, -sine, sine], axis=1)
    spot = jnp.arange(128)[None, :] % HD
    seg, valid = seg[:, None], valid[:, None] > 0
    qext = jnp.where((spot < 3) & (spot != seg) | (spot == 3), -NEG, 0.0).astype(bf16)
    kext = ((spot == seg) & (spot < 3) | (spot == 3) & ~valid | (spot >= 4) & (spot < 7)).astype(bf16)
    return cosine, sine, qext, kext


def swap(v, mask):
    return lax.ppermute(v, "seq", [(i, i ^ mask) for i in range(4)])


def spread(v):
    near = swap(v, 1)
    far = swap(v, 2)
    return [v, near, far, swap(far, 1)]


def collect(parts):
    low = [part.astype(bf16) for part in parts]
    far_near = swap(low[3], 1)
    near = swap(low[1], 1)
    far = swap((low[2].astype(f32) + far_near.astype(f32)).astype(bf16), 2)
    return parts[0] + near.astype(f32) + far.astype(f32)


def exchange(parts):
    return [parts[0], swap(parts[1], 1), swap(parts[2], 2), swap(parts[3], 3)]


def by_place(parts, me):
    odd, high = (me & 1) == 1, (me & 2) == 2
    parts = [jnp.where(odd, parts[t ^ 1], parts[t]) for t in range(4)]
    return [jnp.where(high, parts[t ^ 2], parts[t]) for t in range(4)]


def ring_step(v, step):
    return lax.ppermute(v, "dp", [(RING[i], RING[(i + step) % 8]) for i in range(8)])


def ring_gather(v, way):
    found = [None] * 8
    found[0] = one = other = v
    for k in range(1, 5):
        one = ring_step(one, way)
        found[(way * k) % 8] = one
        if k < 4:
            other = ring_step(other, -way)
            found[(-way * k) % 8] = other
    return found


def ring_scatter(v, place, way):
    order = jnp.asarray(RING, jnp.int32)

    def block(k):
        return lax.dynamic_index_in_dim(v, order[(place + way * k) % 8], 0, keepdims=False)

    one, other = block(4), block(-3)
    for k in range(3, -1, -1):
        one = ring_step(one, way)
        if k > 0:
            one = (one.astype(f32) + block(k).astype(f32)).astype(bf16)
    for k in range(2, -1, -1):
        other = ring_step(other, -way)
        if k > 0:
            other = (other.astype(f32) + block(-k).astype(f32)).astype(bf16)
    return block(0).astype(f32) + one.astype(f32) + other.astype(f32)


def after(v, *others):
    return lax.optimization_barrier((v, *others))[0]


def assemble_kernel(copies, n_in, n_out, index_ref, *refs):
    arrays, outs, sems = refs[:n_in], refs[n_in : n_in + n_out], refs[-1]
    moves = []
    me = index_ref[8]
    for number, (a, row, count, out, k, j, per_dp, per_seq, column) in enumerate(copies):
        start = index_ref[k] * per_dp + jnp.bitwise_xor(me, j) * per_seq
        target = outs[out].at[
            pl.ds(pl.multiple_of(start, count), count), pl.ds(column, arrays[a].shape[1])
        ]
        moves.append(
            pltpu.make_async_copy(arrays[a].at[pl.ds(row, count), :], target, sems.at[number])
        )
    for move in moves:
        move.start()
    for move in moves:
        move.wait()


def assemble(index, arrays, copies, shapes):
    anywhere = pl.BlockSpec(memory_space=pl.ANY)
    return pl.pallas_call(
        functools.partial(assemble_kernel, tuple(copies), len(arrays), len(shapes)),
        grid_spec=pltpu.PrefetchScalarGridSpec(
            num_scalar_prefetch=1,
            grid=(1,),
            in_specs=[anywhere] * len(arrays),
            out_specs=[anywhere] * len(shapes),
            scratch_shapes=[pltpu.SemaphoreType.DMA((len(copies),))],
        ),
        out_shape=[jax.ShapeDtypeStruct(shape, bf16) for shape in shapes],
        name="assemble",
    )(index, *arrays)


class Gather:
    def __init__(self, index):
        self.index, self.arrays, self.copies, self.shapes = index, [], [], []

    def out(self, rows, columns):
        self.shapes.append((rows, columns))
        return len(self.shapes) - 1

    def add(self, piece, k, blocks):
        self.arrays.append(piece)
        for row, count, out, j, per_dp, per_seq, column in blocks:
            self.copies.append(
                (len(self.arrays) - 1, row, count, out, k, j, per_dp, per_seq, column)
            )

    def run(self):
        return assemble(self.index, self.arrays, self.copies, self.shapes)


def scatter_full(grad, me, place, groups, way):
    rows, columns = grad.shape
    if groups != 8:
        low = grad.astype(bf16).reshape(groups * 4, rows // (groups * 4), columns)
        return lax.psum_scatter(low, ("dp", "seq"), scatter_dimension=0).astype(f32)
    low = grad.astype(bf16).reshape(groups, 2, 2, rows // (groups * 4), columns)
    odd, high = (me & 1) == 1, (me & 2) == 2
    keep = jnp.where(odd, low[:, :, 1], low[:, :, 0])
    send = jnp.where(odd, low[:, :, 0], low[:, :, 1])
    both = (keep.astype(f32) + swap(send, 1).astype(f32)).astype(bf16)
    mine = ring_scatter(both, place, way)
    keep = jnp.where(high, mine[1], mine[0])
    send = jnp.where(high, mine[0], mine[1]).astype(bf16)
    return keep + swap(send, 2).astype(f32)


def scatter_dp(grad, place, groups, way):
    low = grad.astype(bf16)
    if groups != 8:
        return lax.psum_scatter(low, "dp", scatter_dimension=0).astype(f32)
    return ring_scatter(low, place, way)


def to_rows(block, me):
    rows = block.shape[0] // 4
    low = block.astype(bf16)
    parts = by_place([low[t * rows : (t + 1) * rows] for t in range(4)], me)
    return by_place(exchange(parts), me)


def on_device(
    layer_input,
    skip_input,
    time_embed,
    segment_ids,
    positions,
    valid_mask,
    skip_weight,
    time_weight,
    query_weight,
    key_weight,
    value_weight,
    out_weight,
    up_weight,
    down_weight,
    cotangent,
):
    rows, frames, width = layer_input.shape
    hidden = up_weight.shape[1]
    groups = lax.axis_size("dp")
    me, dp = lax.axis_index("seq"), lax.axis_index("dp")
    local = width // 4
    local_hidden = hidden // 4

    triple = jnp.stack(
        [w.reshape(-1, 4, local) for w in (query_weight, key_weight, value_weight)], axis=2
    )
    triple = triple.reshape(-1, 4, 3 * local)
    upper_w = up_weight.reshape(-1, groups, 4, hidden // (groups * 4)).transpose(0, 2, 1, 3)
    upper_w = upper_w.reshape(-1, 4, local_hidden)
    qkv_parts = exchange(by_place([triple[:, t] for t in range(4)], me))
    up_parts = exchange(by_place([upper_w[:, t] for t in range(4)], me))

    time_a, time_b = time_weight[:, : 2 * width], time_weight[:, 2 * width :]
    if groups == 8:
        place = jnp.asarray(PLACE, jnp.int32)[dp]
        order = jnp.asarray(RING, jnp.int32)[(place - jnp.arange(8)) % 8]
        index = jnp.concatenate([order, me[None].astype(jnp.int32)])
        n_skip, n_time, n_out = skip_weight.shape[0], time_weight.shape[0], out_weight.shape[0]

        def full_piece(gather, piece, k, j, layout):
            near = swap(piece, 1)
            for array, jj in ((piece, j), (near, j ^ 1)):
                gather.add(
                    array,
                    k,
                    [(row, count, out, jj, 4 * count, count, column) for row, count, out, column in layout],
                )

        first = Gather(index)
        o_skip, o_time_a = first.out(32 * n_skip, width), first.out(32 * n_time, 2 * width)
        own = jnp.concatenate([skip_weight, time_a[:, :width], time_a[:, width:]], axis=0)
        layout = [
            (0, n_skip, o_skip, 0),
            (n_skip, n_time, o_time_a, 0),
            (n_skip + n_time, n_time, o_time_a, width),
        ]
        found_own, found_far = ring_gather(own, 1), ring_gather(swap(own, 2), -1)
        for k in range(8):
            full_piece(first, found_own[k], k, 0, layout)
            full_piece(first, found_far[k], k, 2, layout)
        skip_full, time_a_full = first.run()

        second = Gather(index)
        o_triple, o_out = second.out(width, 3 * local), second.out(width, width)
        triple_own = jnp.concatenate(qkv_parts, axis=0)
        out_own = jnp.concatenate([out_weight, swap(out_weight, 2)], axis=0)
        triple_own, out_own = after(
            (triple_own, out_own), found_own[4], found_far[4], found_own[5], found_far[3]
        )
        found_triple, found_out = ring_gather(triple_own, 1), ring_gather(out_own, -1)
        n_triple = query_weight.shape[0]
        for k in range(8):
            second.add(
                found_triple[k],
                k,
                [(j * n_triple, n_triple, o_triple, j, 4 * n_triple, n_triple, 0) for j in range(4)],
            )
            near = swap(found_out[k], 1)
            for array, flip in ((found_out[k], 0), (near, 1)):
                second.add(
                    array,
                    k,
                    [(jj * n_out, n_out, o_out, (2 * jj) ^ flip, 4 * n_out, n_out, 0) for jj in range(2)],
                )
        triple_full, out_full = second.run()

        third = Gather(index)
        o_up, o_down = third.out(width, local_hidden), third.out(local_hidden, width)
        o_time_b = third.out(32 * n_time, 3 * width)
        up_own = jnp.concatenate(up_parts, axis=0)
        down_own, time_own = down_weight, time_b
        up_own, down_own, time_own, time_far = after(
            (up_own, down_own, time_own, swap(time_b, 2)),
            found_triple[4],
            found_out[4],
            found_triple[5],
            found_out[3],
        )
        found_up, found_down = ring_gather(up_own, 1), ring_gather(down_own, -1)
        found_own, found_far = ring_gather(time_own, 1), ring_gather(time_far, -1)
        n_up, n_down = up_weight.shape[0], down_weight.shape[0]
        for k in range(8):
            third.add(
                found_up[k], k, [(j * n_up, n_up, o_up, j, 4 * n_up, n_up, 0) for j in range(4)]
            )
            third.add(found_down[k], k, [(0, n_down, o_down, 0, n_down, 0, 0)])
            full_piece(third, found_own[k], k, 0, [(0, n_time, o_time_b, 0)])
            full_piece(third, found_far[k], k, 2, [(0, n_time, o_time_b, 0)])
        up_full, down_full, time_b_full = third.run()
    else:
        place = dp
        skip_full, time_a_full, time_b_full, out_full = (
            lax.all_gather(w, ("dp", "seq"), axis=0, tiled=True)
            for w in (skip_weight, time_a, time_b, out_weight)
        )
        triple_full, up_full = (
            lax.all_gather(jnp.concatenate(by_place(parts, me), axis=0), "dp", axis=0, tiled=True)
            for parts in (qkv_parts, up_parts)
        )
        down_full = lax.all_gather(down_weight, "dp", axis=0, tiled=True)

    marks = jnp.concatenate(spread(jnp.concatenate([segment_ids, positions, valid_mask])), axis=1)
    cosine, sine, query_marks, key_marks = frame_tables(marks[0], marks[1], marks[2])
    first_in, second_in = layer_input.reshape(frames, width), skip_input.reshape(frames, width)
    joined = jnp.concatenate([first_in, second_in], axis=1)
    base = dot_nn(joined, skip_full)
    time_value = time_embed.reshape(frames, width).astype(f32)
    time_act = (time_value * jax.nn.sigmoid(time_value)).astype(bf16)
    shift_a, scale_a = jnp.split(dot_nn(time_act, time_a_full), 2, axis=1)
    normed_a, inverse_a = norm_rows(base)
    hidden_a = spread((normed_a * (1.0 + scale_a) + shift_a).astype(bf16))
    qkv = [dot_nn(h, triple_full).astype(bf16) for h in hidden_a]
    att, logsum, query_rot, key_rot = attend(qkv, cosine, sine, query_marks, key_marks)
    attended = jnp.concatenate(
        by_place(exchange([att[j * frames : (j + 1) * frames] for j in range(4)]), me), axis=1
    )

    shift_b, scale_b, gate_b = jnp.split(dot_nn(time_act, time_b_full), 3, axis=1)
    upstream = cotangent.reshape(frames, width).astype(f32)
    ffn_grad = spread((upstream * gate_b).astype(bf16))
    middle = base + dot_nn(attended, out_full)
    normed_b, inverse_b = norm_rows(middle)
    hidden_b = spread((normed_b * (1.0 + scale_b) + shift_b).astype(bf16))
    hb = [jnp.concatenate(hidden_b[:2]), jnp.concatenate(hidden_b[2:])]
    fg = [jnp.concatenate(ffn_grad[:2]), jnp.concatenate(ffn_grad[2:])]
    upper = [dot_nn(h, up_full) for h in hb]
    acted = [gelu_value(u).astype(bf16) for u in upper]
    ug = [(dot_nt(g, down_full) * gelu_slope(u)).astype(bf16) for g, u in zip(fg, upper)]
    back = [dot_nt(u, up_full) for u in ug]
    hidden_b_grad = collect(
        [back[0][:frames], back[0][frames:], back[1][:frames], back[1][frames:]]
    )
    part = [dot_nn(a, down_full) for a in acted]
    ffn = collect([part[0][:frames], part[0][frames:], part[1][:frames], part[1][frames:]])
    grad_down = dot_tn(acted[0], fg[0]) + dot_tn(acted[1], fg[1])
    grad_up = dot_tn(hb[0], ug[0]) + dot_tn(hb[1], ug[1])
    output = (middle + gate_b * ffn).astype(bf16).reshape(rows, frames, width)
    gate_b_grad = upstream * ffn

    scale_b_grad = hidden_b_grad * normed_b
    middle_grad = upstream + norm_back(hidden_b_grad * (1.0 + scale_b), normed_b, inverse_b)
    branch_grad = middle_grad.astype(bf16)
    attended_grad = dot_nt(branch_grad, out_full).astype(bf16)
    att_grad = exchange(
        by_place([attended_grad[:, t * local : (t + 1) * local] for t in range(4)], me)
    )
    grad_out = dot_tn(attended, branch_grad)
    modul_b_grad = jnp.concatenate([hidden_b_grad, scale_b_grad, gate_b_grad], axis=1).astype(bf16)
    grad_time_b = dot_tn(time_act, modul_b_grad)
    time_back_b = dot_nt(modul_b_grad, time_b_full)
    triple_grad = attend_back(
        att_grad, qkv, query_rot, key_rot, att, logsum, cosine, sine, query_marks, key_marks
    )
    back = dot_nt(triple_grad, triple_full)
    hidden_a_grad = collect([back[j * frames : (j + 1) * frames] for j in range(4)])
    grad_triple = dot_tn(jnp.concatenate(hidden_a), triple_grad)

    scale_a_grad = hidden_a_grad * normed_a
    base_grad = (
        middle_grad + norm_back(hidden_a_grad * (1.0 + scale_a), normed_a, inverse_a)
    ).astype(bf16)
    grad_skip = dot_tn(joined, base_grad)
    joined_grad = dot_nt(base_grad, skip_full)
    modul_a_grad = jnp.concatenate([hidden_a_grad, scale_a_grad], axis=1).astype(bf16)
    grad_time_a = dot_tn(time_act, modul_a_grad)
    time_back = dot_nt(modul_a_grad, time_a_full) + time_back_b
    time_grad = (time_back * silu_slope(time_value)).reshape(rows, frames, width)

    by_dp = lambda grad: grad.reshape(groups, grad.shape[0] // groups, grad.shape[1])
    down_sum = scatter_dp(by_dp(grad_down), place, groups, 1)
    up_sum = to_rows(scatter_dp(by_dp(grad_up), place, groups, -1), me)
    up_sum = jnp.stack(
        [u.reshape(-1, groups, hidden // (groups * 4)) for u in up_sum], axis=2
    ).reshape(-1, hidden)
    out_sum = scatter_full(grad_out, me, place, groups, 1)
    time_b_sum = scatter_full(grad_time_b, me, place, groups, -1)
    qkv_sum = to_rows(scatter_dp(by_dp(grad_triple), place, groups, 1), me)
    qkv_sum = [
        jnp.concatenate([q[:, i * local : (i + 1) * local] for q in qkv_sum], axis=1)
        for i in range(3)
    ]
    skip_sum = scatter_full(grad_skip, me, place, groups, 1)
    time_a_sum = scatter_full(grad_time_a, me, place, groups, -1)
    return (
        output,
        joined_grad[:, :width].reshape(rows, frames, width),
        joined_grad[:, width:].reshape(rows, frames, width),
        time_grad,
        skip_sum,
        jnp.concatenate([time_a_sum, time_b_sum], axis=1),
        qkv_sum[0].astype(f32),
        qkv_sum[1].astype(f32),
        qkv_sum[2].astype(f32),
        out_sum,
        up_sum.astype(f32),
        down_sum,
    )


def solution(mesh):
    frames = P("dp", "seq", None)
    marks = P("dp", "seq")
    weight = P(("dp", "seq"), None)
    return jax.shard_map(
        on_device,
        mesh=mesh,
        in_specs=(frames,) * 3 + (marks,) * 3 + (weight,) * 8 + (frames,),
        out_specs=(frames,) * 4 + (weight,) * 8,
        check_vma=False,
    )
```

```python
import functools

import jax
import jax.numpy as jnp
from jax import lax
from jax.experimental import pallas as pl
from jax.experimental.pallas import tpu as pltpu
from jax.sharding import PartitionSpec as P

HD = 64
NEG = 1e30
norm_eps = 1e-06
gelu_coef = 0.7978845608028654
f32, bf16 = jnp.float32, jnp.bfloat16

RING = (0, 2, 4, 6, 7, 5, 3, 1)
PLACE = tuple(RING.index(d) for d in range(8))


def dot_nt(a, b):
    return lax.dot_general(a, b, (((1,), (1,)), ((), ())), preferred_element_type=f32)


def dot_nn(a, b):
    return lax.dot_general(a, b, (((1,), (0,)), ((), ())), preferred_element_type=f32)


def dot_tn(a, b):
    return lax.dot_general(a, b, (((0,), (0,)), ((), ())), preferred_element_type=f32)


def silu_slope(v):
    sig = jax.nn.sigmoid(v)
    return sig * (1.0 + v * (1.0 - sig))


def gelu_value(u):
    return 0.5 * u * (1.0 + jnp.tanh(gelu_coef * (u + 0.044715 * u * u * u)))


def gelu_slope(u):
    inner = jnp.tanh(gelu_coef * (u + 0.044715 * u * u * u))
    return 0.5 * (1.0 + inner) + 0.5 * u * (1.0 - inner * inner) * gelu_coef * (
        1.0 + 3.0 * 0.044715 * u * u
    )


def norm_rows(v):
    mean = jnp.mean(v, axis=-1, keepdims=True)
    centred = v - mean
    inverse = lax.rsqrt(jnp.mean(centred * centred, axis=-1, keepdims=True) + norm_eps)
    return (centred * inverse, inverse)


def norm_back(grad, normed, inverse):
    return inverse * (
        grad
        - jnp.mean(grad, axis=-1, keepdims=True)
        - normed * jnp.mean(grad * normed, axis=-1, keepdims=True)
    )

def lanes_of(shape):
    return lax.broadcasted_iota(jnp.int32, shape, 1)


def swap_halves(v):
    lane = lanes_of(v.shape)
    return jnp.where(lane % HD < HD // 2, pltpu.roll(v, 128 - HD // 2, 1), pltpu.roll(v, HD // 2, 1))


def three_parts(v):
    hi = v.astype(bf16)
    rest = v - hi.astype(f32)
    mid = rest.astype(bf16)
    low = (rest - mid.astype(f32)).astype(bf16)
    return hi, mid, low


def attend_kernel(pieces, block, scale, *refs):
    qkv = refs[:pieces]
    cos_ref, sin_ref, qext_ref, kext_ref = refs[pieces : pieces + 4]
    att_ref, lse_ref, qrot_ref, krot_ref = refs[pieces + 4 : pieces + 8]
    kx, vx = refs[pieces + 8 :]
    pair, step = pl.program_id(0), pl.program_id(1)
    frames = qkv[0].shape[0]
    per_piece = frames // block

    @pl.when(step == 0)
    def _():
        for j in range(pieces):
            rows = pl.ds(j * frames, frames)
            k = qkv[j][:, pl.ds(pl.multiple_of(256 + pair * 128, 128), 128)].astype(f32)
            k = (k * cos_ref[rows, :] + swap_halves(k) * sin_ref[rows, :]).astype(bf16)
            krot_ref[rows, :] = k
            v = qkv[j][:, pl.ds(pl.multiple_of(512 + pair * 128, 128), 128)]
            ext = kext_ref[rows, :]
            lane = lanes_of(k.shape)
            one = jnp.where(lane % HD == 0, 1.0, 0.0).astype(bf16)
            low_lane = lane < HD
            kx[0, rows, :] = jnp.where(low_lane, k, ext)
            kx[1, rows, :] = jnp.where(low_lane, ext, k)
            vx[0, rows, :] = jnp.where(low_lane, v, one)
            vx[1, rows, :] = jnp.where(low_lane, one, v)

    rows = pl.ds(pl.multiple_of(step * block, block), block)
    for j in range(pieces):

        @pl.when(step // per_piece == j)
        def _(j=j):
            sub = pl.ds(pl.multiple_of((step - j * per_piece) * block, block), block)
            q = qkv[j][sub, pl.ds(pl.multiple_of(pair * 128, 128), 128)].astype(f32)
            q = (q * cos_ref[rows, :] + swap_halves(q) * sin_ref[rows, :]).astype(bf16)
            qrot_ref[...] = (q.astype(f32) * scale).astype(bf16)

    q = qrot_ref[...]
    ext = qext_ref[rows, :]
    low_lane = lanes_of(q.shape) < HD
    outs = []
    for h in range(2):
        qx = jnp.where(low_lane, q, ext) if h == 0 else jnp.where(low_lane, ext, q)
        scores = dot_nt(qx, kx[h])
        top = jnp.max(scores, axis=1, keepdims=True)
        expo = jnp.exp(scores - top)
        mixed = dot_nn(expo.astype(bf16), vx[h])
        total = mixed[:, HD : HD + 1] if h == 0 else mixed[:, 0:1]
        outs.append((mixed / total, top + jnp.log(total)))
    low_out = lanes_of((block, 128)) < HD
    att_ref[...] = jnp.where(low_out, outs[0][0], outs[1][0]).astype(bf16)
    lse_ref[...] = jnp.where(low_out, outs[0][1], outs[1][1])


def attend(qkv, cosine, sine, qext, kext, block=384, scale=HD**-0.5):
    pieces = len(qkv)
    total = pieces * qkv[0].shape[0]
    whole = lambda p, i: (0, 0)
    full = lambda a: pl.BlockSpec(a.shape, whole)
    tile = pl.BlockSpec((block, 128), lambda p, i: (i, p))
    column = pl.BlockSpec((total, 128), lambda p, i: (0, p))
    return pl.pallas_call(
        functools.partial(attend_kernel, pieces, block, scale),
        grid=(2, total // block),
        in_specs=[full(a) for a in (*qkv, cosine, sine, qext, kext)],
        out_specs=[tile, tile, tile, column],
        out_shape=[
            jax.ShapeDtypeStruct((total, 256), bf16),
            jax.ShapeDtypeStruct((total, 256), f32),
            jax.ShapeDtypeStruct((total, 256), bf16),
            jax.ShapeDtypeStruct((total, 256), bf16),
        ],
        scratch_shapes=[pltpu.VMEM((2, total, 128), bf16), pltpu.VMEM((2, total, 128), bf16)],
        compiler_params=pltpu.CompilerParams(vmem_limit_bytes=48 * 2**20),
        cost_estimate=pl.CostEstimate(
            flops=4 * total * total * 512, bytes_accessed=total * 4096, transcendentals=4 * total * total
        ),
        name="attend",
    )(*qkv, cosine, sine, qext, kext)


def attend_back_kernel(pieces, block, scale, *refs):
    grads = refs[:pieces]
    values = refs[pieces : 2 * pieces]
    qrot_ref, krot_ref, att_ref, lse_ref, cos_ref, sin_ref, qext_ref, kext_ref = refs[2 * pieces : 2 * pieces + 8]
    out_ref = refs[2 * pieces + 8]
    qx, gx, qm, gm, dq = refs[2 * pieces + 9 :]
    pair, step = pl.program_id(0), pl.program_id(1)
    last = pl.num_programs(1) - 1
    frames = grads[0].shape[0]
    per_piece = frames // block

    @pl.when(step == 0)
    def _():
        for j in range(pieces):
            rows = pl.ds(j * frames, frames)
            q = qrot_ref[rows, :]
            g = grads[j][:, pl.ds(pl.multiple_of(pair * 128, 128), 128)]
            lane = lanes_of(q.shape)
            low_lane = lane < HD
            spot = lane % HD
            prod = g.astype(f32) * att_ref[rows, :].astype(f32)
            zero = jnp.zeros_like(q)
            lse = lse_ref[rows, :]
            for h in range(2):
                own = low_lane if h == 0 else jnp.logical_not(low_lane)
                lse_h = lse[:, 0:1] if h == 0 else lse[:, HD : HD + 1]
                delta = jnp.sum(jnp.where(own, prod, 0.0), axis=1, keepdims=True)
                a, b, c = (t.astype(f32) for t in three_parts(-lse_h))
                part = jnp.where(spot == 4, a, jnp.where(spot == 5, b, jnp.where(spot == 6, c, qext_ref[rows, :].astype(f32))))
                qx[h, rows, :] = jnp.where(own, q, part.astype(bf16))
                a, b, c = (t.astype(f32) for t in three_parts(-delta))
                part = jnp.where(spot == 0, a, jnp.where(spot == 1, b, jnp.where(spot == 2, c, 0.0)))
                gx[h, rows, :] = jnp.where(own, g, part.astype(bf16))
                qm[h, rows, :] = jnp.where(own, q, zero)
                gm[h, rows, :] = jnp.where(own, g, zero)
        dq[...] = jnp.zeros_like(dq)

    rows = pl.ds(pl.multiple_of(step * block, block), block)
    for j in range(pieces):

        @pl.when(step // per_piece == j)
        def _(j=j):
            sub = pl.ds(pl.multiple_of((step - j * per_piece) * block, block), block)
            k = krot_ref[rows, :]
            v = values[j][sub, pl.ds(pl.multiple_of(512 + pair * 128, 128), 128)]
            ext = kext_ref[rows, :]
            lane = lanes_of(k.shape)
            low_lane = lane < HD
            three = jnp.where(lane % HD < 3, 1.0, 0.0).astype(bf16)
            zero = jnp.zeros_like(k)
            small = k.astype(f32) * scale
            dk = jnp.zeros((block, 128), f32)
            dv = jnp.zeros((block, 128), f32)
            for h in range(2):
                own = low_lane if h == 0 else jnp.logical_not(low_lane)
                kx = jnp.where(own, k, ext)
                vx = jnp.where(own, v, three)
                probs = jnp.exp(dot_nt(kx, qx[h]))
                grad = (probs * dot_nt(vx, gx[h])).astype(bf16)
                dv = dv + dot_nn(probs.astype(bf16), gm[h])
                dk = dk + dot_nn(grad, qm[h])
                turned = jnp.transpose(jnp.where(own, small, 0.0)).astype(bf16)
                dq[...] += dot_nn(turned, grad)
            dk = dk * cos_ref[rows, :] - swap_halves(dk) * sin_ref[rows, :]
            out_ref[rows, pl.ds(pl.multiple_of(256 + pair * 128, 128), 128)] = dk.astype(bf16)
            out_ref[rows, pl.ds(pl.multiple_of(512 + pair * 128, 128), 128)] = dv.astype(bf16)

    @pl.when(step == last)
    def _():
        g = jnp.transpose(dq[...])
        g = g * cos_ref[...] - swap_halves(g) * sin_ref[...]
        out_ref[:, pl.ds(pl.multiple_of(pair * 128, 128), 128)] = g.astype(bf16)


def attend_back(grads, qkv, qrot, krot, att, lse, cosine, sine, qext, kext, block=384, scale=HD**-0.5):
    pieces = len(grads)
    total = pieces * grads[0].shape[0]
    whole = lambda p, i: (0, 0)
    full = lambda a: pl.BlockSpec(a.shape, whole)
    column = pl.BlockSpec((total, 128), lambda p, i: (0, p))
    return pl.pallas_call(
        functools.partial(attend_back_kernel, pieces, block, scale),
        grid=(2, total // block),
        in_specs=[full(a) for a in (*grads, *qkv)] + [column] * 4 + [full(a) for a in (cosine, sine, qext, kext)],
        out_specs=pl.BlockSpec((total, 768), whole),
        out_shape=jax.ShapeDtypeStruct((total, 768), bf16),
        scratch_shapes=[pltpu.VMEM((2, total, 128), bf16)] * 4 + [pltpu.VMEM((128, total), f32)],
        compiler_params=pltpu.CompilerParams(vmem_limit_bytes=56 * 2**20),
        cost_estimate=pl.CostEstimate(
            flops=10 * total * total * 512, bytes_accessed=total * 8192, transcendentals=4 * total * total
        ),
        name="attend_back",
    )(*grads, *qkv, qrot, krot, att, lse, cosine, sine, qext, kext)


def frame_tables(seg, pos, valid):
    half = HD // 2
    freq = 10000.0 ** (-jnp.arange(half, dtype=f32) / half)
    angle = pos.astype(f32)[:, None] * freq
    cosine, sine = jnp.cos(angle), jnp.sin(angle)
    cosine = jnp.concatenate([cosine] * 4, axis=1)
    sine = jnp.concatenate([-sine, sine, -sine, sine], axis=1)
    spot = jnp.arange(128)[None, :] % HD
    seg, valid = seg[:, None], valid[:, None] > 0
    qext = jnp.where((spot < 3) & (spot != seg) | (spot == 3), -NEG, 0.0).astype(bf16)
    kext = ((spot == seg) & (spot < 3) | (spot == 3) & ~valid | (spot >= 4) & (spot < 7)).astype(bf16)
    return cosine, sine, qext, kext


def swap(v, mask):
    return lax.ppermute(v, "seq", [(i, i ^ mask) for i in range(4)])


def spread(v):
    near = swap(v, 1)
    far = swap(v, 2)
    return [v, near, far, swap(far, 1)]


def collect(parts, wait=()):
    low = [part.astype(bf16) for part in parts]
    if wait:
        low = list(after(tuple(low), *wait))
    far_near = swap(low[3], 1)
    near = swap(low[1], 1)
    far = swap((low[2].astype(f32) + far_near.astype(f32)).astype(bf16), 2)
    return parts[0] + near.astype(f32) + far.astype(f32)


def exchange(parts):
    return [parts[0], swap(parts[1], 1), swap(parts[2], 2), swap(parts[3], 3)]


def by_place(parts, me):
    odd, high = (me & 1) == 1, (me & 2) == 2
    parts = [jnp.where(odd, parts[t ^ 1], parts[t]) for t in range(4)]
    return [jnp.where(high, parts[t ^ 2], parts[t]) for t in range(4)]


def ring_step(v, step):
    return lax.ppermute(v, "dp", [(RING[i], RING[(i + step) % 8]) for i in range(8)])


def ring_gather(v, way):
    found = [None] * 8
    found[0] = one = other = v
    for k in range(1, 5):
        one = ring_step(one, way)
        found[(way * k) % 8] = one
        if k < 4:
            other = ring_step(other, -way)
            found[(-way * k) % 8] = other
    return found


def ring_scatter(v, place, way):
    order = jnp.asarray(RING, jnp.int32)

    def block(k):
        return lax.dynamic_index_in_dim(v, order[(place + way * k) % 8], 0, keepdims=False)

    one, other = block(4), block(-3)
    for k in range(3, -1, -1):
        one = ring_step(one, way)
        if k > 0:
            one = (one.astype(f32) + block(k).astype(f32)).astype(bf16)
    for k in range(2, -1, -1):
        other = ring_step(other, -way)
        if k > 0:
            other = (other.astype(f32) + block(-k).astype(f32)).astype(bf16)
    return block(0).astype(f32) + one.astype(f32) + other.astype(f32)


def after(v, *others):
    return lax.optimization_barrier((v, *others))[0]


def assemble_kernel(copies, n_in, n_out, index_ref, *refs):
    arrays, outs, sems = refs[:n_in], refs[n_in : n_in + n_out], refs[-1]
    moves = []
    me = index_ref[8]
    for number, (a, row, count, out, k, j, per_dp, per_seq, column) in enumerate(copies):
        start = index_ref[k] * per_dp + jnp.bitwise_xor(me, j) * per_seq
        target = outs[out].at[
            pl.ds(pl.multiple_of(start, count), count), pl.ds(column, arrays[a].shape[1])
        ]
        moves.append(
            pltpu.make_async_copy(arrays[a].at[pl.ds(row, count), :], target, sems.at[number])
        )
    for move in moves:
        move.start()
    for move in moves:
        move.wait()


def assemble(index, arrays, copies, shapes):
    anywhere = pl.BlockSpec(memory_space=pl.ANY)
    return pl.pallas_call(
        functools.partial(assemble_kernel, tuple(copies), len(arrays), len(shapes)),
        grid_spec=pltpu.PrefetchScalarGridSpec(
            num_scalar_prefetch=1,
            grid=(1,),
            in_specs=[anywhere] * len(arrays),
            out_specs=[pl.BlockSpec(shape, lambda i, index: (0, 0)) for shape in shapes],
            scratch_shapes=[pltpu.SemaphoreType.DMA((len(copies),))],
        ),
        out_shape=[jax.ShapeDtypeStruct(shape, bf16) for shape in shapes],
        compiler_params=pltpu.CompilerParams(vmem_limit_bytes=40 * 2**20),
        name="assemble",
    )(index, *arrays)


class Gather:
    def __init__(self, index):
        self.index, self.arrays, self.copies, self.shapes = index, [], [], []

    def out(self, rows, columns):
        self.shapes.append((rows, columns))
        return len(self.shapes) - 1

    def add(self, piece, k, blocks):
        self.arrays.append(piece)
        for row, count, out, j, per_dp, per_seq, column in blocks:
            self.copies.append(
                (len(self.arrays) - 1, row, count, out, k, j, per_dp, per_seq, column)
            )

    def run(self):
        return assemble(self.index, self.arrays, self.copies, self.shapes)


def half(v, which):
    middle = v.shape[1] // 2
    return jnp.where(which == 1, v[:, middle:], v[:, :middle])


def merge(mine, other, core):
    return jnp.concatenate(
        [jnp.where(core == 1, other, mine), jnp.where(core == 1, mine, other)], axis=1
    )


def by_dp(grad, groups):
    return grad.reshape(groups, grad.shape[0] // groups, grad.shape[1])


def scatter_dp(grad, place, groups, way):
    low = grad.astype(bf16)
    if groups != 8:
        return lax.psum_scatter(low, "dp", scatter_dimension=0).astype(f32)
    return ring_scatter(low, place, way)


def finish(block, me):
    rows = block.shape[0] // 4
    low = block.astype(bf16)
    parts = by_place([low[t * rows : (t + 1) * rows] for t in range(4)], me)
    return by_place(exchange(parts), me)


def halves_sum(parts):
    total = [parts[c].astype(f32) + parts[2 + c].astype(f32) for c in range(2)]
    return jnp.concatenate(total, axis=1)


def on_device(
    layer_input,
    skip_input,
    time_embed,
    segment_ids,
    positions,
    valid_mask,
    skip_weight,
    time_weight,
    query_weight,
    key_weight,
    value_weight,
    out_weight,
    up_weight,
    down_weight,
    cotangent,
):
    rows, frames, width = layer_input.shape
    hidden = up_weight.shape[1]
    groups = lax.axis_size("dp")
    me, dp = lax.axis_index("seq"), lax.axis_index("dp")
    local = width // 4
    local_hidden = hidden // 4

    core = me & 1
    hidden_block = hidden // (groups * 4)

    triple = [
        jnp.concatenate(
            [w[:, t * local : (t + 1) * local] for w in (query_weight, key_weight, value_weight)],
            axis=1,
        )
        for t in range(4)
    ]
    upper_w = [
        jnp.concatenate(
            [
                up_weight[:, (g * 4 + t) * hidden_block : (g * 4 + t + 1) * hidden_block]
                for g in range(groups)
            ],
            axis=1,
        )
        for t in range(4)
    ]
    time_a, time_b = time_weight[:, : 2 * width], time_weight[:, 2 * width :]
    if groups == 8:
        place = jnp.asarray(PLACE, jnp.int32)[dp]
        order = jnp.asarray(RING, jnp.int32)[(place - jnp.arange(8)) % 8]
        index = jnp.concatenate([order, me[None].astype(jnp.int32)])
        n_skip, n_time = skip_weight.shape[0], time_weight.shape[0]

        first = Gather(index)
        o_skip, o_time_a = first.out(32 * n_skip, width), first.out(32 * n_time, 2 * width)
        own = jnp.concatenate([skip_weight, time_a[:, :width], time_a[:, width:]], axis=0)
        layout = [
            (0, n_skip, o_skip, 0),
            (n_skip, n_time, o_time_a, 0),
            (n_skip + n_time, n_time, o_time_a, width),
        ]
        found_own, found_far = ring_gather(own, 1), ring_gather(swap(own, 2), -1)
        for k in range(8):
            for piece, j in ((found_own[k], 0), (found_far[k], 2)):
                for array, jj in ((piece, j), (swap(piece, 1), j ^ 1)):
                    first.add(
                        array,
                        k,
                        [(row, count, out, jj, 4 * count, count, column) for row, count, out, column in layout],
                    )
        skip_full, time_a_full = first.run()

        rest = []
        for t in range(4):
            sides = jnp.concatenate(
                [
                    w[:, (t & 1) * (w.shape[1] // 2) : ((t & 1) + 1) * (w.shape[1] // 2)]
                    for w in (time_b, out_weight)
                ],
                axis=1,
            )
            rest.append(jnp.concatenate([triple[t], upper_w[t], sides], axis=1))
        rest = jnp.concatenate(by_place(exchange(by_place(rest, me)), me), axis=0)
        split = 3 * local, 3 * local + local_hidden
        wide = lax.all_gather(rest[:, split[1] :], "dp", axis=0, tiled=True)
        wide = (wide, swap(wide, 1))
        time_b_sides = [w[:, : 3 * width // 2] for w in wide]
        out_sides = [w[:, 3 * width // 2 :] for w in wide]

        second = Gather(index)
        o_triple = second.out(width, 3 * local)
        triple_own = after(rest[:, : split[0]], found_own[4], found_far[4], found_own[5], found_far[3])
        found = ring_gather(triple_own, 1)
        for k in range(8):
            second.add(found[k], k, [(0, width // 8, o_triple, 0, width // 8, 0, 0)])
        (triple_full,) = second.run()

        third = Gather(index)
        o_up, o_down = third.out(width, local_hidden), third.out(local_hidden, width)
        up_own, down_own = after((rest[:, split[0] : split[1]], down_weight), found[4], found[5])
        found_up, found_down = ring_gather(up_own, 1), ring_gather(down_own, -1)
        n_down = down_weight.shape[0]
        for k in range(8):
            third.add(found_up[k], k, [(0, width // 8, o_up, 0, width // 8, 0, 0)])
            third.add(found_down[k], k, [(0, n_down, o_down, 0, n_down, 0, 0)])
        up_full, down_full = third.run()
    else:
        place = dp
        skip_full, time_a_full, time_b_full, out_full = (
            lax.all_gather(w, ("dp", "seq"), axis=0, tiled=True)
            for w in (skip_weight, time_a, time_b, out_weight)
        )
        triple_full, up_full = (
            lax.all_gather(
                jnp.concatenate(by_place(exchange(by_place(parts, me)), me), axis=0),
                "dp",
                axis=0,
                tiled=True,
            )
            for parts in (triple, upper_w)
        )
        down_full = lax.all_gather(down_weight, "dp", axis=0, tiled=True)
        time_b_sides = [half(time_b_full, core), half(time_b_full, 1 - core)]
        out_sides = [half(out_full, core), half(out_full, 1 - core)]

    marks = jnp.concatenate(spread(jnp.concatenate([segment_ids, positions, valid_mask])), axis=1)
    cosine, sine, query_marks, key_marks = frame_tables(marks[0], marks[1], marks[2])
    first_in, second_in = layer_input.reshape(frames, width), skip_input.reshape(frames, width)
    joined = jnp.concatenate([first_in, second_in], axis=1)
    base = dot_nn(joined, skip_full)
    time_value = time_embed.reshape(frames, width).astype(f32)
    time_act = (time_value * jax.nn.sigmoid(time_value)).astype(bf16)
    shift_a, scale_a = jnp.split(dot_nn(time_act, time_a_full), 2, axis=1)
    normed_a, inverse_a = norm_rows(base)
    hidden_a = spread((normed_a * (1.0 + scale_a) + shift_a).astype(bf16))
    qkv = [dot_nn(h, triple_full).astype(bf16) for h in hidden_a]
    att, logsum, query_rot, key_rot = attend(qkv, cosine, sine, query_marks, key_marks)
    attended = jnp.concatenate(
        by_place(exchange([att[j * frames : (j + 1) * frames] for j in range(4)]), me), axis=1
    )

    shift_b, scale_b, gate_b = jnp.split(
        merge(dot_nn(time_act, time_b_sides[0]), dot_nn(time_act, time_b_sides[1]), core),
        3,
        axis=1,
    )
    upstream = cotangent.reshape(frames, width).astype(f32)
    ffn_grad = spread((upstream * gate_b).astype(bf16))
    middle = base + merge(dot_nn(attended, out_sides[0]), dot_nn(attended, out_sides[1]), core)
    normed_b, inverse_b = norm_rows(middle)
    hidden_b = spread((normed_b * (1.0 + scale_b) + shift_b).astype(bf16))
    hb = [jnp.concatenate(hidden_b[:2]), jnp.concatenate(hidden_b[2:])]
    fg = [jnp.concatenate(ffn_grad[:2]), jnp.concatenate(ffn_grad[2:])]
    upper = [dot_nn(h, up_full) for h in hb]
    acted = [gelu_value(u).astype(bf16) for u in upper]
    ug = [(dot_nt(g, down_full) * gelu_slope(u)).astype(bf16) for g, u in zip(fg, upper)]
    back = [dot_nt(u, up_full) for u in ug]
    hidden_b_grad = collect(
        [back[0][:frames], back[0][frames:], back[1][:frames], back[1][frames:]]
    )
    part = [dot_nn(a, down_full) for a in acted]
    ffn = collect(
        [part[0][:frames], part[0][frames:], part[1][:frames], part[1][frames:]], (hidden_b_grad,)
    )
    grad_down = dot_tn(acted[0], fg[0]) + dot_tn(acted[1], fg[1])
    grad_up = dot_tn(hb[0], ug[0]) + dot_tn(hb[1], ug[1])
    output = (middle + gate_b * ffn).astype(bf16).reshape(rows, frames, width)
    gate_b_grad = upstream * ffn

    scale_b_grad = hidden_b_grad * normed_b
    middle_grad = upstream + norm_back(hidden_b_grad * (1.0 + scale_b), normed_b, inverse_b)
    branch_grad = middle_grad.astype(bf16)
    branch_sides = [half(branch_grad, core), half(branch_grad, 1 - core)]
    attended_grad = (
        dot_nt(branch_sides[0], out_sides[0]) + dot_nt(branch_sides[1], out_sides[1])
    ).astype(bf16)
    att_grad = exchange(
        by_place([attended_grad[:, t * local : (t + 1) * local] for t in range(4)], me)
    )
    modul_b_grad = jnp.concatenate([hidden_b_grad, scale_b_grad, gate_b_grad], axis=1).astype(bf16)
    modul_sides = [half(modul_b_grad, core), half(modul_b_grad, 1 - core)]
    time_back_b = dot_nt(modul_sides[0], time_b_sides[0]) + dot_nt(modul_sides[1], time_b_sides[1])
    grad_wide = [
        jnp.concatenate(
            [dot_tn(time_act, modul_sides[i]).astype(bf16), dot_tn(attended, branch_sides[i]).astype(bf16)],
            axis=1,
        )
        for i in (0, 1)
    ]
    grad_wide = grad_wide[0].astype(f32) + swap(grad_wide[1], 1).astype(f32)
    wide_sum = scatter_dp(by_dp(grad_wide, groups), place, groups, 1)
    ffn_sum = lax.psum_scatter(
        by_dp(jnp.concatenate([grad_up.astype(bf16), grad_down.astype(bf16)], axis=1), groups),
        "dp",
        scatter_dimension=0,
    ).astype(f32)
    triple_grad = attend_back(
        att_grad, qkv, query_rot, key_rot, att, logsum, cosine, sine, query_marks, key_marks
    )
    back = dot_nt(triple_grad, triple_full)
    hidden_a_grad = collect([back[j * frames : (j + 1) * frames] for j in range(4)])
    grad_triple = dot_tn(jnp.concatenate(hidden_a), triple_grad)

    scale_a_grad = hidden_a_grad * normed_a
    base_grad = (
        middle_grad + norm_back(hidden_a_grad * (1.0 + scale_a), normed_a, inverse_a)
    ).astype(bf16)
    joined_grad = dot_nt(base_grad, skip_full)
    modul_a_grad = jnp.concatenate([hidden_a_grad, scale_a_grad], axis=1).astype(bf16)
    time_back = dot_nt(modul_a_grad, time_a_full) + time_back_b
    time_grad = (time_back * silu_slope(time_value)).reshape(rows, frames, width)

    grad_last = []
    for i in (0, 1):
        skip_side = by_dp(dot_tn(joined, half(base_grad, core ^ i)).astype(bf16), groups)
        rows_skip = skip_side.shape[1] // 8
        skip_side = skip_side.reshape(groups, 4, 2, rows_skip, -1)
        skip_side = jnp.concatenate([skip_side[:, :, 0], skip_side[:, :, 1]], axis=3)
        time_side = by_dp(dot_tn(time_act, half(modul_a_grad, core ^ i)).astype(bf16), groups)
        grad_last.append(
            jnp.concatenate([skip_side.reshape(groups, 4 * rows_skip, -1), time_side], axis=2)
        )
    grad_last = grad_last[0].astype(f32) + swap(grad_last[1], 1).astype(f32)
    qkv_sum = scatter_dp(by_dp(grad_triple, groups), place, groups, -1)
    last_sum = scatter_dp(grad_last, place, groups, 1)

    parts = finish(jnp.concatenate([ffn_sum[:, :local_hidden], wide_sum], axis=1), me)
    up_sum = jnp.concatenate(
        [
            p[:, g * hidden_block : (g + 1) * hidden_block]
            for g in range(groups)
            for p in parts
        ],
        axis=1,
    )
    split = local_hidden, local_hidden + 3 * width // 2
    time_b_sum = halves_sum([p[:, split[0] : split[1]] for p in parts])
    out_sum = halves_sum([p[:, split[1] :] for p in parts])
    parts = finish(jnp.concatenate([qkv_sum, last_sum], axis=1), me)
    qkv_sum = [
        jnp.concatenate([p[:, i * local : (i + 1) * local] for p in parts], axis=1) for i in range(3)
    ]
    split = 3 * local, 3 * local + width // 2, 3 * local + width
    skip_sum = jnp.concatenate(
        [
            halves_sum([p[:, split[i] : split[i + 1]] for p in parts]) for i in range(2)
        ],
        axis=0,
    )
    time_a_sum = halves_sum([p[:, split[2] :] for p in parts])
    return (
        output,
        joined_grad[:, :width].reshape(rows, frames, width),
        joined_grad[:, width:].reshape(rows, frames, width),
        time_grad,
        skip_sum,
        jnp.concatenate([time_a_sum, time_b_sum], axis=1),
        qkv_sum[0].astype(f32),
        qkv_sum[1].astype(f32),
        qkv_sum[2].astype(f32),
        out_sum,
        up_sum.astype(f32),
        ffn_sum[:, local_hidden:],
    )


def solution(mesh):
    frames = P("dp", "seq", None)
    marks = P("dp", "seq")
    weight = P(("dp", "seq"), None)
    return jax.shard_map(
        on_device,
        mesh=mesh,
        in_specs=(frames,) * 3 + (marks,) * 3 + (weight,) * 8 + (frames,),
        out_specs=(frames,) * 4 + (weight,) * 8,
        check_vma=False,
    )
```

```python
import functools

import jax
import jax.numpy as jnp
from jax import lax
from jax.experimental import pallas as pl
from jax.experimental.pallas import tpu as pltpu
from jax.sharding import PartitionSpec as P

HD = 64
NEG = 1e30
norm_eps = 1e-06
gelu_coef = 0.7978845608028654
f32, bf16 = jnp.float32, jnp.bfloat16

RING = (0, 2, 4, 6, 7, 5, 3, 1)
PLACE = tuple(RING.index(d) for d in range(8))


def dot_nt(a, b):
    return lax.dot_general(a, b, (((1,), (1,)), ((), ())), preferred_element_type=f32)


def dot_nn(a, b):
    return lax.dot_general(a, b, (((1,), (0,)), ((), ())), preferred_element_type=f32)


def dot_tn(a, b):
    return lax.dot_general(a, b, (((0,), (0,)), ((), ())), preferred_element_type=f32)


def silu_slope(v):
    sig = jax.nn.sigmoid(v)
    return sig * (1.0 + v * (1.0 - sig))


def gelu_value(u):
    return 0.5 * u * (1.0 + jnp.tanh(gelu_coef * (u + 0.044715 * u * u * u)))


def gelu_slope(u):
    inner = jnp.tanh(gelu_coef * (u + 0.044715 * u * u * u))
    return 0.5 * (1.0 + inner) + 0.5 * u * (1.0 - inner * inner) * gelu_coef * (
        1.0 + 3.0 * 0.044715 * u * u
    )


def norm_rows(v):
    mean = jnp.mean(v, axis=-1, keepdims=True)
    centred = v - mean
    inverse = lax.rsqrt(jnp.mean(centred * centred, axis=-1, keepdims=True) + norm_eps)
    return (centred * inverse, inverse)


def norm_back(grad, normed, inverse):
    return inverse * (
        grad
        - jnp.mean(grad, axis=-1, keepdims=True)
        - normed * jnp.mean(grad * normed, axis=-1, keepdims=True)
    )

def lanes_of(shape):
    return lax.broadcasted_iota(jnp.int32, shape, 1)


def swap_halves(v):
    lane = lanes_of(v.shape)
    return jnp.where(lane % HD < HD // 2, pltpu.roll(v, 128 - HD // 2, 1), pltpu.roll(v, HD // 2, 1))


def three_parts(v):
    hi = v.astype(bf16)
    rest = v - hi.astype(f32)
    mid = rest.astype(bf16)
    low = (rest - mid.astype(f32)).astype(bf16)
    return hi, mid, low


def attend_kernel(pieces, block, scale, *refs):
    qkv = refs[:pieces]
    cos_ref, sin_ref, qext_ref, kext_ref = refs[pieces : pieces + 4]
    att_ref, lse_ref, qrot_ref, krot_ref = refs[pieces + 4 : pieces + 8]
    kx, vx = refs[pieces + 8 :]
    step = pl.program_id(1)
    frames = qkv[0].shape[0]
    per_piece = frames // block

    @pl.when(step == 0)
    def _():
        for j in range(pieces):
            rows = pl.ds(j * frames, frames)
            k = qkv[j][:, 128:256].astype(f32)
            k = (k * cos_ref[rows, :] + swap_halves(k) * sin_ref[rows, :]).astype(bf16)
            krot_ref[rows, :] = k
            v = qkv[j][:, 256:384]
            ext = kext_ref[rows, :]
            lane = lanes_of(k.shape)
            one = jnp.where(lane % HD == 0, 1.0, 0.0).astype(bf16)
            low_lane = lane < HD
            kx[0, rows, :] = jnp.where(low_lane, k, ext)
            kx[1, rows, :] = jnp.where(low_lane, ext, k)
            vx[0, rows, :] = jnp.where(low_lane, v, one)
            vx[1, rows, :] = jnp.where(low_lane, one, v)

    rows = pl.ds(pl.multiple_of(step * block, block), block)
    for j in range(pieces):

        @pl.when(step // per_piece == j)
        def _(j=j):
            sub = pl.ds(pl.multiple_of((step - j * per_piece) * block, block), block)
            q = qkv[j][sub, 0:128].astype(f32)
            q = (q * cos_ref[rows, :] + swap_halves(q) * sin_ref[rows, :]).astype(bf16)
            qrot_ref[...] = (q.astype(f32) * scale).astype(bf16)

    q = qrot_ref[...]
    ext = qext_ref[rows, :]
    low_lane = lanes_of(q.shape) < HD
    outs = []
    for h in range(2):
        qx = jnp.where(low_lane, q, ext) if h == 0 else jnp.where(low_lane, ext, q)
        scores = dot_nt(qx, kx[h])
        top = jnp.max(scores, axis=1, keepdims=True)
        expo = jnp.exp(scores - top)
        mixed = dot_nn(expo.astype(bf16), vx[h])
        total = mixed[:, HD : HD + 1] if h == 0 else mixed[:, 0:1]
        outs.append((mixed / total, top + jnp.log(total)))
    low_out = lanes_of((block, 128)) < HD
    att_ref[...] = jnp.where(low_out, outs[0][0], outs[1][0]).astype(bf16)
    lse_ref[...] = jnp.where(low_out, outs[0][1], outs[1][1])


def attend(qkv, cosine, sine, qext, kext, block=384, scale=HD**-0.5):
    pieces = len(qkv)
    frames = qkv[0].shape[0]
    total = pieces * frames
    full = lambda a: pl.BlockSpec(a.shape, lambda p, i: (0, 0))
    tile = pl.BlockSpec((block, 128), lambda p, i: (i, p))
    return pl.pallas_call(
        functools.partial(attend_kernel, pieces, block, scale),
        grid=(2, total // block),
        in_specs=[pl.BlockSpec((frames, 384), lambda p, i: (0, p))] * pieces
        + [full(a) for a in (cosine, sine, qext, kext)],
        out_specs=[tile, tile, tile, pl.BlockSpec((total, 128), lambda p, i: (0, p))],
        out_shape=[jax.ShapeDtypeStruct((total, 256), t) for t in (bf16, f32, bf16, bf16)],
        scratch_shapes=[pltpu.VMEM((2, total, 128), bf16), pltpu.VMEM((2, total, 128), bf16)],
        compiler_params=pltpu.CompilerParams(vmem_limit_bytes=24 * 2**20),
        cost_estimate=pl.CostEstimate(
            flops=8 * total * total * 256, bytes_accessed=total * 4096, transcendentals=4 * total * total
        ),
        name="attend",
    )(*qkv, cosine, sine, qext, kext)


def attend_back_kernel(pieces, block, scale, *refs):
    grads = refs[:pieces]
    values = refs[pieces : 2 * pieces]
    qrot_ref, krot_ref, att_ref, lse_ref, cos_ref, sin_ref, qext_ref, kext_ref = refs[2 * pieces : 2 * pieces + 8]
    out_ref = refs[2 * pieces + 8]
    qx, gx, qm, gm, dq = refs[2 * pieces + 9 :]
    step = pl.program_id(1)
    last = pl.num_programs(1) - 1
    frames = grads[0].shape[0]
    per_piece = frames // block

    @pl.when(step == 0)
    def _():
        for j in range(pieces):
            rows = pl.ds(j * frames, frames)
            q = qrot_ref[rows, :]
            g = grads[j][...]
            lane = lanes_of(q.shape)
            low_lane = lane < HD
            spot = lane % HD
            prod = g.astype(f32) * att_ref[rows, :].astype(f32)
            zero = jnp.zeros_like(q)
            lse = lse_ref[rows, :]
            for h in range(2):
                own = low_lane if h == 0 else jnp.logical_not(low_lane)
                lse_h = lse[:, 0:1] if h == 0 else lse[:, HD : HD + 1]
                delta = jnp.sum(jnp.where(own, prod, 0.0), axis=1, keepdims=True)
                a, b, c = (t.astype(f32) for t in three_parts(-lse_h))
                part = jnp.where(spot == 4, a, jnp.where(spot == 5, b, jnp.where(spot == 6, c, qext_ref[rows, :].astype(f32))))
                qx[h, rows, :] = jnp.where(own, q, part.astype(bf16))
                a, b, c = (t.astype(f32) for t in three_parts(-delta))
                part = jnp.where(spot == 0, a, jnp.where(spot == 1, b, jnp.where(spot == 2, c, 0.0)))
                gx[h, rows, :] = jnp.where(own, g, part.astype(bf16))
                qm[h, rows, :] = jnp.where(own, q, zero)
                gm[h, rows, :] = jnp.where(own, g, zero)
        dq[...] = jnp.zeros_like(dq)

    rows = pl.ds(pl.multiple_of(step * block, block), block)
    for j in range(pieces):

        @pl.when(step // per_piece == j)
        def _(j=j):
            sub = pl.ds(pl.multiple_of((step - j * per_piece) * block, block), block)
            k = krot_ref[rows, :]
            v = values[j][sub, 256:384]
            ext = kext_ref[rows, :]
            lane = lanes_of(k.shape)
            low_lane = lane < HD
            three = jnp.where(lane % HD < 3, 1.0, 0.0).astype(bf16)
            zero = jnp.zeros_like(k)
            small = k.astype(f32) * scale
            dk = jnp.zeros((block, 128), f32)
            dv = jnp.zeros((block, 128), f32)
            for h in range(2):
                own = low_lane if h == 0 else jnp.logical_not(low_lane)
                kx = jnp.where(own, k, ext)
                vx = jnp.where(own, v, three)
                probs = jnp.exp(dot_nt(kx, qx[h]))
                grad = (probs * dot_nt(vx, gx[h])).astype(bf16)
                dv = dv + dot_nn(probs.astype(bf16), gm[h])
                dk = dk + dot_nn(grad, qm[h])
                turned = jnp.transpose(jnp.where(own, small, 0.0)).astype(bf16)
                dq[...] += dot_nn(turned, grad)
            dk = dk * cos_ref[rows, :] - swap_halves(dk) * sin_ref[rows, :]
            out_ref[rows, 128:256] = dk.astype(bf16)
            out_ref[rows, 256:384] = dv.astype(bf16)

    @pl.when(step == last)
    def _():
        g = jnp.transpose(dq[...])
        g = g * cos_ref[...] - swap_halves(g) * sin_ref[...]
        out_ref[:, 0:128] = g.astype(bf16)


def attend_back(grads, qkv, qrot, krot, att, lse, cosine, sine, qext, kext, block=384, scale=HD**-0.5):
    pieces = len(grads)
    frames = grads[0].shape[0]
    total = pieces * frames
    full = lambda a: pl.BlockSpec(a.shape, lambda p, i: (0, 0))
    return pl.pallas_call(
        functools.partial(attend_back_kernel, pieces, block, scale),
        grid=(2, total // block),
        in_specs=[pl.BlockSpec((frames, 128), lambda p, i: (0, p))] * pieces
        + [pl.BlockSpec((frames, 384), lambda p, i: (0, p))] * pieces
        + [pl.BlockSpec((total, 128), lambda p, i: (0, p))] * 4
        + [full(a) for a in (cosine, sine, qext, kext)],
        out_specs=pl.BlockSpec((total, 384), lambda p, i: (0, p)),
        out_shape=jax.ShapeDtypeStruct((total, 768), bf16),
        scratch_shapes=[pltpu.VMEM((2, total, 128), bf16)] * 4 + [pltpu.VMEM((128, total), f32)],
        compiler_params=pltpu.CompilerParams(vmem_limit_bytes=34 * 2**20),
        cost_estimate=pl.CostEstimate(
            flops=20 * total * total * 256, bytes_accessed=total * 8192, transcendentals=4 * total * total
        ),
        name="attend_back",
    )(*grads, *qkv, qrot, krot, att, lse, cosine, sine, qext, kext)


def frame_tables(seg, pos, valid):
    half = HD // 2
    freq = 10000.0 ** (-jnp.arange(half, dtype=f32) / half)
    angle = pos.astype(f32)[:, None] * freq
    cosine, sine = jnp.cos(angle), jnp.sin(angle)
    cosine = jnp.concatenate([cosine] * 4, axis=1)
    sine = jnp.concatenate([-sine, sine, -sine, sine], axis=1)
    spot = jnp.arange(128)[None, :] % HD
    seg, valid = seg[:, None], valid[:, None] > 0
    qext = jnp.where((spot < 3) & (spot != seg) | (spot == 3), -NEG, 0.0).astype(bf16)
    kext = ((spot == seg) & (spot < 3) | (spot == 3) & ~valid | (spot >= 4) & (spot < 7)).astype(bf16)
    return cosine, sine, qext, kext


def swap(v, mask):
    return lax.ppermute(v, "seq", [(i, i ^ mask) for i in range(4)])


def spread(v, before=()):
    near = swap(v, 1)
    far = swap(v, 2)
    return [v, near, far, swap(after(far, *before) if before else far, 1)]


def collect(parts, wait=()):
    low = [part.astype(bf16) for part in parts]
    if wait:
        low = list(after(tuple(low), *wait))
    far_near = swap(low[3], 1)
    near = swap(low[1], 1)
    sent = (low[2].astype(f32) + far_near.astype(f32)).astype(bf16)
    far = swap(sent, 2)
    return parts[0] + near.astype(f32) + far.astype(f32), sent


def exchange(parts):
    return [parts[0], swap(parts[1], 1), swap(parts[2], 2), swap(parts[3], 3)]


def by_place(parts, me):
    odd, high = (me & 1) == 1, (me & 2) == 2
    parts = [jnp.where(odd, parts[t ^ 1], parts[t]) for t in range(4)]
    return [jnp.where(high, parts[t ^ 2], parts[t]) for t in range(4)]


def ring_step(v, step):
    return lax.ppermute(v, "dp", [(RING[i], RING[(i + step) % 8]) for i in range(8)])


class RingGather:
    def __init__(self, v):
        self.found, self.front, self.count = [(0, 0, v)], (v, v), 0

    def step(self, *before):
        one, other = after(self.front, *before) if before else self.front
        self.count += 1
        k = self.count
        if k < 4:
            self.front = ring_step(one, 1), ring_step(other, -1)
            self.found += [(k, 0, self.front[0]), (8 - k, 0, self.front[1])]
        else:
            middle = one.shape[0] // 2
            self.front = ring_step(one[:middle], 1), ring_step(other[middle:], -1)
            self.found += [(4, 0, self.front[0]), (4, middle, self.front[1])]
        return self.front


def ring_add_kernel(k, count, index_ref, *refs):
    plus, minus = refs[:count], refs[count : 2 * count]
    moving = refs[2 * count : -1 if k == 0 else -2]
    outs = refs[-1:] if k == 0 else refs[-2:]
    rows = plus[0].shape[1]
    middle = rows // 2
    upper, lower = slice(0, middle), slice(middle, rows)
    start = 0
    for i in range(count):
        columns = slice(start, start + plus[i].shape[2])
        start += plus[i].shape[2]
        if k == 4:
            outs[0][:, columns] = plus[i][0, upper, :].astype(bf16)
            outs[1][:, columns] = plus[i][0, lower, :].astype(bf16)
            continue
        ahead = plus[i][0].astype(f32)
        if k == 0:
            outs[0][:, columns] = (
                ahead + moving[0][:, columns].astype(f32) + moving[1][:, columns].astype(f32)
            )
            continue
        behind = minus[i][0].astype(f32)
        one, other = moving[0][:, columns].astype(f32), moving[1][:, columns].astype(f32)
        if k == 3:
            outs[0][upper, columns] = (ahead[upper] + one).astype(bf16)
            outs[0][lower, columns] = ahead[lower].astype(bf16)
            outs[1][upper, columns] = behind[upper].astype(bf16)
            outs[1][lower, columns] = (behind[lower] + other).astype(bf16)
        else:
            outs[0][:, columns] = (ahead + one).astype(bf16)
            outs[1][:, columns] = (behind + other).astype(bf16)


def ring_add(index, arrays, moving, k):
    rows, columns = arrays[0].shape[1], sum(a.shape[2] for a in arrays)
    ahead = [pl.BlockSpec((1, rows, a.shape[2]), lambda i, index: (index[(8 - k) % 8], 0, 0)) for a in arrays]
    behind = [pl.BlockSpec((1, rows, a.shape[2]), lambda i, index: (index[k], 0, 0)) for a in arrays]
    whole = lambda shape: pl.BlockSpec(shape, lambda i, index: (0, 0))
    height = rows // 2 if k == 4 else rows
    n_out = 1 if k == 0 else 2
    return pl.pallas_call(
        functools.partial(ring_add_kernel, k, len(arrays)),
        grid_spec=pltpu.PrefetchScalarGridSpec(
            num_scalar_prefetch=1,
            grid=(1,),
            in_specs=ahead + behind + [whole(m.shape) for m in moving],
            out_specs=[whole((height, columns))] * n_out,
        ),
        out_shape=[jax.ShapeDtypeStruct((height, columns), f32 if k == 0 else bf16)] * n_out,
        compiler_params=pltpu.CompilerParams(vmem_limit_bytes=16 * 2**20),
        name="ring_add",
    )(index, *arrays, *arrays, *moving)


class RingSum:
    def __init__(self, arrays, index, ringed):
        self.arrays, self.index, self.ringed = arrays, index, ringed
        self.front, self.count = (), 4

    def step(self, *before):
        if self.ringed:
            arrays, front = self.arrays, self.front
            if before:
                arrays, front = after((arrays, front), *before)
            moving = ring_add(self.index, arrays, front, self.count)
            self.front = ring_step(moving[0], 1), ring_step(moving[1], -1)
            self.count -= 1
        return self.front

    def total(self):
        if self.ringed:
            return ring_add(self.index, self.arrays, self.front, 0)[0]
        low = jnp.concatenate([a.astype(bf16) for a in self.arrays], axis=2)
        return lax.psum_scatter(low, "dp", scatter_dimension=0).astype(f32)


def after(v, *others):
    return lax.optimization_barrier((v, *others))[0]


def assemble_kernel(copies, n_in, n_out, index_ref, *refs):
    arrays, outs, sems = refs[:n_in], refs[n_in : n_in + n_out], refs[-1]
    moves = []
    me = index_ref[8]
    for number, (a, row, count, out, k, j, per_dp, per_seq, column, more) in enumerate(copies):
        start = index_ref[k] * per_dp + jnp.bitwise_xor(me, j) * per_seq + more
        target = outs[out].at[
            pl.ds(pl.multiple_of(start, count), count), pl.ds(column, arrays[a].shape[1])
        ]
        moves.append(
            pltpu.make_async_copy(arrays[a].at[pl.ds(row, count), :], target, sems.at[number])
        )
    for move in moves:
        move.start()
    for move in moves:
        move.wait()


def assemble(index, arrays, copies, shapes):
    anywhere = pl.BlockSpec(memory_space=pl.ANY)
    return pl.pallas_call(
        functools.partial(assemble_kernel, tuple(copies), len(arrays), len(shapes)),
        grid_spec=pltpu.PrefetchScalarGridSpec(
            num_scalar_prefetch=1,
            grid=(1,),
            in_specs=[anywhere] * len(arrays),
            out_specs=[pl.BlockSpec(shape, lambda i, index: (0, 0)) for shape in shapes],
            scratch_shapes=[pltpu.SemaphoreType.DMA((len(copies),))],
        ),
        out_shape=[jax.ShapeDtypeStruct(shape, bf16) for shape in shapes],
        compiler_params=pltpu.CompilerParams(vmem_limit_bytes=8 * 2**20 + 5 * sum(r * c for r, c in shapes)),
        name="assemble",
    )(index, *arrays)


class Gather:
    def __init__(self, index):
        self.index, self.arrays, self.copies, self.shapes = index, [], [], []

    def out(self, rows, columns):
        self.shapes.append((rows, columns))
        return len(self.shapes) - 1

    def add(self, piece, k, blocks):
        self.arrays.append(piece)
        for row, count, out, j, per_dp, per_seq, column, more in blocks:
            self.copies.append(
                (len(self.arrays) - 1, row, count, out, k, j, per_dp, per_seq, column, more)
            )

    def run(self):
        return assemble(self.index, self.arrays, self.copies, self.shapes)


def half(v, which):
    middle = v.shape[1] // 2
    return jnp.where(which == 1, v[:, middle:], v[:, :middle])


def merge(mine, other, core):
    return jnp.concatenate(
        [jnp.where(core == 1, other, mine), jnp.where(core == 1, mine, other)], axis=1
    )


def by_dp(grad, groups):
    return grad.reshape(groups, grad.shape[0] // groups, grad.shape[1])


def finish(block, me):
    rows = block.shape[0] // 4
    low = block.astype(bf16)
    parts = by_place([low[t * rows : (t + 1) * rows] for t in range(4)], me)
    return by_place(exchange(parts), me)


def halves_sum(parts):
    total = [parts[c].astype(f32) + parts[2 + c].astype(f32) for c in range(2)]
    return jnp.concatenate(total, axis=1)


def on_device(
    layer_input,
    skip_input,
    time_embed,
    segment_ids,
    positions,
    valid_mask,
    skip_weight,
    time_weight,
    query_weight,
    key_weight,
    value_weight,
    out_weight,
    up_weight,
    down_weight,
    cotangent,
):
    rows, frames, width = layer_input.shape
    hidden = up_weight.shape[1]
    groups = lax.axis_size("dp")
    me, dp = lax.axis_index("seq"), lax.axis_index("dp")
    local = width // 4
    local_hidden = hidden // 4

    core = me & 1
    hidden_block = hidden // (groups * 4)
    ringed = groups == 8
    first_in, second_in = layer_input.reshape(frames, width), skip_input.reshape(frames, width)
    time_a, time_b = time_weight[:, : 2 * width], time_weight[:, 2 * width :]
    n_skip, n_time = skip_weight.shape[0], time_weight.shape[0]

    def needed():
        triple = [
            jnp.concatenate(
                [
                    w[:, t * local + p * 128 : t * local + (p + 1) * 128]
                    for p in range(2)
                    for w in (query_weight, key_weight, value_weight)
                ],
                axis=1,
            )
            for t in range(4)
        ]
        upper_w = [
            jnp.concatenate(
                [
                    up_weight[:, (g * 4 + t) * hidden_block : (g * 4 + t + 1) * hidden_block]
                    for g in range(groups)
                ],
                axis=1,
            )
            for t in range(4)
        ]
        return triple, upper_w

    triple, upper_w = needed()
    index = None
    marks = jnp.concatenate(spread(jnp.concatenate([segment_ids, positions, valid_mask])), axis=1)
    tables = frame_tables(marks[0], marks[1], marks[2])
    time_value = time_embed.reshape(frames, width).astype(f32)
    time_act = (time_value * jax.nn.sigmoid(time_value)).astype(bf16)
    joined = jnp.concatenate([first_in, second_in], axis=1)
    row_own = jnp.concatenate([first_in, second_in, time_act], axis=1)

    if ringed:
        place = jnp.asarray(PLACE, jnp.int32)[dp]
        order = jnp.asarray(RING, jnp.int32)[(place - jnp.arange(8)) % 8]
        index = jnp.concatenate([order, me[None].astype(jnp.int32)])

        first = Gather(index)
        o_skip, o_time_a = first.out(32 * n_skip, width), first.out(32 * n_time, 2 * width)
        own = jnp.concatenate([skip_weight, time_a[:, :width], time_a[:, width:]], axis=0)
        layout = [
            (0, n_skip, o_skip, 0),
            (n_skip, n_time, o_time_a, 0),
            (n_skip + n_time, n_time, o_time_a, width),
        ]
        n_own = own.shape[0]
        ring_a = RingGather(jnp.concatenate([own, swap(own, 2)], axis=0))
        ring_a.step()
        triple, upper_w, time_b, out_weight = after(
            (triple, upper_w, time_b, out_weight), ring_a.found[0][2]
        )

        def to_core(entries):
            near = [swap(piece, 1) for _, _, piece in entries]
            for (k, row, piece), other in zip(entries, near):
                for array, flip in ((piece, 0), (other, 1)):
                    for part in range(row // n_own, (row + piece.shape[0]) // n_own):
                        at_row = part * n_own - row
                        first.add(
                            array,
                            k,
                            [
                                (at_row + at, count, out, (2 * part) ^ flip, 4 * count, count, column, 0)
                                for at, count, out, column in layout
                            ],
                        )
            return near

        rest = []
        for t in range(4):
            sides = jnp.concatenate(
                [
                    w[:, (t & 1) * (w.shape[1] // 2) : ((t & 1) + 1) * (w.shape[1] // 2)]
                    for w in (out_weight, time_b)
                ],
                axis=1,
            )
            rest.append(jnp.concatenate([triple[t], sides, upper_w[t]], axis=1))
        rest = by_place(rest, me)
        near = to_core(ring_a.found[:1])
        ring_a.step(*near, *rest)
        near = to_core(ring_a.found[1:3])
        time_far = swap(after(time_act, *rest), 2)
        second_far = swap(after(second_in, *rest), 2)
        first_far = swap(after(first_in, *rest), 2)
        rest = exchange(rest)
        ring_a.step(*near, *rest, time_act)
        near = to_core(ring_a.found[3:5])
        ring_a.step(*near, *tables, time_far)
        rest = jnp.concatenate(by_place(rest, me), axis=0)
        cut = 3 * local + width // 2, 3 * local + width // 2 + 3 * width // 2
        ring_b_own, ring_c_own, ring_d_own = after(
            (
                rest[:, : cut[0]],
                rest[:, cut[0] : cut[1]],
                jnp.concatenate([rest[:, cut[1] :], down_weight], axis=1),
            ),
            *ring_a.found[5][2:],
            *ring_a.found[6][2:],
        )
        ring_b, ring_c, ring_d = (RingGather(v) for v in (ring_b_own, ring_c_own, ring_d_own))
        step = ring_b.step()
        near = to_core(ring_a.found[5:9])
        first.arrays[0] = after(first.arrays[0], *step)
        step = ring_b.step()
        ring_c.step(*ring_b.found[1][2:])
        skip_full, time_a_full = first.run()

        def block_rows(ring, shape):
            gather = Gather(index)
            out = gather.out(*shape)
            for k, row, piece in ring.found:
                gather.add(piece, k, [(0, piece.shape[0], out, 0, width // 8, 0, 0, row)])
            return gather.run()[0]

        joined, time_act = after((joined, time_act), *step)
    else:
        first_far, second_far, time_far = swap(first_in, 2), swap(second_in, 2), swap(time_act, 2)
        skip_full, time_a_full, time_b_full, out_full = (
            lax.all_gather(w, ("dp", "seq"), axis=0, tiled=True)
            for w in (skip_weight, time_a, time_b, out_weight)
        )
        triple_full, up_full = (
            lax.all_gather(
                jnp.concatenate(by_place(exchange(by_place(parts, me)), me), axis=0),
                "dp",
                axis=0,
                tiled=True,
            )
            for parts in (triple, upper_w)
        )
        down_full = lax.all_gather(down_weight, "dp", axis=0, tiled=True)
        time_b_sides = [half(time_b_full, core), half(time_b_full, 1 - core)]
        out_sides = [half(out_full, core), half(out_full, 1 - core)]

    base = dot_nn(joined, skip_full)
    shift_a, scale_a = jnp.split(dot_nn(time_act, time_a_full), 2, axis=1)
    normed_a, inverse_a = norm_rows(base)
    hidden_own = (normed_a * (1.0 + scale_a) + shift_a).astype(bf16)
    if ringed:
        step = ring_b.step()
        hidden_own = after(hidden_own, second_far, *step)
        ring_c.step()
        ring_b.step(hidden_own)
        ring_c.step(hidden_own)
        hidden_a = spread(hidden_own, ring_b.front)
        wide = block_rows(ring_b, (width, cut[0]))
        triple_full = wide[:, : 3 * local]
        out_mine = wide[:, 3 * local :]
        out_sides = [out_mine, swap(out_mine, 1)]
    else:
        hidden_a = spread(hidden_own)
    qkv = [dot_nn(h, triple_full).astype(bf16) for h in hidden_a]
    if ringed:
        ring_c.step(qkv[0])
        ring_d.step(qkv[0])
        mine = block_rows(ring_c, (width, 3 * width // 2))
        time_b_sides = [mine, swap(mine, 1)]
        qkv = list(after(tuple(qkv), mine))
    att, logsum, query_rot, key_rot = attend(qkv, *tables)
    if ringed:
        att = after(att, time_b_sides[1], *ring_d.front)
    att = after(att, first_far)
    att_parts = [att[j * frames : (j + 1) * frames] for j in range(4)]
    attended = exchange(att_parts)
    row_near = swap(after(row_own, att), 1)
    row_far = jnp.concatenate([first_far, second_far, time_far], axis=1)
    row_inputs = [row_own, row_near, row_far, swap(row_far, 1)]
    upstream = cotangent.reshape(frames, width).astype(f32)
    time_act_b = time_act
    if ringed:
        ring_d.step(att)
        time_act_b = after(time_act, att)
    shift_b, scale_b, gate_b = jnp.split(
        merge(dot_nn(time_act_b, time_b_sides[0]), dot_nn(time_act_b, time_b_sides[1]), core),
        3,
        axis=1,
    )
    ffn_grad = (upstream * gate_b).astype(bf16)
    attended = list(after(tuple(attended), ffn_grad))
    ffn_grad = spread(ffn_grad)
    attended = jnp.concatenate(by_place(attended, me), axis=1)
    if ringed:
        step = ring_d.front
        ring_d.step(attended)
        attended = after(attended, *step)
    middle = base + merge(dot_nn(attended, out_sides[0]), dot_nn(attended, out_sides[1]), core)
    normed_b, inverse_b = norm_rows(middle)

    hidden_own = (normed_b * (1.0 + scale_b) + shift_b).astype(bf16)
    if ringed:
        hidden_own = after(hidden_own, *ring_d.front)
        ring_d.step()
    hidden_b = spread(hidden_own)
    if ringed:
        ffn_full = block_rows(ring_d, (width, 2 * local_hidden))
        up_full, down_full = ffn_full[:, :local_hidden], ffn_full[:, local_hidden:]
    hb = [jnp.concatenate(hidden_b[:2]), jnp.concatenate(hidden_b[2:])]
    fg = [jnp.concatenate(ffn_grad[:2]), jnp.concatenate(ffn_grad[2:])]
    upper = dot_nn(hb[1], up_full)
    acted_far = gelu_value(upper).astype(bf16)
    ug_far = (dot_nt(fg[1], down_full) * gelu_slope(upper)).astype(bf16)
    far = dot_nt(ug_far, up_full)
    far_low = far.astype(bf16)
    hb[0] = after(hb[0], far_low)
    upper = dot_nn(hb[0], up_full)
    sent = (far[:frames] + swap(far_low[frames:], 1).astype(f32)).astype(bf16)
    fg[0] = after(fg[0], sent)
    acted = [gelu_value(upper).astype(bf16), acted_far]
    ug = [(dot_nt(fg[0], down_full) * gelu_slope(upper)).astype(bf16), ug_far]
    own = dot_nt(ug[0], up_full)
    hidden_b_grad = (
        own[:frames] + swap(own[frames:].astype(bf16), 1).astype(f32) + swap(sent, 2).astype(f32)
    )
    acted, fg, ug, hb = after((acted, fg, ug, hb), own)
    part = [dot_nn(a, down_full) for a in acted]
    grad_down = dot_tn(acted[0], fg[0]) + dot_tn(acted[1], fg[1])
    grad_up = dot_tn(hb[0], ug[0]) + dot_tn(hb[1], ug[1])
    grad_ffn = jnp.concatenate([grad_up.astype(bf16), grad_down.astype(bf16)], axis=1)
    hidden_b_grad = after(hidden_b_grad, grad_ffn, *part)
    ffn, _ = collect(
        [part[0][:frames], part[0][frames:], part[1][:frames], part[1][frames:]], (hidden_b_grad,)
    )
    ffn_sum = lax.psum_scatter(grad_ffn, "dp", scatter_dimension=0, tiled=True).astype(f32)

    scale_b_grad = hidden_b_grad * normed_b
    middle_grad = upstream + norm_back(hidden_b_grad * (1.0 + scale_b), normed_b, inverse_b)
    branch_grad = middle_grad.astype(bf16)
    branch_sides = [half(branch_grad, core), half(branch_grad, 1 - core)]
    attended_grad = (
        dot_nt(branch_sides[0], out_sides[0]) + dot_nt(branch_sides[1], out_sides[1])
    ).astype(bf16)
    att_grad_parts = by_place([attended_grad[:, t * local : (t + 1) * local] for t in range(4)], me)
    att_grad = exchange(att_grad_parts)
    def to_columns(grads):
        return [
            jnp.concatenate([g[:, t * local : (t + 1) * local] for g in grads], axis=1) for t in range(4)
        ]

    modul_sent = by_place(to_columns([hidden_b_grad.astype(bf16), scale_b_grad.astype(bf16)]), me)
    modul_b_parts = exchange(after(tuple(modul_sent), *att_grad_parts))
    grad_out = [dot_tn(attended, side).astype(bf16) for side in branch_sides]
    near_out = swap(grad_out[1], 1)
    att_grad = after(tuple(att_grad), *modul_sent, *grad_out)
    triple_grad = attend_back(att_grad, qkv, query_rot, key_rot, att, logsum, *tables)
    triple_grad = after(triple_grad, *modul_b_parts, near_out)
    back = dot_nt(triple_grad, triple_full)
    far_low = back[3 * frames :].astype(bf16)
    triple_grad, ffn, hidden_a_all = after((triple_grad, ffn, jnp.concatenate(hidden_a)), far_low)
    grad_triple = dot_tn(hidden_a_all, triple_grad).astype(bf16)
    sent = (back[2 * frames : 3 * frames] + swap(far_low, 1).astype(f32)).astype(bf16)
    hidden_a_grad = (
        back[:frames]
        + swap(back[frames : 2 * frames].astype(bf16), 1).astype(f32)
        + swap(sent, 2).astype(f32)
    )
    modul_b_parts = after(tuple(modul_b_parts), sent, grad_triple)
    grad_time_b = sum(dot_tn(v[:, 2 * width :], g) for v, g in zip(row_inputs, modul_b_parts))
    grad_out = (grad_out[0].astype(f32) + near_out.astype(f32)).astype(bf16)
    ring_w = RingSum(
        [by_dp(g, groups) for g in (grad_time_b.astype(bf16), grad_out, grad_triple)], index, ringed
    )
    ring_w.step()
    ffn = after(ffn, grad_time_b, grad_triple)
    output = (middle + gate_b * ffn).astype(bf16).reshape(rows, frames, width)
    gate_b_grad = (upstream * ffn).astype(bf16)
    modul_b_grad = jnp.concatenate(
        [hidden_b_grad.astype(bf16), scale_b_grad.astype(bf16), gate_b_grad], axis=1
    )
    modul_sides = [half(modul_b_grad, core), half(modul_b_grad, 1 - core)]
    time_back_b = dot_nt(modul_sides[0], time_b_sides[0]) + dot_nt(modul_sides[1], time_b_sides[1])
    hidden_a_grad = after(hidden_a_grad, time_back_b)

    scale_a_grad = hidden_a_grad * normed_a
    modul_a_grad = jnp.concatenate([hidden_a_grad, scale_a_grad], axis=1).astype(bf16)
    modul_sent = by_place(
        to_columns([modul_a_grad[:, :width], modul_a_grad[:, width:], gate_b_grad]), me
    )
    modul_parts = exchange(modul_sent)
    base_grad = (
        middle_grad + norm_back(hidden_a_grad * (1.0 + scale_a), normed_a, inverse_a)
    ).astype(bf16)
    base_sent = by_place([base_grad[:, t * local : (t + 1) * local] for t in range(4)], me)
    base_parts = exchange(base_sent)
    step = ring_w.step(*base_sent)
    base_grad, modul_a_grad = after((base_grad, modul_a_grad), *base_sent)
    joined_grad = dot_nt(base_grad, skip_full)
    time_back = dot_nt(modul_a_grad, time_a_full) + time_back_b
    time_grad = (time_back * silu_slope(time_value)).reshape(rows, frames, width)
    modul_parts = after(tuple(modul_parts), joined_grad, *step)
    ring_w.step()
    grad_time_a = sum(dot_tn(v[:, 2 * width :], g) for v, g in zip(row_inputs, modul_parts))
    grad_skip = sum(dot_tn(v[:, : 2 * width], g) for v, g in zip(row_inputs, base_parts))
    rows_skip = n_skip // 2
    grad_skip = grad_skip.reshape(groups, 4, 2, rows_skip, local)
    grad_skip = jnp.concatenate([grad_skip[:, :, 0], grad_skip[:, :, 1]], axis=3)
    ring_l = RingSum(
        [
            grad_skip.reshape(groups, 4 * rows_skip, 2 * local).astype(bf16),
            by_dp(grad_time_a.astype(bf16), groups),
        ],
        index,
        ringed,
    )
    ring_l.step()
    ring_w.step()
    ring_l.step()
    wide_sum = ring_w.total()
    ring_l.step(wide_sum)
    parts = finish(
        after(jnp.concatenate([ffn_sum[:, :local_hidden], wide_sum], axis=1), *ring_l.front), me
    )
    ring_l.step()
    up_sum = jnp.concatenate(
        [
            p[:, g * hidden_block : (g + 1) * hidden_block]
            for g in range(groups)
            for p in parts
        ],
        axis=1,
    )
    split = local_hidden + 2 * local, local_hidden + 2 * local + width // 2
    by_blocks = lambda parts, start, i: jnp.concatenate(
        [p[:, start + i * local : start + (i + 1) * local] for p in parts], axis=1
    ).astype(f32)
    out_sum = halves_sum([p[:, split[0] : split[1]] for p in parts])
    triples = [
        jnp.concatenate(
            [
                p[:, split[1] + i * 128 + q * 384 : split[1] + (i + 1) * 128 + q * 384]
                for p in parts
                for q in range(2)
            ],
            axis=1,
        ).astype(f32)
        for i in range(3)
    ]
    last = finish(ring_l.total(), me)
    columns = [by_blocks(last, 0, i) for i in range(5)]
    time_b_sum = jnp.concatenate(
        [by_blocks(parts, local_hidden, 0), by_blocks(parts, local_hidden, 1), columns[4]], axis=1
    )
    skip_sum = jnp.concatenate(columns[:2], axis=0)
    time_a_sum = jnp.concatenate(columns[2:4], axis=1)
    return (
        output,
        joined_grad[:, :width].reshape(rows, frames, width),
        joined_grad[:, width:].reshape(rows, frames, width),
        time_grad,
        skip_sum,
        jnp.concatenate([time_a_sum, time_b_sum], axis=1),
        *triples,
        out_sum,
        up_sum.astype(f32),
        ffn_sum[:, local_hidden:],
    )


def solution(mesh):
    frames = P("dp", "seq", None)
    marks = P("dp", "seq")
    weight = P(("dp", "seq"), None)
    return jax.shard_map(
        on_device,
        mesh=mesh,
        in_specs=(frames,) * 3 + (marks,) * 3 + (weight,) * 8 + (frames,),
        out_specs=(frames,) * 4 + (weight,) * 8,
        check_vma=False,
    )
```

```python
import functools

import jax
import jax.numpy as jnp
from jax import lax
from jax.experimental import pallas as pl
from jax.experimental.pallas import tpu as pltpu
from jax.sharding import PartitionSpec as P

HD = 64
NEG = 1e30
norm_eps = 1e-06
gelu_coef = 0.7978845608028654
f32, bf16 = jnp.float32, jnp.bfloat16

RING = (0, 2, 4, 6, 7, 5, 3, 1)
PLACE = tuple(RING.index(d) for d in range(8))


def dot_nt(a, b):
    return lax.dot_general(a, b, (((1,), (1,)), ((), ())), preferred_element_type=f32)


def dot_nn(a, b):
    return lax.dot_general(a, b, (((1,), (0,)), ((), ())), preferred_element_type=f32)


def dot_tn(a, b):
    return lax.dot_general(a, b, (((0,), (0,)), ((), ())), preferred_element_type=f32)


def silu_slope(v):
    sig = jax.nn.sigmoid(v)
    return sig * (1.0 + v * (1.0 - sig))


def gelu_value(u):
    return 0.5 * u * (1.0 + jnp.tanh(gelu_coef * (u + 0.044715 * u * u * u)))


def gelu_slope(u):
    inner = jnp.tanh(gelu_coef * (u + 0.044715 * u * u * u))
    return 0.5 * (1.0 + inner) + 0.5 * u * (1.0 - inner * inner) * gelu_coef * (
        1.0 + 3.0 * 0.044715 * u * u
    )


def norm_rows(v):
    mean = jnp.mean(v, axis=-1, keepdims=True)
    centred = v - mean
    inverse = lax.rsqrt(jnp.mean(centred * centred, axis=-1, keepdims=True) + norm_eps)
    return (centred * inverse, inverse)


def norm_back(grad, normed, inverse):
    return inverse * (
        grad
        - jnp.mean(grad, axis=-1, keepdims=True)
        - normed * jnp.mean(grad * normed, axis=-1, keepdims=True)
    )

def lanes_of(shape):
    return lax.broadcasted_iota(jnp.int32, shape, 1)


def swap_halves(v):
    lane = lanes_of(v.shape)
    return jnp.where(lane % HD < HD // 2, pltpu.roll(v, 128 - HD // 2, 1), pltpu.roll(v, HD // 2, 1))


def three_parts(v):
    hi = v.astype(bf16)
    rest = v - hi.astype(f32)
    mid = rest.astype(bf16)
    low = (rest - mid.astype(f32)).astype(bf16)
    return hi, mid, low


def attend_kernel(pieces, block, scale, *refs):
    qkv = refs[:pieces]
    cos_ref, sin_ref, qext_ref, kext_ref = refs[pieces : pieces + 4]
    att_ref, lse_ref, qrot_ref, krot_ref = refs[pieces + 4 : pieces + 8]
    kx, vx = refs[pieces + 8 :]
    step = pl.program_id(1)
    frames = qkv[0].shape[0]
    per_piece = frames // block

    @pl.when(step == 0)
    def _():
        for j in range(pieces):
            rows = pl.ds(j * frames, frames)
            k = qkv[j][:, 128:256].astype(f32)
            k = (k * cos_ref[rows, :] + swap_halves(k) * sin_ref[rows, :]).astype(bf16)
            krot_ref[rows, :] = k
            v = qkv[j][:, 256:384]
            ext = kext_ref[rows, :]
            lane = lanes_of(k.shape)
            one = jnp.where(lane % HD == 0, 1.0, 0.0).astype(bf16)
            low_lane = lane < HD
            kx[0, rows, :] = jnp.where(low_lane, k, ext)
            kx[1, rows, :] = jnp.where(low_lane, ext, k)
            vx[0, rows, :] = jnp.where(low_lane, v, one)
            vx[1, rows, :] = jnp.where(low_lane, one, v)

    rows = pl.ds(pl.multiple_of(step * block, block), block)
    for j in range(pieces):

        @pl.when(step // per_piece == j)
        def _(j=j):
            sub = pl.ds(pl.multiple_of((step - j * per_piece) * block, block), block)
            q = qkv[j][sub, 0:128].astype(f32)
            q = (q * cos_ref[rows, :] + swap_halves(q) * sin_ref[rows, :]).astype(bf16)
            qrot_ref[...] = (q.astype(f32) * scale).astype(bf16)

    q = qrot_ref[...]
    ext = qext_ref[rows, :]
    low_lane = lanes_of(q.shape) < HD
    outs = []
    for h in range(2):
        qx = jnp.where(low_lane, q, ext) if h == 0 else jnp.where(low_lane, ext, q)
        scores = dot_nt(qx, kx[h])
        top = jnp.max(scores, axis=1, keepdims=True)
        expo = jnp.exp(scores - top)
        mixed = dot_nn(expo.astype(bf16), vx[h])
        total = mixed[:, HD : HD + 1] if h == 0 else mixed[:, 0:1]
        outs.append((mixed / total, top + jnp.log(total)))
    low_out = lanes_of((block, 128)) < HD
    att_ref[...] = jnp.where(low_out, outs[0][0], outs[1][0]).astype(bf16)
    lse_ref[...] = jnp.where(low_out, outs[0][1], outs[1][1])


def attend(qkv, cosine, sine, qext, kext, block=384, scale=HD**-0.5):
    pieces = len(qkv)
    frames = qkv[0].shape[0]
    total = pieces * frames
    full = lambda a: pl.BlockSpec(a.shape, lambda p, i: (0, 0))
    tile = pl.BlockSpec((block, 128), lambda p, i: (i, p))
    return pl.pallas_call(
        functools.partial(attend_kernel, pieces, block, scale),
        grid=(2, total // block),
        in_specs=[pl.BlockSpec((frames, 384), lambda p, i: (0, p))] * pieces
        + [full(a) for a in (cosine, sine, qext, kext)],
        out_specs=[tile, tile, tile, pl.BlockSpec((total, 128), lambda p, i: (0, p))],
        out_shape=[jax.ShapeDtypeStruct((total, 256), t) for t in (bf16, f32, bf16, bf16)],
        scratch_shapes=[pltpu.VMEM((2, total, 128), bf16), pltpu.VMEM((2, total, 128), bf16)],
        compiler_params=pltpu.CompilerParams(vmem_limit_bytes=24 * 2**20),
        cost_estimate=pl.CostEstimate(
            flops=8 * total * total * 256, bytes_accessed=total * 4096, transcendentals=4 * total * total
        ),
        name="attend",
    )(*qkv, cosine, sine, qext, kext)


def attend_back_kernel(pieces, block, scale, *refs):
    grads = refs[:pieces]
    values = refs[pieces : 2 * pieces]
    qrot_ref, krot_ref, att_ref, lse_ref, cos_ref, sin_ref, qext_ref, kext_ref = refs[2 * pieces : 2 * pieces + 8]
    out_ref = refs[2 * pieces + 8]
    qx, gx, qm, gm, dq = refs[2 * pieces + 9 :]
    step = pl.program_id(1)
    last = pl.num_programs(1) - 1
    frames = grads[0].shape[0]
    per_piece = frames // block

    @pl.when(step == 0)
    def _():
        for j in range(pieces):
            rows = pl.ds(j * frames, frames)
            q = qrot_ref[rows, :]
            g = grads[j][...]
            lane = lanes_of(q.shape)
            low_lane = lane < HD
            spot = lane % HD
            prod = g.astype(f32) * att_ref[rows, :].astype(f32)
            zero = jnp.zeros_like(q)
            lse = lse_ref[rows, :]
            for h in range(2):
                own = low_lane if h == 0 else jnp.logical_not(low_lane)
                lse_h = lse[:, 0:1] if h == 0 else lse[:, HD : HD + 1]
                delta = jnp.sum(jnp.where(own, prod, 0.0), axis=1, keepdims=True)
                a, b, c = (t.astype(f32) for t in three_parts(-lse_h))
                part = jnp.where(spot == 4, a, jnp.where(spot == 5, b, jnp.where(spot == 6, c, qext_ref[rows, :].astype(f32))))
                qx[h, rows, :] = jnp.where(own, q, part.astype(bf16))
                a, b, c = (t.astype(f32) for t in three_parts(-delta))
                part = jnp.where(spot == 0, a, jnp.where(spot == 1, b, jnp.where(spot == 2, c, 0.0)))
                gx[h, rows, :] = jnp.where(own, g, part.astype(bf16))
                qm[h, rows, :] = jnp.where(own, q, zero)
                gm[h, rows, :] = jnp.where(own, g, zero)
        dq[...] = jnp.zeros_like(dq)

    rows = pl.ds(pl.multiple_of(step * block, block), block)
    for j in range(pieces):

        @pl.when(step // per_piece == j)
        def _(j=j):
            sub = pl.ds(pl.multiple_of((step - j * per_piece) * block, block), block)
            k = krot_ref[rows, :]
            v = values[j][sub, 256:384]
            ext = kext_ref[rows, :]
            lane = lanes_of(k.shape)
            low_lane = lane < HD
            three = jnp.where(lane % HD < 3, 1.0, 0.0).astype(bf16)
            zero = jnp.zeros_like(k)
            small = k.astype(f32) * scale
            dk = jnp.zeros((block, 128), f32)
            dv = jnp.zeros((block, 128), f32)
            for h in range(2):
                own = low_lane if h == 0 else jnp.logical_not(low_lane)
                kx = jnp.where(own, k, ext)
                vx = jnp.where(own, v, three)
                probs = jnp.exp(dot_nt(kx, qx[h]))
                grad = (probs * dot_nt(vx, gx[h])).astype(bf16)
                dv = dv + dot_nn(probs.astype(bf16), gm[h])
                dk = dk + dot_nn(grad, qm[h])
                turned = jnp.transpose(jnp.where(own, small, 0.0)).astype(bf16)
                dq[...] += dot_nn(turned, grad)
            dk = dk * cos_ref[rows, :] - swap_halves(dk) * sin_ref[rows, :]
            out_ref[rows, 128:256] = dk.astype(bf16)
            out_ref[rows, 256:384] = dv.astype(bf16)

    @pl.when(step == last)
    def _():
        g = jnp.transpose(dq[...])
        g = g * cos_ref[...] - swap_halves(g) * sin_ref[...]
        out_ref[:, 0:128] = g.astype(bf16)


def attend_back(grads, qkv, qrot, krot, att, lse, cosine, sine, qext, kext, block=384, scale=HD**-0.5):
    pieces = len(grads)
    frames = grads[0].shape[0]
    total = pieces * frames
    full = lambda a: pl.BlockSpec(a.shape, lambda p, i: (0, 0))
    return pl.pallas_call(
        functools.partial(attend_back_kernel, pieces, block, scale),
        grid=(2, total // block),
        in_specs=[pl.BlockSpec((frames, 128), lambda p, i: (0, p))] * pieces
        + [pl.BlockSpec((frames, 384), lambda p, i: (0, p))] * pieces
        + [pl.BlockSpec((total, 128), lambda p, i: (0, p))] * 4
        + [full(a) for a in (cosine, sine, qext, kext)],
        out_specs=pl.BlockSpec((total, 384), lambda p, i: (0, p)),
        out_shape=jax.ShapeDtypeStruct((total, 768), bf16),
        scratch_shapes=[pltpu.VMEM((2, total, 128), bf16)] * 4 + [pltpu.VMEM((128, total), f32)],
        compiler_params=pltpu.CompilerParams(vmem_limit_bytes=34 * 2**20),
        cost_estimate=pl.CostEstimate(
            flops=20 * total * total * 256, bytes_accessed=total * 8192, transcendentals=4 * total * total
        ),
        name="attend_back",
    )(*grads, *qkv, qrot, krot, att, lse, cosine, sine, qext, kext)


def frame_tables(seg, pos, valid):
    half = HD // 2
    freq = 10000.0 ** (-jnp.arange(half, dtype=f32) / half)
    angle = pos.astype(f32)[:, None] * freq
    cosine, sine = jnp.cos(angle), jnp.sin(angle)
    cosine = jnp.concatenate([cosine] * 4, axis=1)
    sine = jnp.concatenate([-sine, sine, -sine, sine], axis=1)
    spot = jnp.arange(128)[None, :] % HD
    seg, valid = seg[:, None], valid[:, None] > 0
    qext = jnp.where((spot < 3) & (spot != seg) | (spot == 3), -NEG, 0.0).astype(bf16)
    kext = ((spot == seg) & (spot < 3) | (spot == 3) & ~valid | (spot >= 4) & (spot < 7)).astype(bf16)
    return cosine, sine, qext, kext


def swap(v, mask):
    return lax.ppermute(v, "seq", [(i, i ^ mask) for i in range(4)])


def spread(v, before=()):
    near = swap(v, 1)
    far = swap(v, 2)
    return [v, near, far, swap(after(far, *before) if before else far, 1)]


def collect(parts, wait=()):
    low = [part.astype(bf16) for part in parts]
    if wait:
        low = list(after(tuple(low), *wait))
    far_near = swap(low[3], 1)
    near = swap(low[1], 1)
    sent = (low[2].astype(f32) + far_near.astype(f32)).astype(bf16)
    far = swap(sent, 2)
    return parts[0] + near.astype(f32) + far.astype(f32), sent


def exchange(parts):
    return [parts[0], swap(parts[1], 1), swap(parts[2], 2), swap(parts[3], 3)]


def by_place(parts, me):
    odd, high = (me & 1) == 1, (me & 2) == 2
    parts = [jnp.where(odd, parts[t ^ 1], parts[t]) for t in range(4)]
    return [jnp.where(high, parts[t ^ 2], parts[t]) for t in range(4)]


def ring_step(v, step):
    return lax.ppermute(v, "dp", [(RING[i], RING[(i + step) % 8]) for i in range(8)])


class RingGather:
    def __init__(self, v):
        self.found, self.front, self.count = [(0, 0, v)], (v, v), 0

    def step(self, *before):
        one, other = after(self.front, *before) if before else self.front
        self.count += 1
        k = self.count
        if k < 4:
            self.front = ring_step(one, 1), ring_step(other, -1)
            self.found += [(k, 0, self.front[0]), (8 - k, 0, self.front[1])]
        else:
            middle = one.shape[0] // 2
            self.front = ring_step(one[:middle], 1), ring_step(other[middle:], -1)
            self.found += [(4, 0, self.front[0]), (4, middle, self.front[1])]
        return self.front


def ring_add_kernel(k, count, index_ref, *refs):
    plus, minus = refs[:count], refs[count : 2 * count]
    moving = refs[2 * count : -1 if k == 0 else -2]
    outs = refs[-1:] if k == 0 else refs[-2:]
    rows = plus[0].shape[1]
    middle = rows // 2
    upper, lower = slice(0, middle), slice(middle, rows)
    start = 0
    for i in range(count):
        columns = slice(start, start + plus[i].shape[2])
        start += plus[i].shape[2]
        if k == 4:
            outs[0][:, columns] = plus[i][0, upper, :].astype(bf16)
            outs[1][:, columns] = plus[i][0, lower, :].astype(bf16)
            continue
        ahead = plus[i][0].astype(f32)
        if k == 0:
            outs[0][:, columns] = (
                ahead + moving[0][:, columns].astype(f32) + moving[1][:, columns].astype(f32)
            )
            continue
        behind = minus[i][0].astype(f32)
        one, other = moving[0][:, columns].astype(f32), moving[1][:, columns].astype(f32)
        if k == 3:
            outs[0][upper, columns] = (ahead[upper] + one).astype(bf16)
            outs[0][lower, columns] = ahead[lower].astype(bf16)
            outs[1][upper, columns] = behind[upper].astype(bf16)
            outs[1][lower, columns] = (behind[lower] + other).astype(bf16)
        else:
            outs[0][:, columns] = (ahead + one).astype(bf16)
            outs[1][:, columns] = (behind + other).astype(bf16)


def ring_add(index, arrays, moving, k):
    rows, columns = arrays[0].shape[1], sum(a.shape[2] for a in arrays)
    ahead = [pl.BlockSpec((1, rows, a.shape[2]), lambda i, index: (index[(8 - k) % 8], 0, 0)) for a in arrays]
    behind = [pl.BlockSpec((1, rows, a.shape[2]), lambda i, index: (index[k], 0, 0)) for a in arrays]
    whole = lambda shape: pl.BlockSpec(shape, lambda i, index: (0, 0))
    height = rows // 2 if k == 4 else rows
    n_out = 1 if k == 0 else 2
    return pl.pallas_call(
        functools.partial(ring_add_kernel, k, len(arrays)),
        grid_spec=pltpu.PrefetchScalarGridSpec(
            num_scalar_prefetch=1,
            grid=(1,),
            in_specs=ahead + behind + [whole(m.shape) for m in moving],
            out_specs=[whole((height, columns))] * n_out,
        ),
        out_shape=[jax.ShapeDtypeStruct((height, columns), f32 if k == 0 else bf16)] * n_out,
        compiler_params=pltpu.CompilerParams(vmem_limit_bytes=16 * 2**20),
        name="ring_add",
    )(index, *arrays, *arrays, *moving)


class RingSum:
    def __init__(self, arrays, index, ringed):
        self.arrays, self.index, self.ringed = arrays, index, ringed
        self.front, self.count = (), 4

    def step(self, *before):
        if self.ringed:
            arrays, front = self.arrays, self.front
            if before:
                arrays, front = after((arrays, front), *before)
            moving = ring_add(self.index, arrays, front, self.count)
            self.front = ring_step(moving[0], 1), ring_step(moving[1], -1)
            self.count -= 1
        return self.front

    def total(self):
        if self.ringed:
            return ring_add(self.index, self.arrays, self.front, 0)[0]
        low = jnp.concatenate([a.astype(bf16) for a in self.arrays], axis=2)
        return lax.psum_scatter(low, "dp", scatter_dimension=0).astype(f32)


def after(v, *others):
    return lax.optimization_barrier((v, *others))[0]


def assemble_kernel(copies, n_in, n_out, index_ref, *refs):
    arrays, outs, sems = refs[:n_in], refs[n_in : n_in + n_out], refs[-1]
    moves = []
    me = index_ref[8]
    for number, (a, row, count, out, k, j, per_dp, per_seq, column, more) in enumerate(copies):
        start = index_ref[k] * per_dp + jnp.bitwise_xor(me, j) * per_seq + more
        target = outs[out].at[
            pl.ds(pl.multiple_of(start, count), count), pl.ds(column, arrays[a].shape[1])
        ]
        moves.append(
            pltpu.make_async_copy(arrays[a].at[pl.ds(row, count), :], target, sems.at[number])
        )
    for move in moves:
        move.start()
    for move in moves:
        move.wait()


def assemble(index, arrays, copies, shapes):
    anywhere = pl.BlockSpec(memory_space=pl.ANY)
    return pl.pallas_call(
        functools.partial(assemble_kernel, tuple(copies), len(arrays), len(shapes)),
        grid_spec=pltpu.PrefetchScalarGridSpec(
            num_scalar_prefetch=1,
            grid=(1,),
            in_specs=[anywhere] * len(arrays),
            out_specs=[pl.BlockSpec(shape, lambda i, index: (0, 0)) for shape in shapes],
            scratch_shapes=[pltpu.SemaphoreType.DMA((len(copies),))],
        ),
        out_shape=[jax.ShapeDtypeStruct(shape, bf16) for shape in shapes],
        compiler_params=pltpu.CompilerParams(vmem_limit_bytes=8 * 2**20 + 5 * sum(r * c for r, c in shapes)),
        name="assemble",
    )(index, *arrays)


class Gather:
    def __init__(self, index):
        self.index, self.arrays, self.copies, self.shapes = index, [], [], []

    def out(self, rows, columns):
        self.shapes.append((rows, columns))
        return len(self.shapes) - 1

    def add(self, piece, k, blocks):
        self.arrays.append(piece)
        for row, count, out, j, per_dp, per_seq, column, more in blocks:
            self.copies.append(
                (len(self.arrays) - 1, row, count, out, k, j, per_dp, per_seq, column, more)
            )

    def run(self):
        return assemble(self.index, self.arrays, self.copies, self.shapes)


def half(v, which):
    middle = v.shape[1] // 2
    return jnp.where(which == 1, v[:, middle:], v[:, :middle])


def merge(mine, other, core):
    return jnp.concatenate(
        [jnp.where(core == 1, other, mine), jnp.where(core == 1, mine, other)], axis=1
    )


def by_dp(grad, groups):
    return grad.reshape(groups, grad.shape[0] // groups, grad.shape[1])


def finish(block, me):
    rows = block.shape[0] // 4
    low = block.astype(bf16)
    parts = by_place([low[t * rows : (t + 1) * rows] for t in range(4)], me)
    return by_place(exchange(parts), me)


def halves_sum(parts):
    total = [parts[c].astype(f32) + parts[2 + c].astype(f32) for c in range(2)]
    return jnp.concatenate(total, axis=1)


def on_device(
    layer_input,
    skip_input,
    time_embed,
    segment_ids,
    positions,
    valid_mask,
    skip_weight,
    time_weight,
    query_weight,
    key_weight,
    value_weight,
    out_weight,
    up_weight,
    down_weight,
    cotangent,
):
    rows, frames, width = layer_input.shape
    hidden = up_weight.shape[1]
    groups = lax.axis_size("dp")
    me, dp = lax.axis_index("seq"), lax.axis_index("dp")
    local = width // 4
    local_hidden = hidden // 4

    core = me & 1
    hidden_block = hidden // (groups * 4)
    ringed = groups == 8
    first_in, second_in = layer_input.reshape(frames, width), skip_input.reshape(frames, width)
    time_a, time_b = time_weight[:, : 2 * width], time_weight[:, 2 * width :]
    n_skip, n_time = skip_weight.shape[0], time_weight.shape[0]

    def needed():
        triple = [
            jnp.concatenate(
                [
                    w[:, t * local + p * 128 : t * local + (p + 1) * 128]
                    for p in range(2)
                    for w in (query_weight, key_weight, value_weight)
                ],
                axis=1,
            )
            for t in range(4)
        ]
        upper_w = [
            jnp.concatenate(
                [
                    up_weight[:, (g * 4 + t) * hidden_block : (g * 4 + t + 1) * hidden_block]
                    for g in range(groups)
                ],
                axis=1,
            )
            for t in range(4)
        ]
        return triple, upper_w

    triple, upper_w = needed()
    index = None
    marks = jnp.concatenate(spread(jnp.concatenate([segment_ids, positions, valid_mask])), axis=1)
    tables = frame_tables(marks[0], marks[1], marks[2])
    time_value = time_embed.reshape(frames, width).astype(f32)
    time_act = (time_value * jax.nn.sigmoid(time_value)).astype(bf16)
    joined = jnp.concatenate([first_in, second_in], axis=1)
    row_own = jnp.concatenate([first_in, second_in, time_act], axis=1)

    if ringed:
        place = jnp.asarray(PLACE, jnp.int32)[dp]
        order = jnp.asarray(RING, jnp.int32)[(place - jnp.arange(8)) % 8]
        index = jnp.concatenate([order, me[None].astype(jnp.int32)])

        first = Gather(index)
        o_skip, o_time_a = first.out(32 * n_skip, width), first.out(32 * n_time, 2 * width)
        own = jnp.concatenate([skip_weight, time_a[:, :width], time_a[:, width:]], axis=0)
        layout = [
            (0, n_skip, o_skip, 0),
            (n_skip, n_time, o_time_a, 0),
            (n_skip + n_time, n_time, o_time_a, width),
        ]
        n_own = own.shape[0]
        ring_a = RingGather(jnp.concatenate([own, swap(own, 2)], axis=0))
        ring_a.step()
        triple, upper_w, time_b, out_weight = after(
            (triple, upper_w, time_b, out_weight), ring_a.found[0][2]
        )

        def to_core(gather, entries, layout, n_own):
            near = [swap(piece, 1) for _, _, piece in entries]
            for (k, row, piece), other in zip(entries, near):
                for array, flip in ((piece, 0), (other, 1)):
                    for part in range(row // n_own, (row + piece.shape[0]) // n_own):
                        at_row = part * n_own - row
                        gather.add(
                            array,
                            k,
                            [
                                (at_row + at, count, out, (2 * part) ^ flip, 4 * count, count, column, 0)
                                for at, count, out, column in layout
                            ],
                        )
            return near

        rest = []
        for t in range(4):
            sides = [
                w[:, (t & 1) * (w.shape[1] // 2) : ((t & 1) + 1) * (w.shape[1] // 2)]
                for w in (out_weight, time_b)
            ]
            rest.append(jnp.concatenate([triple[t], *sides, upper_w[t]], axis=1))
        rest = by_place(rest, me)
        near = to_core(first, ring_a.found[:1], layout, n_own)
        ring_a.step(*near, *rest)
        near = to_core(first, ring_a.found[1:3], layout, n_own)
        rest = exchange(after(tuple(rest), ring_a.found[1][2]))
        time_far = swap(after(time_act, rest[2]), 2)
        second_far = swap(after(second_in, time_far), 2)
        ring_a.step(*near, *rest)
        near = to_core(first, ring_a.found[3:5], layout, n_own)
        ring_a.step(*near, *tables, time_far)
        rest = jnp.concatenate(by_place(rest, me), axis=0)
        cut = 3 * local + width // 2, 3 * local + 2 * width
        ring_b_own, ring_c_own, ring_d_own = after(
            (
                rest[:, : cut[0]],
                rest[:, cut[0] : cut[1]],
                jnp.concatenate([rest[:, cut[1] :], down_weight], axis=1),
            ),
            *ring_a.found[5][2:],
            *ring_a.found[6][2:],
        )
        ring_b, ring_c, ring_d = (RingGather(v) for v in (ring_b_own, ring_c_own, ring_d_own))
        near = to_core(first, ring_a.found[5:9], layout, n_own)
        ring_b.step()
        skip_full, time_a_full = first.run()
        ring_b.step(skip_full)

        def block_rows(ring, shape):
            gather = Gather(index)
            out = gather.out(*shape)
            for k, row, piece in ring.found:
                gather.add(piece, k, [(0, piece.shape[0], out, 0, width // 8, 0, 0, row)])
            return gather.run()[0]

    else:
        first_far, second_far, time_far = swap(first_in, 2), swap(second_in, 2), swap(time_act, 2)
        skip_full, time_a_full, time_b_full, out_full = (
            lax.all_gather(w, ("dp", "seq"), axis=0, tiled=True)
            for w in (skip_weight, time_a, time_b, out_weight)
        )
        triple_full, up_full = (
            lax.all_gather(
                jnp.concatenate(by_place(exchange(by_place(parts, me)), me), axis=0),
                "dp",
                axis=0,
                tiled=True,
            )
            for parts in (triple, upper_w)
        )
        down_full = lax.all_gather(down_weight, "dp", axis=0, tiled=True)
        out_sides = [half(out_full, core), half(out_full, 1 - core)]
        time_b_sides = [half(time_b_full, core), half(time_b_full, 1 - core)]

    base = dot_nn(joined, skip_full)
    shift_a, scale_a = jnp.split(dot_nn(time_act, time_a_full), 2, axis=1)
    normed_a, inverse_a = norm_rows(base)
    hidden_own = (normed_a * (1.0 + scale_a) + shift_a).astype(bf16)
    if ringed:
        hidden_own = after(hidden_own, second_far)
        ring_c.step(skip_full)
        ring_b.step(hidden_own)
        ring_b.step()
        ring_c.step(*ring_b.found[5][2:])
        ring_c.step(*ring_b.front)
        hidden_a = spread(hidden_own, ring_b.front)
        first_far = swap(after(first_in, hidden_a[2]), 2)
        wide = block_rows(ring_b, (width, cut[0]))
        triple_full = wide[:, : 3 * local]
        out_mine = wide[:, 3 * local :]
        out_sides = [out_mine, swap(after(out_mine, hidden_a[3]), 1)]
        ring_d.step(hidden_a[2])
    else:
        hidden_a = spread(hidden_own)
    qkv = [dot_nn(h, triple_full).astype(bf16) for h in hidden_a]
    att, logsum, query_rot, key_rot = attend(qkv, *tables)
    time_act_b = after(time_act, att)
    if ringed:
        att = after(att, *ring_c.front, *ring_d.front)
    att = after(att, first_far)
    att_parts = [att[j * frames : (j + 1) * frames] for j in range(4)]
    attended = exchange(att_parts)
    if ringed:
        ring_c.step(att)
        mine = block_rows(ring_c, (width, 3 * width // 2))
        time_b_sides = [mine, swap(mine, 1)]
        ring_d.step(att)
    shift_b, scale_b, gate_b = jnp.split(
        merge(dot_nn(time_act_b, time_b_sides[0]), dot_nn(time_act_b, time_b_sides[1]), core),
        3,
        axis=1,
    )
    upstream = cotangent.reshape(frames, width).astype(f32)
    ffn_grad = (upstream * gate_b).astype(bf16)
    attended = list(after(tuple(attended), ffn_grad))
    ffn_grad = spread(ffn_grad)
    attended = jnp.concatenate(by_place(attended, me), axis=1)
    if ringed:
        ring_d.step(attended)
    middle = base + merge(dot_nn(attended, out_sides[0]), dot_nn(attended, out_sides[1]), core)
    normed_b, inverse_b = norm_rows(middle)

    hidden_own = (normed_b * (1.0 + scale_b) + shift_b).astype(bf16)
    hidden_b = spread(hidden_own, ring_d.front if ringed else ())
    if ringed:
        ring_d.step()
    if ringed:
        ffn_full = block_rows(ring_d, (width, 2 * local_hidden))
        up_full, down_full = ffn_full[:, :local_hidden], ffn_full[:, local_hidden:]
    row_near = swap(after(row_own, hidden_b[3]), 1)
    row_far = jnp.concatenate([first_far, second_far, time_far], axis=1)
    row_inputs = [row_own, row_near, row_far, swap(after(row_far, hidden_b[3]), 1)]
    hb = [jnp.concatenate(hidden_b[:2]), jnp.concatenate(hidden_b[2:])]
    fg = [jnp.concatenate(ffn_grad[:2]), jnp.concatenate(ffn_grad[2:])]
    upper = dot_nn(hb[1], up_full)
    acted_far = gelu_value(upper).astype(bf16)
    part_far = dot_nn(acted_far, down_full)
    part_low = part_far.astype(bf16)
    fg[1] = after(fg[1], part_low)
    ug_far = (dot_nt(fg[1], down_full) * gelu_slope(upper)).astype(bf16)
    part_sent = (part_far[:frames] + swap(part_low[frames:], 1).astype(f32)).astype(bf16)
    far = dot_nt(after(ug_far, part_sent), up_full)
    far_low = far.astype(bf16)
    hb[0] = after(hb[0], far_low)
    upper = dot_nn(hb[0], up_full)
    sent = (far[:frames] + swap(far_low[frames:], 1).astype(f32)).astype(bf16)
    fg[0] = after(fg[0], sent)
    acted = [gelu_value(upper).astype(bf16), acted_far]
    ug = [(dot_nt(fg[0], down_full) * gelu_slope(upper)).astype(bf16), ug_far]
    own = dot_nt(ug[0], up_full)
    hidden_b_grad = (
        own[:frames] + swap(own[frames:].astype(bf16), 1).astype(f32) + swap(sent, 2).astype(f32)
    )
    acted, fg, ug, hb = after((acted, fg, ug, hb), own, row_near, row_inputs[3])
    part = dot_nn(acted[0], down_full)
    ffn = (
        part[:frames]
        + swap(part[frames:].astype(bf16), 1).astype(f32)
        + swap(part_sent, 2).astype(f32)
    )
    grad_down = dot_tn(acted[0], fg[0]) + dot_tn(acted[1], fg[1])
    grad_up = dot_tn(hb[0], ug[0]) + dot_tn(hb[1], ug[1])
    grad_ffn = jnp.concatenate([grad_up.astype(bf16), grad_down.astype(bf16)], axis=1)
    hidden_b_grad = after(hidden_b_grad, grad_ffn, part)
    ffn_sum = lax.psum_scatter(grad_ffn, "dp", scatter_dimension=0, tiled=True).astype(f32)

    scale_b_grad = hidden_b_grad * normed_b
    middle_grad = upstream + norm_back(hidden_b_grad * (1.0 + scale_b), normed_b, inverse_b)
    branch_grad = middle_grad.astype(bf16)
    branch_sides = [half(branch_grad, core), half(branch_grad, 1 - core)]
    attended_grad = (
        dot_nt(branch_sides[0], out_sides[0]) + dot_nt(branch_sides[1], out_sides[1])
    ).astype(bf16)
    att_grad_parts = by_place([attended_grad[:, t * local : (t + 1) * local] for t in range(4)], me)
    att_grad = exchange(att_grad_parts)
    def to_columns(grads):
        return [
            jnp.concatenate([g[:, t * local : (t + 1) * local] for g in grads], axis=1) for t in range(4)
        ]

    ffn = after(ffn, *att_grad_parts)
    output = (middle + gate_b * ffn).astype(bf16).reshape(rows, frames, width)
    modul_b_grad = [v.astype(bf16) for v in (hidden_b_grad, scale_b_grad, upstream * ffn)]
    modul_sent = by_place(to_columns(modul_b_grad), me)
    modul_b_parts = exchange(modul_sent)
    grad_out = [dot_tn(attended, side).astype(bf16) for side in branch_sides]
    near_out = swap(grad_out[1], 1)
    att_grad = after(tuple(att_grad), *modul_sent, *grad_out, row_inputs[3])
    triple_grad = attend_back(att_grad, qkv, query_rot, key_rot, att, logsum, *tables)
    triple_grad = after(triple_grad, *modul_b_parts, near_out)
    back = dot_nt(triple_grad, triple_full)
    far_low = back[3 * frames :].astype(bf16)
    triple_grad, modul_b_grad, hidden_a_all = after(
        (triple_grad, tuple(modul_b_grad), jnp.concatenate(hidden_a)), far_low
    )
    grad_triple = dot_tn(hidden_a_all, triple_grad).astype(bf16)
    sent = (back[2 * frames : 3 * frames] + swap(far_low, 1).astype(f32)).astype(bf16)
    hidden_a_grad = (
        back[:frames]
        + swap(back[frames : 2 * frames].astype(bf16), 1).astype(f32)
        + swap(sent, 2).astype(f32)
    )
    modul_b_parts = after(tuple(modul_b_parts), sent, grad_triple)
    grad_time_b = sum(dot_tn(v[:, 2 * width :], g) for v, g in zip(row_inputs, modul_b_parts))
    grad_out = (grad_out[0].astype(f32) + near_out.astype(f32)).astype(bf16)
    ring_w = RingSum(
        [by_dp(g, groups) for g in (grad_time_b.astype(bf16), grad_out, grad_triple)], index, ringed
    )
    ring_w.step()
    modul_b_grad = jnp.concatenate(modul_b_grad, axis=1)
    time_back_b = dot_nt(half(modul_b_grad, core), time_b_sides[0]) + dot_nt(
        half(modul_b_grad, 1 - core), time_b_sides[1]
    )
    hidden_a_grad = after(hidden_a_grad, time_back_b)

    scale_a_grad = hidden_a_grad * normed_a
    modul_a_grad = jnp.concatenate([hidden_a_grad, scale_a_grad], axis=1).astype(bf16)
    modul_sent = by_place(to_columns([modul_a_grad[:, :width], modul_a_grad[:, width:]]), me)
    modul_parts = exchange(modul_sent)
    base_grad = (
        middle_grad + norm_back(hidden_a_grad * (1.0 + scale_a), normed_a, inverse_a)
    ).astype(bf16)
    base_sent = by_place([base_grad[:, t * local : (t + 1) * local] for t in range(4)], me)
    base_parts = exchange(base_sent)
    step = ring_w.step(*modul_sent)
    base_grad, modul_a_grad = after((base_grad, modul_a_grad), *base_sent)
    joined_grad = dot_nt(base_grad, skip_full)
    time_back = dot_nt(modul_a_grad, time_a_full) + time_back_b
    time_grad = (time_back * silu_slope(time_value)).reshape(rows, frames, width)
    modul_parts = after(tuple(modul_parts), joined_grad, *step)
    ring_w.step()
    grad_time_a = sum(dot_tn(v[:, 2 * width :], g) for v, g in zip(row_inputs, modul_parts))
    grad_skip = sum(dot_tn(v[:, : 2 * width], g) for v, g in zip(row_inputs, base_parts))
    rows_skip = n_skip // 2
    grad_skip = grad_skip.reshape(groups, 4, 2, rows_skip, local)
    grad_skip = jnp.concatenate([grad_skip[:, :, 0], grad_skip[:, :, 1]], axis=3)
    ring_l = RingSum(
        [
            grad_skip.reshape(groups, 4 * rows_skip, 2 * local).astype(bf16),
            by_dp(grad_time_a.astype(bf16), groups),
        ],
        index,
        ringed,
    )
    ring_l.step(*ring_w.front)
    ring_w.step()
    ring_l.step()
    wide_sum = ring_w.total()
    ring_l.step(wide_sum)
    parts = finish(jnp.concatenate([ffn_sum[:, :local_hidden], wide_sum], axis=1), me)
    ring_l.step(*parts)
    up_sum = jnp.concatenate(
        [
            p[:, g * hidden_block : (g + 1) * hidden_block]
            for g in range(groups)
            for p in parts
        ],
        axis=1,
    )
    split = local_hidden + 3 * local, local_hidden + 3 * local + width // 2
    by_blocks = lambda parts, start, i: jnp.concatenate(
        [p[:, start + i * local : start + (i + 1) * local] for p in parts], axis=1
    ).astype(f32)
    out_sum = halves_sum([p[:, split[0] : split[1]] for p in parts])
    triples = [
        jnp.concatenate(
            [
                p[:, split[1] + i * 128 + q * 384 : split[1] + (i + 1) * 128 + q * 384]
                for p in parts
                for q in range(2)
            ],
            axis=1,
        ).astype(f32)
        for i in range(3)
    ]
    last = finish(ring_l.total(), me)
    columns = [by_blocks(last, 0, i) for i in range(4)]
    time_b_sum = jnp.concatenate([by_blocks(parts, local_hidden, i) for i in range(3)], axis=1)
    skip_sum = jnp.concatenate(columns[:2], axis=0)
    time_a_sum = jnp.concatenate(columns[2:4], axis=1)
    return (
        output,
        joined_grad[:, :width].reshape(rows, frames, width),
        joined_grad[:, width:].reshape(rows, frames, width),
        time_grad,
        skip_sum,
        jnp.concatenate([time_a_sum, time_b_sum], axis=1),
        *triples,
        out_sum,
        up_sum.astype(f32),
        ffn_sum[:, local_hidden:],
    )


def solution(mesh):
    frames = P("dp", "seq", None)
    marks = P("dp", "seq")
    weight = P(("dp", "seq"), None)
    return jax.shard_map(
        on_device,
        mesh=mesh,
        in_specs=(frames,) * 3 + (marks,) * 3 + (weight,) * 8 + (frames,),
        out_specs=(frames,) * 4 + (weight,) * 8,
        check_vma=False,
    )
```

```python
import functools

import jax
import jax.numpy as jnp
from jax import lax
from jax.experimental import pallas as pl
from jax.experimental.pallas import tpu as pltpu
from jax.sharding import PartitionSpec as P

HD = 64
NEG = 1e30
norm_eps = 1e-06
gelu_coef = 0.7978845608028654
f32, bf16 = jnp.float32, jnp.bfloat16

RING = (0, 2, 4, 6, 7, 5, 3, 1)
PLACE = tuple(RING.index(d) for d in range(8))


def dot_nt(a, b):
    return lax.dot_general(a, b, (((1,), (1,)), ((), ())), preferred_element_type=f32)


def dot_nn(a, b):
    return lax.dot_general(a, b, (((1,), (0,)), ((), ())), preferred_element_type=f32)


def dot_tn(a, b):
    return lax.dot_general(a, b, (((0,), (0,)), ((), ())), preferred_element_type=f32)


def silu_slope(v):
    sig = jax.nn.sigmoid(v)
    return sig * (1.0 + v * (1.0 - sig))


def gelu_value(u):
    return 0.5 * u * (1.0 + jnp.tanh(gelu_coef * (u + 0.044715 * u * u * u)))


def gelu_slope(u):
    inner = jnp.tanh(gelu_coef * (u + 0.044715 * u * u * u))
    return 0.5 * (1.0 + inner) + 0.5 * u * (1.0 - inner * inner) * gelu_coef * (
        1.0 + 3.0 * 0.044715 * u * u
    )


def norm_rows(v):
    mean = jnp.mean(v, axis=-1, keepdims=True)
    centred = v - mean
    inverse = lax.rsqrt(jnp.mean(centred * centred, axis=-1, keepdims=True) + norm_eps)
    return (centred * inverse, inverse)


def norm_back(grad, normed, inverse):
    return inverse * (
        grad
        - jnp.mean(grad, axis=-1, keepdims=True)
        - normed * jnp.mean(grad * normed, axis=-1, keepdims=True)
    )

def lanes_of(shape):
    return lax.broadcasted_iota(jnp.int32, shape, 1)


def swap_halves(v):
    lane = lanes_of(v.shape)
    return jnp.where(lane % HD < HD // 2, pltpu.roll(v, 128 - HD // 2, 1), pltpu.roll(v, HD // 2, 1))


def three_parts(v):
    hi = v.astype(bf16)
    rest = v - hi.astype(f32)
    mid = rest.astype(bf16)
    low = (rest - mid.astype(f32)).astype(bf16)
    return hi, mid, low


def attend_kernel(pieces, block, scale, *refs):
    qkv = refs[:pieces]
    cos_ref, sin_ref, qext_ref, kext_ref = refs[pieces : pieces + 4]
    att_ref, lse_ref, qrot_ref, krot_ref = refs[pieces + 4 : pieces + 8]
    kx, vx = refs[pieces + 8 :]
    step = pl.program_id(1)
    frames = qkv[0].shape[0]
    per_piece = frames // block

    @pl.when(step == 0)
    def _():
        for j in range(pieces):
            rows = pl.ds(j * frames, frames)
            k = qkv[j][:, 128:256].astype(f32)
            k = (k * cos_ref[rows, :] + swap_halves(k) * sin_ref[rows, :]).astype(bf16)
            krot_ref[rows, :] = k
            v = qkv[j][:, 256:384]
            ext = kext_ref[rows, :]
            lane = lanes_of(k.shape)
            one = jnp.where(lane % HD == 0, 1.0, 0.0).astype(bf16)
            low_lane = lane < HD
            kx[0, rows, :] = jnp.where(low_lane, k, ext)
            kx[1, rows, :] = jnp.where(low_lane, ext, k)
            vx[0, rows, :] = jnp.where(low_lane, v, one)
            vx[1, rows, :] = jnp.where(low_lane, one, v)

    rows = pl.ds(pl.multiple_of(step * block, block), block)
    for j in range(pieces):

        @pl.when(step // per_piece == j)
        def _(j=j):
            sub = pl.ds(pl.multiple_of((step - j * per_piece) * block, block), block)
            q = qkv[j][sub, 0:128].astype(f32)
            q = (q * cos_ref[rows, :] + swap_halves(q) * sin_ref[rows, :]).astype(bf16)
            qrot_ref[...] = (q.astype(f32) * scale).astype(bf16)

    q = qrot_ref[...]
    ext = qext_ref[rows, :]
    low_lane = lanes_of(q.shape) < HD
    outs = []
    for h in range(2):
        qx = jnp.where(low_lane, q, ext) if h == 0 else jnp.where(low_lane, ext, q)
        scores = dot_nt(qx, kx[h])
        top = jnp.max(scores, axis=1, keepdims=True)
        expo = jnp.exp(scores - top)
        mixed = dot_nn(expo.astype(bf16), vx[h])
        total = mixed[:, HD : HD + 1] if h == 0 else mixed[:, 0:1]
        outs.append((mixed / total, top + jnp.log(total)))
    low_out = lanes_of((block, 128)) < HD
    att_ref[...] = jnp.where(low_out, outs[0][0], outs[1][0]).astype(bf16)
    lse_ref[...] = jnp.where(low_out, outs[0][1], outs[1][1])


def attend(qkv, cosine, sine, qext, kext, block=384, scale=HD**-0.5):
    pieces = len(qkv)
    frames = qkv[0].shape[0]
    total = pieces * frames
    full = lambda a: pl.BlockSpec(a.shape, lambda p, i: (0, 0))
    tile = pl.BlockSpec((block, 128), lambda p, i: (i, p))
    return pl.pallas_call(
        functools.partial(attend_kernel, pieces, block, scale),
        grid=(2, total // block),
        in_specs=[pl.BlockSpec((frames, 384), lambda p, i: (0, p))] * pieces
        + [full(a) for a in (cosine, sine, qext, kext)],
        out_specs=[tile, tile, tile, pl.BlockSpec((total, 128), lambda p, i: (0, p))],
        out_shape=[jax.ShapeDtypeStruct((total, 256), t) for t in (bf16, f32, bf16, bf16)],
        scratch_shapes=[pltpu.VMEM((2, total, 128), bf16), pltpu.VMEM((2, total, 128), bf16)],
        compiler_params=pltpu.CompilerParams(vmem_limit_bytes=24 * 2**20),
        cost_estimate=pl.CostEstimate(
            flops=21 * 10**9, bytes_accessed=total * 4096, transcendentals=0
        ),
        name="attend",
    )(*qkv, cosine, sine, qext, kext)


def attend_back_kernel(pieces, block, scale, *refs):
    grads = refs[:pieces]
    values = refs[pieces : 2 * pieces]
    qrot_ref, krot_ref, att_ref, lse_ref, cos_ref, sin_ref, qext_ref, kext_ref = refs[2 * pieces : 2 * pieces + 8]
    out_ref = refs[2 * pieces + 8]
    qx, gx, qm, gm, dq = refs[2 * pieces + 9 :]
    step = pl.program_id(1)
    last = pl.num_programs(1) - 1
    frames = grads[0].shape[0]
    per_piece = frames // block

    @pl.when(step == 0)
    def _():
        for j in range(pieces):
            rows = pl.ds(j * frames, frames)
            q = qrot_ref[rows, :]
            g = grads[j][...]
            lane = lanes_of(q.shape)
            low_lane = lane < HD
            spot = lane % HD
            prod = g.astype(f32) * att_ref[rows, :].astype(f32)
            zero = jnp.zeros_like(q)
            lse = lse_ref[rows, :]
            for h in range(2):
                own = low_lane if h == 0 else jnp.logical_not(low_lane)
                lse_h = lse[:, 0:1] if h == 0 else lse[:, HD : HD + 1]
                delta = jnp.sum(jnp.where(own, prod, 0.0), axis=1, keepdims=True)
                a, b, c = (t.astype(f32) for t in three_parts(-lse_h))
                part = jnp.where(spot == 4, a, jnp.where(spot == 5, b, jnp.where(spot == 6, c, qext_ref[rows, :].astype(f32))))
                qx[h, rows, :] = jnp.where(own, q, part.astype(bf16))
                a, b, c = (t.astype(f32) for t in three_parts(-delta))
                part = jnp.where(spot == 0, a, jnp.where(spot == 1, b, jnp.where(spot == 2, c, 0.0)))
                gx[h, rows, :] = jnp.where(own, g, part.astype(bf16))
                qm[h, rows, :] = jnp.where(own, q, zero)
                gm[h, rows, :] = jnp.where(own, g, zero)
        dq[...] = jnp.zeros_like(dq)

    rows = pl.ds(pl.multiple_of(step * block, block), block)
    for j in range(pieces):

        @pl.when(step // per_piece == j)
        def _(j=j):
            sub = pl.ds(pl.multiple_of((step - j * per_piece) * block, block), block)
            k = krot_ref[rows, :]
            v = values[j][sub, 256:384]
            ext = kext_ref[rows, :]
            lane = lanes_of(k.shape)
            low_lane = lane < HD
            three = jnp.where(lane % HD < 3, 1.0, 0.0).astype(bf16)
            zero = jnp.zeros_like(k)
            small = k.astype(f32) * scale
            dk = jnp.zeros((block, 128), f32)
            dv = jnp.zeros((block, 128), f32)
            for h in range(2):
                own = low_lane if h == 0 else jnp.logical_not(low_lane)
                kx = jnp.where(own, k, ext)
                vx = jnp.where(own, v, three)
                probs = jnp.exp(dot_nt(kx, qx[h]))
                grad = (probs * dot_nt(vx, gx[h])).astype(bf16)
                dv = dv + dot_nn(probs.astype(bf16), gm[h])
                dk = dk + dot_nn(grad, qm[h])
                turned = jnp.transpose(jnp.where(own, small, 0.0)).astype(bf16)
                dq[...] += dot_nn(turned, grad)
            dk = dk * cos_ref[rows, :] - swap_halves(dk) * sin_ref[rows, :]
            out_ref[rows, 128:256] = dk.astype(bf16)
            out_ref[rows, 256:384] = dv.astype(bf16)

    @pl.when(step == last)
    def _():
        g = jnp.transpose(dq[...])
        g = g * cos_ref[...] - swap_halves(g) * sin_ref[...]
        out_ref[:, 0:128] = g.astype(bf16)


def attend_back(grads, qkv, qrot, krot, att, lse, cosine, sine, qext, kext, block=384, scale=HD**-0.5):
    pieces = len(grads)
    frames = grads[0].shape[0]
    total = pieces * frames
    full = lambda a: pl.BlockSpec(a.shape, lambda p, i: (0, 0))
    return pl.pallas_call(
        functools.partial(attend_back_kernel, pieces, block, scale),
        grid=(2, total // block),
        in_specs=[pl.BlockSpec((frames, 128), lambda p, i: (0, p))] * pieces
        + [pl.BlockSpec((frames, 384), lambda p, i: (0, p))] * pieces
        + [pl.BlockSpec((total, 128), lambda p, i: (0, p))] * 4
        + [full(a) for a in (cosine, sine, qext, kext)],
        out_specs=pl.BlockSpec((total, 384), lambda p, i: (0, p)),
        out_shape=jax.ShapeDtypeStruct((total, 768), bf16),
        scratch_shapes=[pltpu.VMEM((2, total, 128), bf16)] * 4 + [pltpu.VMEM((128, total), f32)],
        compiler_params=pltpu.CompilerParams(vmem_limit_bytes=34 * 2**20),
        cost_estimate=pl.CostEstimate(
            flops=31 * 10**9, bytes_accessed=total * 8192, transcendentals=0
        ),
        name="attend_back",
    )(*grads, *qkv, qrot, krot, att, lse, cosine, sine, qext, kext)


def frame_tables(seg, pos, valid):
    half = HD // 2
    freq = 10000.0 ** (-jnp.arange(half, dtype=f32) / half)
    angle = pos.astype(f32)[:, None] * freq
    cosine, sine = jnp.cos(angle), jnp.sin(angle)
    cosine = jnp.concatenate([cosine] * 4, axis=1)
    sine = jnp.concatenate([-sine, sine, -sine, sine], axis=1)
    spot = jnp.arange(128)[None, :] % HD
    seg, valid = seg[:, None], valid[:, None] > 0
    qext = jnp.where((spot < 3) & (spot != seg) | (spot == 3), -NEG, 0.0).astype(bf16)
    kext = ((spot == seg) & (spot < 3) | (spot == 3) & ~valid | (spot >= 4) & (spot < 7)).astype(bf16)
    return cosine, sine, qext, kext


def swap(v, mask):
    return lax.ppermute(v, "seq", [(i, i ^ mask) for i in range(4)])


def spread(v, before=(), first=None):
    near = swap(v, 1)
    far = swap(v if first is None else after(v, first), 2)
    return [v, near, far, swap(after(far, *before) if before else far, 1)]


def collect(parts, wait=()):
    low = [part.astype(bf16) for part in parts]
    if wait:
        low = list(after(tuple(low), *wait))
    far_near = swap(low[3], 1)
    near = swap(low[1], 1)
    sent = (low[2].astype(f32) + far_near.astype(f32)).astype(bf16)
    far = swap(sent, 2)
    return parts[0] + near.astype(f32) + far.astype(f32), sent


def exchange(parts):
    return [parts[0], swap(parts[1], 1), swap(parts[2], 2), swap(parts[3], 3)]


def by_place(parts, me):
    odd, high = (me & 1) == 1, (me & 2) == 2
    parts = [jnp.where(odd, parts[t ^ 1], parts[t]) for t in range(4)]
    return [jnp.where(high, parts[t ^ 2], parts[t]) for t in range(4)]


def ring_step(v, step):
    return lax.ppermute(v, "dp", [(RING[i], RING[(i + step) % 8]) for i in range(8)])


class RingGather:
    def __init__(self, v):
        self.found, self.front, self.count = [(0, 0, v)], (v, v), 0

    def step(self, *before):
        one, other = after(self.front, *before) if before else self.front
        self.count += 1
        k = self.count
        if k < 4:
            self.front = ring_step(one, 1), ring_step(other, -1)
            self.found += [(k, 0, self.front[0]), (8 - k, 0, self.front[1])]
        else:
            middle = one.shape[0] // 2
            self.front = ring_step(one[:middle], 1), ring_step(other[middle:], -1)
            self.found += [(4, 0, self.front[0]), (4, middle, self.front[1])]
        return self.front


def ring_add_kernel(k, count, index_ref, *refs):
    plus, minus = refs[:count], refs[count : 2 * count]
    moving = refs[2 * count : -1 if k == 0 else -2]
    outs = refs[-1:] if k == 0 else refs[-2:]
    rows = plus[0].shape[1]
    middle = rows // 2
    upper, lower = slice(0, middle), slice(middle, rows)
    start = 0
    for i in range(count):
        columns = slice(start, start + plus[i].shape[2])
        start += plus[i].shape[2]
        if k == 4:
            outs[0][:, columns] = plus[i][0, upper, :].astype(bf16)
            outs[1][:, columns] = plus[i][0, lower, :].astype(bf16)
            continue
        ahead = plus[i][0].astype(f32)
        if k == 0:
            outs[0][:, columns] = (
                ahead + moving[0][:, columns].astype(f32) + moving[1][:, columns].astype(f32)
            )
            continue
        behind = minus[i][0].astype(f32)
        one, other = moving[0][:, columns].astype(f32), moving[1][:, columns].astype(f32)
        if k == 3:
            outs[0][upper, columns] = (ahead[upper] + one).astype(bf16)
            outs[0][lower, columns] = ahead[lower].astype(bf16)
            outs[1][upper, columns] = behind[upper].astype(bf16)
            outs[1][lower, columns] = (behind[lower] + other).astype(bf16)
        else:
            outs[0][:, columns] = (ahead + one).astype(bf16)
            outs[1][:, columns] = (behind + other).astype(bf16)


def ring_add(index, arrays, moving, k):
    rows, columns = arrays[0].shape[1], sum(a.shape[2] for a in arrays)
    ahead = [pl.BlockSpec((1, rows, a.shape[2]), lambda i, index: (index[(8 - k) % 8], 0, 0)) for a in arrays]
    behind = [pl.BlockSpec((1, rows, a.shape[2]), lambda i, index: (index[k], 0, 0)) for a in arrays]
    whole = lambda shape: pl.BlockSpec(shape, lambda i, index: (0, 0))
    height = rows // 2 if k == 4 else rows
    n_out = 1 if k == 0 else 2
    return pl.pallas_call(
        functools.partial(ring_add_kernel, k, len(arrays)),
        grid_spec=pltpu.PrefetchScalarGridSpec(
            num_scalar_prefetch=1,
            grid=(1,),
            in_specs=ahead + behind + [whole(m.shape) for m in moving],
            out_specs=[whole((height, columns))] * n_out,
        ),
        out_shape=[jax.ShapeDtypeStruct((height, columns), f32 if k == 0 else bf16)] * n_out,
        compiler_params=pltpu.CompilerParams(vmem_limit_bytes=16 * 2**20),
        cost_estimate=pl.CostEstimate(flops=10**9, bytes_accessed=10**6, transcendentals=0),
        name="ring_add",
    )(index, *arrays, *arrays, *moving)


class RingSum:
    def __init__(self, arrays, index, ringed):
        self.arrays, self.index, self.ringed = arrays, index, ringed
        self.front, self.count = (), 4

    def step(self, *before):
        if self.ringed:
            arrays, front = self.arrays, self.front
            if before:
                arrays, front = after((arrays, front), *before)
            moving = ring_add(self.index, arrays, front, self.count)
            self.front = ring_step(moving[0], 1), ring_step(moving[1], -1)
            self.count -= 1
        return self.front

    def total(self):
        if self.ringed:
            return ring_add(self.index, self.arrays, self.front, 0)[0]
        low = jnp.concatenate([a.astype(bf16) for a in self.arrays], axis=2)
        return lax.psum_scatter(low, "dp", scatter_dimension=0).astype(f32)


def after(v, *others):
    return lax.optimization_barrier((v, *others))[0]


def assemble_kernel(copies, n_in, n_out, index_ref, *refs):
    arrays, outs, sems = refs[:n_in], refs[n_in : n_in + n_out], refs[-1]
    moves = []
    me = index_ref[8]
    for number, (a, row, count, out, k, j, per_dp, per_seq, column, more) in enumerate(copies):
        start = index_ref[k] * per_dp + jnp.bitwise_xor(me, j) * per_seq + more
        target = outs[out].at[
            pl.ds(pl.multiple_of(start, count), count), pl.ds(column, arrays[a].shape[1])
        ]
        moves.append(
            pltpu.make_async_copy(arrays[a].at[pl.ds(row, count), :], target, sems.at[number])
        )
    for move in moves:
        move.start()
    for move in moves:
        move.wait()


def assemble(index, arrays, copies, shapes):
    anywhere = pl.BlockSpec(memory_space=pl.ANY)
    return pl.pallas_call(
        functools.partial(assemble_kernel, tuple(copies), len(arrays), len(shapes)),
        grid_spec=pltpu.PrefetchScalarGridSpec(
            num_scalar_prefetch=1,
            grid=(1,),
            in_specs=[anywhere] * len(arrays),
            out_specs=[pl.BlockSpec(shape, lambda i, index: (0, 0)) for shape in shapes],
            scratch_shapes=[pltpu.SemaphoreType.DMA((len(copies),))],
        ),
        out_shape=[jax.ShapeDtypeStruct(shape, bf16) for shape in shapes],
        compiler_params=pltpu.CompilerParams(vmem_limit_bytes=8 * 2**20 + 5 * sum(r * c for r, c in shapes)),
        cost_estimate=pl.CostEstimate(flops=9 * 10**9, bytes_accessed=1024, transcendentals=0),
        name="assemble",
    )(index, *arrays)


class Gather:
    def __init__(self, index):
        self.index, self.arrays, self.copies, self.shapes = index, [], [], []

    def out(self, rows, columns):
        self.shapes.append((rows, columns))
        return len(self.shapes) - 1

    def add(self, piece, k, blocks):
        self.arrays.append(piece)
        for row, count, out, j, per_dp, per_seq, column, more in blocks:
            self.copies.append(
                (len(self.arrays) - 1, row, count, out, k, j, per_dp, per_seq, column, more)
            )

    def run(self):
        return assemble(self.index, self.arrays, self.copies, self.shapes)


def half(v, which):
    middle = v.shape[1] // 2
    return jnp.where(which == 1, v[:, middle:], v[:, :middle])


def merge(mine, other, core):
    return jnp.concatenate(
        [jnp.where(core == 1, other, mine), jnp.where(core == 1, mine, other)], axis=1
    )


def by_dp(grad, groups):
    return grad.reshape(groups, grad.shape[0] // groups, grad.shape[1])


def finish(block, me):
    rows = block.shape[0] // 4
    low = block.astype(bf16)
    parts = by_place([low[t * rows : (t + 1) * rows] for t in range(4)], me)
    return by_place(exchange(parts), me)


def halves_sum(parts):
    total = [parts[c].astype(f32) + parts[2 + c].astype(f32) for c in range(2)]
    return jnp.concatenate(total, axis=1)


def on_device(
    layer_input,
    skip_input,
    time_embed,
    segment_ids,
    positions,
    valid_mask,
    skip_weight,
    time_weight,
    query_weight,
    key_weight,
    value_weight,
    out_weight,
    up_weight,
    down_weight,
    cotangent,
):
    rows, frames, width = layer_input.shape
    hidden = up_weight.shape[1]
    groups = lax.axis_size("dp")
    me, dp = lax.axis_index("seq"), lax.axis_index("dp")
    local = width // 4
    local_hidden = hidden // 4

    core = me & 1
    hidden_block = hidden // (groups * 4)
    ringed = groups == 8
    first_in, second_in = layer_input.reshape(frames, width), skip_input.reshape(frames, width)
    time_a, time_b = time_weight[:, : 2 * width], time_weight[:, 2 * width :]
    n_skip, n_time = skip_weight.shape[0], time_weight.shape[0]

    def needed():
        triple = [
            jnp.concatenate(
                [
                    w[:, t * local + p * 128 : t * local + (p + 1) * 128]
                    for p in range(2)
                    for w in (query_weight, key_weight, value_weight)
                ],
                axis=1,
            )
            for t in range(4)
        ]
        upper_w = [
            jnp.concatenate(
                [
                    up_weight[:, (g * 4 + t) * hidden_block : (g * 4 + t + 1) * hidden_block]
                    for g in range(groups)
                ],
                axis=1,
            )
            for t in range(4)
        ]
        return triple, upper_w

    triple, upper_w = needed()
    index = None
    marks = jnp.concatenate(spread(jnp.concatenate([segment_ids, positions, valid_mask])), axis=1)
    tables = frame_tables(marks[0], marks[1], marks[2])
    time_value = time_embed.reshape(frames, width).astype(f32)
    time_act = (time_value * jax.nn.sigmoid(time_value)).astype(bf16)
    joined = jnp.concatenate([first_in, second_in], axis=1)
    row_own = jnp.concatenate([first_in, second_in, time_act], axis=1)

    if ringed:
        place = jnp.asarray(PLACE, jnp.int32)[dp]
        order = jnp.asarray(RING, jnp.int32)[(place - jnp.arange(8)) % 8]
        index = jnp.concatenate([order, me[None].astype(jnp.int32)])

        first = Gather(index)
        o_skip, o_time_a = first.out(32 * n_skip, width), first.out(32 * n_time, 2 * width)
        own = jnp.concatenate([skip_weight, time_a[:, :width], time_a[:, width:]], axis=0)
        layout = [
            (0, n_skip, o_skip, 0),
            (n_skip, n_time, o_time_a, 0),
            (n_skip + n_time, n_time, o_time_a, width),
        ]
        n_own = own.shape[0]
        ring_a = RingGather(jnp.concatenate([own, swap(own, 2)], axis=0))
        ring_a.step()
        triple, upper_w, time_b, out_weight = after(
            (triple, upper_w, time_b, out_weight), ring_a.found[0][2]
        )

        def to_core(gather, entries, layout, n_own):
            near = [swap(piece, 1) for _, _, piece in entries]
            for (k, row, piece), other in zip(entries, near):
                for array, flip in ((piece, 0), (other, 1)):
                    for part in range(row // n_own, (row + piece.shape[0]) // n_own):
                        at_row = part * n_own - row
                        gather.add(
                            array,
                            k,
                            [
                                (at_row + at, count, out, (2 * part) ^ flip, 4 * count, count, column, 0)
                                for at, count, out, column in layout
                            ],
                        )
            return near

        rest = []
        for t in range(4):
            sides = [
                w[:, (t & 1) * (w.shape[1] // 2) : ((t & 1) + 1) * (w.shape[1] // 2)]
                for w in (out_weight, time_b)
            ]
            rest.append(jnp.concatenate([triple[t], *sides, upper_w[t]], axis=1))
        rest = by_place(rest, me)
        near = to_core(first, ring_a.found[:1], layout, n_own)
        ring_a.step(*near, *rest)
        near = to_core(first, ring_a.found[1:3], layout, n_own)
        rest = exchange(after(tuple(rest), ring_a.found[1][2]))
        time_far = swap(after(time_act, rest[2]), 2)
        second_far = swap(after(second_in, time_far), 2)
        ring_a.step(*near, *rest)
        near = to_core(first, ring_a.found[3:5], layout, n_own)
        ring_a.step(*near, *tables, time_far)
        rest = jnp.concatenate(by_place(rest, me), axis=0)
        cut = 3 * local + width // 2, 3 * local + 2 * width
        ring_b_own, ring_c_own, ring_d_own = after(
            (
                rest[:, : cut[0]],
                rest[:, cut[0] : cut[1]],
                jnp.concatenate([rest[:, cut[1] :], down_weight], axis=1),
            ),
            *ring_a.found[5][2:],
            *ring_a.found[6][2:],
        )
        ring_b, ring_c, ring_d = (RingGather(v) for v in (ring_b_own, ring_c_own, ring_d_own))
        near = to_core(first, ring_a.found[5:9], layout, n_own)
        ring_b.step()
        skip_full, time_a_full = first.run()
        ring_b.step(skip_full)

        def block_rows(ring, shape):
            gather = Gather(index)
            out = gather.out(*shape)
            for k, row, piece in ring.found:
                gather.add(piece, k, [(0, piece.shape[0], out, 0, width // 8, 0, 0, row)])
            return gather.run()[0]

    else:
        first_far, second_far, time_far = swap(first_in, 2), swap(second_in, 2), swap(time_act, 2)
        skip_full, time_a_full, time_b_full, out_full = (
            lax.all_gather(w, ("dp", "seq"), axis=0, tiled=True)
            for w in (skip_weight, time_a, time_b, out_weight)
        )
        triple_full, up_full = (
            lax.all_gather(
                jnp.concatenate(by_place(exchange(by_place(parts, me)), me), axis=0),
                "dp",
                axis=0,
                tiled=True,
            )
            for parts in (triple, upper_w)
        )
        down_full = lax.all_gather(down_weight, "dp", axis=0, tiled=True)
        out_sides = [half(out_full, core), half(out_full, 1 - core)]
        time_b_sides = [half(time_b_full, core), half(time_b_full, 1 - core)]

    base = dot_nn(joined, skip_full)
    shift_a, scale_a = jnp.split(dot_nn(time_act, time_a_full), 2, axis=1)
    normed_a, inverse_a = norm_rows(base)
    hidden_own = (normed_a * (1.0 + scale_a) + shift_a).astype(bf16)
    if ringed:
        hidden_own = after(hidden_own, second_far)
        ring_c.step(skip_full)
        ring_b.step(hidden_own)
        ring_b.step()
        ring_c.step(*ring_b.found[5][2:])
        ring_c.step(*ring_b.front)
        hidden_a = spread(hidden_own, ring_b.front)
        first_far = swap(after(first_in, hidden_a[2]), 2)
        wide = block_rows(ring_b, (width, cut[0]))
        triple_full = wide[:, : 3 * local]
        out_mine = wide[:, 3 * local :]
        out_sides = [out_mine, swap(after(out_mine, hidden_a[3]), 1)]
        ring_d.step(hidden_a[2])
    else:
        hidden_a = spread(hidden_own)
    qkv = [dot_nn(h, triple_full).astype(bf16) for h in hidden_a]
    att, logsum, query_rot, key_rot = attend(qkv, *tables)
    time_act_b = after(time_act, att)
    if ringed:
        att = after(att, *ring_c.front, *ring_d.front)
    att = after(att, first_far)
    att_parts = [att[j * frames : (j + 1) * frames] for j in range(4)]
    attended = exchange(att_parts)
    if ringed:
        ring_c.step(att)
        mine = block_rows(ring_c, (width, 3 * width // 2))
        time_b_sides = [mine, swap(mine, 1)]
        ring_d.step(*attended)
    shift_b, scale_b, gate_b = jnp.split(
        merge(dot_nn(time_act_b, time_b_sides[0]), dot_nn(time_act_b, time_b_sides[1]), core),
        3,
        axis=1,
    )
    upstream = cotangent.reshape(frames, width).astype(f32)
    ffn_grad = (upstream * gate_b).astype(bf16)
    attended = list(after(tuple(attended), ffn_grad))
    ffn_grad = spread(ffn_grad)
    attended = jnp.concatenate(by_place(attended, me), axis=1)
    middle = base + merge(dot_nn(attended, out_sides[0]), dot_nn(attended, out_sides[1]), core)
    normed_b, inverse_b = norm_rows(middle)

    hidden_own = (normed_b * (1.0 + scale_b) + shift_b).astype(bf16)
    if ringed:
        ring_d.step(hidden_own)
        ring_d.step()
    hidden_b = spread(hidden_own, (), ffn_grad[2])
    if ringed:
        ffn_full = block_rows(ring_d, (width, 2 * local_hidden))
        up_full, down_full = ffn_full[:, :local_hidden], ffn_full[:, local_hidden:]
    row_near = swap(after(row_own, hidden_b[3]), 1)
    row_far = jnp.concatenate([first_far, second_far, time_far], axis=1)
    row_inputs = [row_own, row_near, row_far, swap(after(row_far, hidden_b[3]), 1)]
    hb = [jnp.concatenate(hidden_b[:2]), jnp.concatenate(hidden_b[2:])]
    fg = [jnp.concatenate(ffn_grad[:2]), jnp.concatenate(ffn_grad[2:])]
    upper = dot_nn(hb[1], up_full)
    acted_far = gelu_value(upper).astype(bf16)
    part_far = dot_nn(acted_far, down_full)
    part_low = part_far.astype(bf16)
    fg[1] = after(fg[1], part_low)
    ug_far = (dot_nt(fg[1], down_full) * gelu_slope(upper)).astype(bf16)
    part_sent = (part_far[:frames] + swap(part_low[frames:], 1).astype(f32)).astype(bf16)
    far = dot_nt(after(ug_far, part_sent), up_full)
    far_low = far.astype(bf16)
    hb[0] = after(hb[0], far_low)
    upper = dot_nn(hb[0], up_full)
    sent = (far[:frames] + swap(far_low[frames:], 1).astype(f32)).astype(bf16)
    fg[0] = after(fg[0], sent)
    acted = [gelu_value(upper).astype(bf16), acted_far]
    ug = [(dot_nt(fg[0], down_full) * gelu_slope(upper)).astype(bf16), ug_far]
    own = dot_nt(ug[0], up_full)
    hidden_b_grad = (
        own[:frames] + swap(own[frames:].astype(bf16), 1).astype(f32) + swap(sent, 2).astype(f32)
    )
    acted, fg, ug, hb = after((acted, fg, ug, hb), own, row_near, row_inputs[3])
    part = dot_nn(acted[0], down_full)
    ffn = (
        part[:frames]
        + swap(part[frames:].astype(bf16), 1).astype(f32)
        + swap(part_sent, 2).astype(f32)
    )
    grad_down = dot_tn(acted[0], fg[0]) + dot_tn(acted[1], fg[1])
    grad_up = dot_tn(hb[0], ug[0]) + dot_tn(hb[1], ug[1])
    grad_ffn = jnp.concatenate([grad_up.astype(bf16), grad_down.astype(bf16)], axis=1)
    hidden_b_grad = after(hidden_b_grad, grad_ffn, part)
    ffn_sum = lax.psum_scatter(grad_ffn, "dp", scatter_dimension=0, tiled=True).astype(f32)

    scale_b_grad = hidden_b_grad * normed_b
    middle_grad = upstream + norm_back(hidden_b_grad * (1.0 + scale_b), normed_b, inverse_b)
    branch_grad = middle_grad.astype(bf16)
    branch_sides = [half(branch_grad, core), half(branch_grad, 1 - core)]
    attended_grad = (
        dot_nt(branch_sides[0], out_sides[0]) + dot_nt(branch_sides[1], out_sides[1])
    ).astype(bf16)
    att_grad_parts = by_place([attended_grad[:, t * local : (t + 1) * local] for t in range(4)], me)
    att_grad = exchange(att_grad_parts)
    def to_columns(grads):
        return [
            jnp.concatenate([g[:, t * local : (t + 1) * local] for g in grads], axis=1) for t in range(4)
        ]

    ffn = after(ffn, *att_grad_parts)
    output = (middle + gate_b * ffn).astype(bf16).reshape(rows, frames, width)
    modul_b_grad = [v.astype(bf16) for v in (hidden_b_grad, scale_b_grad, upstream * ffn)]
    modul_sent = by_place(to_columns(modul_b_grad), me)
    modul_b_parts = exchange(modul_sent)
    grad_out = [dot_tn(attended, side).astype(bf16) for side in branch_sides]
    near_out = swap(grad_out[1], 1)
    att_grad = after(tuple(att_grad), *modul_sent, *grad_out, row_inputs[3])
    triple_grad = attend_back(att_grad, qkv, query_rot, key_rot, att, logsum, *tables)
    triple_grad = after(triple_grad, *modul_b_parts, near_out)
    back = dot_nt(triple_grad, triple_full)
    far_low = back[3 * frames :].astype(bf16)
    triple_grad, modul_b_grad, hidden_a_all = after(
        (triple_grad, tuple(modul_b_grad), jnp.concatenate(hidden_a)), far_low
    )
    grad_triple = dot_tn(hidden_a_all, triple_grad).astype(bf16)
    sent = (back[2 * frames : 3 * frames] + swap(far_low, 1).astype(f32)).astype(bf16)
    hidden_a_grad = (
        back[:frames]
        + swap(back[frames : 2 * frames].astype(bf16), 1).astype(f32)
        + swap(sent, 2).astype(f32)
    )
    modul_b_parts = after(tuple(modul_b_parts), sent, grad_triple)
    grad_time_b = sum(dot_tn(v[:, 2 * width :], g) for v, g in zip(row_inputs, modul_b_parts))
    grad_out = (grad_out[0].astype(f32) + near_out.astype(f32)).astype(bf16)
    ring_w = RingSum(
        [by_dp(g, groups) for g in (grad_time_b.astype(bf16), grad_out, grad_triple)], index, ringed
    )
    ring_w.step()
    modul_b_grad = jnp.concatenate(modul_b_grad, axis=1)
    time_back_b = dot_nt(half(modul_b_grad, core), time_b_sides[0]) + dot_nt(
        half(modul_b_grad, 1 - core), time_b_sides[1]
    )
    hidden_a_grad = after(hidden_a_grad, time_back_b)

    scale_a_grad = hidden_a_grad * normed_a
    modul_a_grad = jnp.concatenate([hidden_a_grad, scale_a_grad], axis=1).astype(bf16)
    modul_sent = by_place(to_columns([modul_a_grad[:, :width], modul_a_grad[:, width:]]), me)
    modul_parts = exchange(modul_sent)
    base_grad = (
        middle_grad + norm_back(hidden_a_grad * (1.0 + scale_a), normed_a, inverse_a)
    ).astype(bf16)
    base_sent = by_place([base_grad[:, t * local : (t + 1) * local] for t in range(4)], me)
    base_parts = exchange(base_sent)
    step = ring_w.step(*modul_sent)
    base_grad, modul_a_grad = after((base_grad, modul_a_grad), *base_sent)
    joined_grad = dot_nt(base_grad, skip_full)
    time_back = dot_nt(modul_a_grad, time_a_full) + time_back_b
    time_grad = (time_back * silu_slope(time_value)).reshape(rows, frames, width)
    modul_parts = after(tuple(modul_parts), joined_grad, *step)
    ring_w.step()
    grad_time_a = sum(dot_tn(v[:, 2 * width :], g) for v, g in zip(row_inputs, modul_parts))
    grad_skip = sum(dot_tn(v[:, : 2 * width], g) for v, g in zip(row_inputs, base_parts))
    rows_skip = n_skip // 2
    grad_skip = grad_skip.reshape(groups, 4, 2, rows_skip, local)
    grad_skip = jnp.concatenate([grad_skip[:, :, 0], grad_skip[:, :, 1]], axis=3)
    ring_l = RingSum(
        [
            grad_skip.reshape(groups, 4 * rows_skip, 2 * local).astype(bf16),
            by_dp(grad_time_a.astype(bf16), groups),
        ],
        index,
        ringed,
    )
    ring_l.step()
    ring_w.step(grad_skip)
    ring_l.step()
    wide_sum = ring_w.total()
    ring_l.step(wide_sum)
    parts = finish(jnp.concatenate([ffn_sum[:, :local_hidden], wide_sum], axis=1), me)
    ring_l.step(*parts)
    up_sum = jnp.concatenate(
        [
            p[:, g * hidden_block : (g + 1) * hidden_block]
            for g in range(groups)
            for p in parts
        ],
        axis=1,
    )
    split = local_hidden + 3 * local, local_hidden + 3 * local + width // 2
    by_blocks = lambda parts, start, i: jnp.concatenate(
        [p[:, start + i * local : start + (i + 1) * local] for p in parts], axis=1
    ).astype(f32)
    out_sum = halves_sum([p[:, split[0] : split[1]] for p in parts])
    triples = [
        jnp.concatenate(
            [
                p[:, split[1] + i * 128 + q * 384 : split[1] + (i + 1) * 128 + q * 384]
                for p in parts
                for q in range(2)
            ],
            axis=1,
        ).astype(f32)
        for i in range(3)
    ]
    last = finish(ring_l.total(), me)
    columns = [by_blocks(last, 0, i) for i in range(4)]
    time_b_sum = jnp.concatenate([by_blocks(parts, local_hidden, i) for i in range(3)], axis=1)
    skip_sum = jnp.concatenate(columns[:2], axis=0)
    time_a_sum = jnp.concatenate(columns[2:4], axis=1)
    return (
        output,
        joined_grad[:, :width].reshape(rows, frames, width),
        joined_grad[:, width:].reshape(rows, frames, width),
        time_grad,
        skip_sum,
        jnp.concatenate([time_a_sum, time_b_sum], axis=1),
        *triples,
        out_sum,
        up_sum.astype(f32),
        ffn_sum[:, local_hidden:],
    )


def solution(mesh):
    frames = P("dp", "seq", None)
    marks = P("dp", "seq")
    weight = P(("dp", "seq"), None)
    return jax.shard_map(
        on_device,
        mesh=mesh,
        in_specs=(frames,) * 3 + (marks,) * 3 + (weight,) * 8 + (frames,),
        out_specs=(frames,) * 4 + (weight,) * 8,
        check_vma=False,
    )
```

```python
import functools

import jax
import jax.numpy as jnp
from jax import lax
from jax.experimental import pallas as pl
from jax.experimental.pallas import tpu as pltpu
from jax.sharding import PartitionSpec as P

HD = 64
NEG = 1e30
norm_eps = 1e-06
gelu_coef = 0.7978845608028654
f32, bf16 = jnp.float32, jnp.bfloat16

RING = (0, 2, 4, 6, 7, 5, 3, 1)
PLACE = tuple(RING.index(d) for d in range(8))


def dot_nt(a, b):
    return lax.dot_general(a, b, (((1,), (1,)), ((), ())), preferred_element_type=f32)


def dot_nn(a, b):
    return lax.dot_general(a, b, (((1,), (0,)), ((), ())), preferred_element_type=f32)


def dot_tn(a, b):
    return lax.dot_general(a, b, (((0,), (0,)), ((), ())), preferred_element_type=f32)


def silu_slope(v):
    sig = jax.nn.sigmoid(v)
    return sig * (1.0 + v * (1.0 - sig))


def gelu_value(u):
    return 0.5 * u * (1.0 + jnp.tanh(gelu_coef * (u + 0.044715 * u * u * u)))


def gelu_slope(u):
    inner = jnp.tanh(gelu_coef * (u + 0.044715 * u * u * u))
    return 0.5 * (1.0 + inner) + 0.5 * u * (1.0 - inner * inner) * gelu_coef * (
        1.0 + 3.0 * 0.044715 * u * u
    )


def norm_rows(v):
    mean = jnp.mean(v, axis=-1, keepdims=True)
    centred = v - mean
    inverse = lax.rsqrt(jnp.mean(centred * centred, axis=-1, keepdims=True) + norm_eps)
    return (centred * inverse, inverse)


def norm_back(grad, normed, inverse):
    return inverse * (
        grad
        - jnp.mean(grad, axis=-1, keepdims=True)
        - normed * jnp.mean(grad * normed, axis=-1, keepdims=True)
    )

def lanes_of(shape):
    return lax.broadcasted_iota(jnp.int32, shape, 1)


def swap_halves(v):
    lane = lanes_of(v.shape)
    return jnp.where(lane % HD < HD // 2, pltpu.roll(v, 128 - HD // 2, 1), pltpu.roll(v, HD // 2, 1))


def three_parts(v):
    hi = v.astype(bf16)
    rest = v - hi.astype(f32)
    mid = rest.astype(bf16)
    low = (rest - mid.astype(f32)).astype(bf16)
    return hi, mid, low


def attend_kernel(pieces, block, scale, *refs):
    qkv = refs[:pieces]
    cos_ref, sin_ref, qext_ref, kext_ref = refs[pieces : pieces + 4]
    att_ref, lse_ref, qrot_ref, krot_ref = refs[pieces + 4 : pieces + 8]
    kx, vx = refs[pieces + 8 :]
    step = pl.program_id(1)
    frames = qkv[0].shape[0]
    per_piece = frames // block

    @pl.when(step == 0)
    def _():
        for j in range(pieces):
            rows = pl.ds(j * frames, frames)
            k = qkv[j][:, 128:256].astype(f32)
            k = (k * cos_ref[rows, :] + swap_halves(k) * sin_ref[rows, :]).astype(bf16)
            krot_ref[rows, :] = k
            v = qkv[j][:, 256:384]
            ext = kext_ref[rows, :]
            lane = lanes_of(k.shape)
            one = jnp.where(lane % HD == 0, 1.0, 0.0).astype(bf16)
            low_lane = lane < HD
            kx[0, rows, :] = jnp.where(low_lane, k, ext)
            kx[1, rows, :] = jnp.where(low_lane, ext, k)
            vx[0, rows, :] = jnp.where(low_lane, v, one)
            vx[1, rows, :] = jnp.where(low_lane, one, v)

    rows = pl.ds(pl.multiple_of(step * block, block), block)
    for j in range(pieces):

        @pl.when(step // per_piece == j)
        def _(j=j):
            sub = pl.ds(pl.multiple_of((step - j * per_piece) * block, block), block)
            q = qkv[j][sub, 0:128].astype(f32)
            q = (q * cos_ref[rows, :] + swap_halves(q) * sin_ref[rows, :]).astype(bf16)
            qrot_ref[...] = (q.astype(f32) * scale).astype(bf16)

    q = qrot_ref[...]
    ext = qext_ref[rows, :]
    low_lane = lanes_of(q.shape) < HD
    outs = []
    for h in range(2):
        qx = jnp.where(low_lane, q, ext) if h == 0 else jnp.where(low_lane, ext, q)
        scores = dot_nt(qx, kx[h])
        top = jnp.max(scores, axis=1, keepdims=True)
        expo = jnp.exp(scores - top)
        mixed = dot_nn(expo.astype(bf16), vx[h])
        total = mixed[:, HD : HD + 1] if h == 0 else mixed[:, 0:1]
        outs.append((mixed / total, top + jnp.log(total)))
    low_out = lanes_of((block, 128)) < HD
    att_ref[...] = jnp.where(low_out, outs[0][0], outs[1][0]).astype(bf16)
    lse_ref[...] = jnp.where(low_out, outs[0][1], outs[1][1])


def attend(qkv, cosine, sine, qext, kext, block=384, scale=HD**-0.5):
    pieces = len(qkv)
    frames = qkv[0].shape[0]
    total = pieces * frames
    full = lambda a: pl.BlockSpec(a.shape, lambda p, i: (0, 0))
    tile = pl.BlockSpec((block, 128), lambda p, i: (i, p))
    return pl.pallas_call(
        functools.partial(attend_kernel, pieces, block, scale),
        grid=(2, total // block),
        in_specs=[pl.BlockSpec((frames, 384), lambda p, i: (0, p))] * pieces
        + [full(a) for a in (cosine, sine, qext, kext)],
        out_specs=[tile, tile, tile, pl.BlockSpec((total, 128), lambda p, i: (0, p))],
        out_shape=[jax.ShapeDtypeStruct((total, 256), t) for t in (bf16, f32, bf16, bf16)],
        scratch_shapes=[pltpu.VMEM((2, total, 128), bf16), pltpu.VMEM((2, total, 128), bf16)],
        compiler_params=pltpu.CompilerParams(vmem_limit_bytes=24 * 2**20),
        cost_estimate=pl.CostEstimate(
            flops=21 * 10**9, bytes_accessed=total * 4096, transcendentals=0
        ),
        name="attend",
    )(*qkv, cosine, sine, qext, kext)


def attend_back_kernel(pieces, block, scale, *refs):
    grads = refs[:pieces]
    values = refs[pieces : 2 * pieces]
    qrot_ref, krot_ref, att_ref, lse_ref, cos_ref, sin_ref, qext_ref, kext_ref = refs[2 * pieces : 2 * pieces + 8]
    out_ref = refs[2 * pieces + 8]
    qx, gx, qm, gm, dq = refs[2 * pieces + 9 :]
    step = pl.program_id(1)
    last = pl.num_programs(1) - 1
    frames = grads[0].shape[0]
    per_piece = frames // block

    @pl.when(step == 0)
    def _():
        for j in range(pieces):
            rows = pl.ds(j * frames, frames)
            q = qrot_ref[rows, :]
            g = grads[j][...]
            lane = lanes_of(q.shape)
            low_lane = lane < HD
            spot = lane % HD
            prod = g.astype(f32) * att_ref[rows, :].astype(f32)
            zero = jnp.zeros_like(q)
            lse = lse_ref[rows, :]
            for h in range(2):
                own = low_lane if h == 0 else jnp.logical_not(low_lane)
                lse_h = lse[:, 0:1] if h == 0 else lse[:, HD : HD + 1]
                delta = jnp.sum(jnp.where(own, prod, 0.0), axis=1, keepdims=True)
                a, b, c = (t.astype(f32) for t in three_parts(-lse_h))
                part = jnp.where(spot == 4, a, jnp.where(spot == 5, b, jnp.where(spot == 6, c, qext_ref[rows, :].astype(f32))))
                qx[h, rows, :] = jnp.where(own, q, part.astype(bf16))
                a, b, c = (t.astype(f32) for t in three_parts(-delta))
                part = jnp.where(spot == 0, a, jnp.where(spot == 1, b, jnp.where(spot == 2, c, 0.0)))
                gx[h, rows, :] = jnp.where(own, g, part.astype(bf16))
                qm[h, rows, :] = jnp.where(own, q, zero)
                gm[h, rows, :] = jnp.where(own, g, zero)
        dq[...] = jnp.zeros_like(dq)

    rows = pl.ds(pl.multiple_of(step * block, block), block)
    for j in range(pieces):

        @pl.when(step // per_piece == j)
        def _(j=j):
            sub = pl.ds(pl.multiple_of((step - j * per_piece) * block, block), block)
            k = krot_ref[rows, :]
            v = values[j][sub, 256:384]
            ext = kext_ref[rows, :]
            lane = lanes_of(k.shape)
            low_lane = lane < HD
            three = jnp.where(lane % HD < 3, 1.0, 0.0).astype(bf16)
            zero = jnp.zeros_like(k)
            small = k.astype(f32) * scale
            dk = jnp.zeros((block, 128), f32)
            dv = jnp.zeros((block, 128), f32)
            for h in range(2):
                own = low_lane if h == 0 else jnp.logical_not(low_lane)
                kx = jnp.where(own, k, ext)
                vx = jnp.where(own, v, three)
                probs = jnp.exp(dot_nt(kx, qx[h]))
                grad = (probs * dot_nt(vx, gx[h])).astype(bf16)
                dv = dv + dot_nn(probs.astype(bf16), gm[h])
                dk = dk + dot_nn(grad, qm[h])
                turned = jnp.transpose(jnp.where(own, small, 0.0)).astype(bf16)
                dq[...] += dot_nn(turned, grad)
            dk = dk * cos_ref[rows, :] - swap_halves(dk) * sin_ref[rows, :]
            out_ref[rows, 128:256] = dk.astype(bf16)
            out_ref[rows, 256:384] = dv.astype(bf16)

    @pl.when(step == last)
    def _():
        g = jnp.transpose(dq[...])
        g = g * cos_ref[...] - swap_halves(g) * sin_ref[...]
        out_ref[:, 0:128] = g.astype(bf16)


def attend_back(grads, qkv, qrot, krot, att, lse, cosine, sine, qext, kext, block=384, scale=HD**-0.5):
    pieces = len(grads)
    frames = grads[0].shape[0]
    total = pieces * frames
    full = lambda a: pl.BlockSpec(a.shape, lambda p, i: (0, 0))
    return pl.pallas_call(
        functools.partial(attend_back_kernel, pieces, block, scale),
        grid=(2, total // block),
        in_specs=[pl.BlockSpec((frames, 128), lambda p, i: (0, p))] * pieces
        + [pl.BlockSpec((frames, 384), lambda p, i: (0, p))] * pieces
        + [pl.BlockSpec((total, 128), lambda p, i: (0, p))] * 4
        + [full(a) for a in (cosine, sine, qext, kext)],
        out_specs=pl.BlockSpec((total, 384), lambda p, i: (0, p)),
        out_shape=jax.ShapeDtypeStruct((total, 768), bf16),
        scratch_shapes=[pltpu.VMEM((2, total, 128), bf16)] * 4 + [pltpu.VMEM((128, total), f32)],
        compiler_params=pltpu.CompilerParams(vmem_limit_bytes=34 * 2**20),
        cost_estimate=pl.CostEstimate(
            flops=31 * 10**9, bytes_accessed=total * 8192, transcendentals=0
        ),
        name="attend_back",
    )(*grads, *qkv, qrot, krot, att, lse, cosine, sine, qext, kext)


def frame_tables(seg, pos, valid):
    half = HD // 2
    freq = 10000.0 ** (-jnp.arange(half, dtype=f32) / half)
    angle = pos.astype(f32)[:, None] * freq
    cosine, sine = jnp.cos(angle), jnp.sin(angle)
    cosine = jnp.concatenate([cosine] * 4, axis=1)
    sine = jnp.concatenate([-sine, sine, -sine, sine], axis=1)
    spot = jnp.arange(128)[None, :] % HD
    seg, valid = seg[:, None], valid[:, None] > 0
    qext = jnp.where((spot < 3) & (spot != seg) | (spot == 3), -NEG, 0.0).astype(bf16)
    kext = ((spot == seg) & (spot < 3) | (spot == 3) & ~valid | (spot >= 4) & (spot < 7)).astype(bf16)
    return cosine, sine, qext, kext


def swap(v, mask):
    return lax.ppermute(v, "seq", [(i, i ^ mask) for i in range(4)])


def spread(v, before=(), first=None):
    near = swap(v, 1)
    far = swap(v if first is None else after(v, first), 2)
    return [v, near, far, swap(after(far, *before) if before else far, 1)]


def collect(parts, wait=()):
    low = [part.astype(bf16) for part in parts]
    if wait:
        low = list(after(tuple(low), *wait))
    far_near = swap(low[3], 1)
    near = swap(low[1], 1)
    sent = (low[2].astype(f32) + far_near.astype(f32)).astype(bf16)
    far = swap(sent, 2)
    return parts[0] + near.astype(f32) + far.astype(f32), sent


def exchange(parts):
    return [parts[0], swap(parts[1], 1), swap(parts[2], 2), swap(parts[3], 3)]


def by_place(parts, me):
    odd, high = (me & 1) == 1, (me & 2) == 2
    parts = [jnp.where(odd, parts[t ^ 1], parts[t]) for t in range(4)]
    return [jnp.where(high, parts[t ^ 2], parts[t]) for t in range(4)]


def ring_step(v, step):
    return lax.ppermute(v, "dp", [(RING[i], RING[(i + step) % 8]) for i in range(8)])


class RingGather:
    def __init__(self, v):
        self.found, self.front, self.count = [(0, 0, v)], (v, v), 0

    def step(self, *before):
        one, other = after(self.front, *before) if before else self.front
        self.count += 1
        k = self.count
        if k < 4:
            self.front = ring_step(one, 1), ring_step(other, -1)
            self.found += [(k, 0, self.front[0]), (8 - k, 0, self.front[1])]
        else:
            middle = one.shape[0] // 2
            self.front = ring_step(one[:middle], 1), ring_step(other[middle:], -1)
            self.found += [(4, 0, self.front[0]), (4, middle, self.front[1])]
        return self.front


def ring_add_kernel(k, count, index_ref, *refs):
    plus, minus = refs[:count], refs[count : 2 * count]
    moving = refs[2 * count : -1 if k == 0 else -2]
    outs = refs[-1:] if k == 0 else refs[-2:]
    rows = plus[0].shape[1]
    middle = rows // 2
    upper, lower = slice(0, middle), slice(middle, rows)
    start = 0
    for i in range(count):
        columns = slice(start, start + plus[i].shape[2])
        start += plus[i].shape[2]
        if k == 4:
            outs[0][:, columns] = plus[i][0, upper, :].astype(bf16)
            outs[1][:, columns] = plus[i][0, lower, :].astype(bf16)
            continue
        ahead = plus[i][0].astype(f32)
        if k == 0:
            outs[0][:, columns] = (
                ahead + moving[0][:, columns].astype(f32) + moving[1][:, columns].astype(f32)
            )
            continue
        behind = minus[i][0].astype(f32)
        one, other = moving[0][:, columns].astype(f32), moving[1][:, columns].astype(f32)
        if k == 3:
            outs[0][upper, columns] = (ahead[upper] + one).astype(bf16)
            outs[0][lower, columns] = ahead[lower].astype(bf16)
            outs[1][upper, columns] = behind[upper].astype(bf16)
            outs[1][lower, columns] = (behind[lower] + other).astype(bf16)
        else:
            outs[0][:, columns] = (ahead + one).astype(bf16)
            outs[1][:, columns] = (behind + other).astype(bf16)


def ring_add(index, arrays, moving, k):
    rows, columns = arrays[0].shape[1], sum(a.shape[2] for a in arrays)
    ahead = [pl.BlockSpec((1, rows, a.shape[2]), lambda i, index: (index[(8 - k) % 8], 0, 0)) for a in arrays]
    behind = [pl.BlockSpec((1, rows, a.shape[2]), lambda i, index: (index[k], 0, 0)) for a in arrays]
    whole = lambda shape: pl.BlockSpec(shape, lambda i, index: (0, 0))
    height = rows // 2 if k == 4 else rows
    n_out = 1 if k == 0 else 2
    return pl.pallas_call(
        functools.partial(ring_add_kernel, k, len(arrays)),
        grid_spec=pltpu.PrefetchScalarGridSpec(
            num_scalar_prefetch=1,
            grid=(1,),
            in_specs=ahead + behind + [whole(m.shape) for m in moving],
            out_specs=[whole((height, columns))] * n_out,
        ),
        out_shape=[jax.ShapeDtypeStruct((height, columns), f32 if k == 0 else bf16)] * n_out,
        compiler_params=pltpu.CompilerParams(vmem_limit_bytes=16 * 2**20),
        cost_estimate=pl.CostEstimate(flops=10**9, bytes_accessed=10**6, transcendentals=0),
        name="ring_add",
    )(index, *arrays, *arrays, *moving)


class RingSum:
    def __init__(self, arrays, index, ringed):
        self.arrays, self.index, self.ringed = arrays, index, ringed
        self.front, self.count = (), 4

    def step(self, *before):
        if self.ringed:
            arrays, front = self.arrays, self.front
            if before:
                arrays, front = after((arrays, front), *before)
            moving = ring_add(self.index, arrays, front, self.count)
            self.front = ring_step(moving[0], 1), ring_step(moving[1], -1)
            self.count -= 1
        return self.front

    def total(self):
        if self.ringed:
            return ring_add(self.index, self.arrays, self.front, 0)[0]
        low = jnp.concatenate([a.astype(bf16) for a in self.arrays], axis=2)
        return lax.psum_scatter(low, "dp", scatter_dimension=0).astype(f32)


def after(v, *others):
    return lax.optimization_barrier((v, *others))[0]


def assemble_kernel(copies, n_in, n_out, index_ref, *refs):
    arrays, outs, sems = refs[:n_in], refs[n_in : n_in + n_out], refs[-1]
    moves = []
    me = index_ref[8]
    for number, (a, row, count, out, k, j, per_dp, per_seq, column, more) in enumerate(copies):
        start = index_ref[k] * per_dp + jnp.bitwise_xor(me, j) * per_seq + more
        target = outs[out].at[
            pl.ds(pl.multiple_of(start, count), count), pl.ds(column, arrays[a].shape[1])
        ]
        moves.append(
            pltpu.make_async_copy(arrays[a].at[pl.ds(row, count), :], target, sems.at[number])
        )
    for move in moves:
        move.start()
    for move in moves:
        move.wait()


def assemble(index, arrays, copies, shapes):
    anywhere = pl.BlockSpec(memory_space=pl.ANY)
    return pl.pallas_call(
        functools.partial(assemble_kernel, tuple(copies), len(arrays), len(shapes)),
        grid_spec=pltpu.PrefetchScalarGridSpec(
            num_scalar_prefetch=1,
            grid=(1,),
            in_specs=[anywhere] * len(arrays),
            out_specs=[pl.BlockSpec(shape, lambda i, index: (0, 0)) for shape in shapes],
            scratch_shapes=[pltpu.SemaphoreType.DMA((len(copies),))],
        ),
        out_shape=[jax.ShapeDtypeStruct(shape, bf16) for shape in shapes],
        compiler_params=pltpu.CompilerParams(vmem_limit_bytes=8 * 2**20 + 5 * sum(r * c for r, c in shapes)),
        cost_estimate=pl.CostEstimate(flops=9 * 10**9, bytes_accessed=1024, transcendentals=0),
        name="assemble",
    )(index, *arrays)


class Gather:
    def __init__(self, index):
        self.index, self.arrays, self.copies, self.shapes = index, [], [], []

    def out(self, rows, columns):
        self.shapes.append((rows, columns))
        return len(self.shapes) - 1

    def add(self, piece, k, blocks):
        self.arrays.append(piece)
        for row, count, out, j, per_dp, per_seq, column, more in blocks:
            self.copies.append(
                (len(self.arrays) - 1, row, count, out, k, j, per_dp, per_seq, column, more)
            )

    def run(self):
        return assemble(self.index, self.arrays, self.copies, self.shapes)


def half(v, which):
    middle = v.shape[1] // 2
    return jnp.where(which == 1, v[:, middle:], v[:, :middle])


def merge(mine, other, core):
    return jnp.concatenate(
        [jnp.where(core == 1, other, mine), jnp.where(core == 1, mine, other)], axis=1
    )


def by_dp(grad, groups):
    return grad.reshape(groups, grad.shape[0] // groups, grad.shape[1])


def finish(block, me):
    rows = block.shape[0] // 4
    low = block.astype(bf16)
    parts = by_place([low[t * rows : (t + 1) * rows] for t in range(4)], me)
    return by_place(exchange(parts), me)


def halves_sum(parts):
    total = [parts[c].astype(f32) + parts[2 + c].astype(f32) for c in range(2)]
    return jnp.concatenate(total, axis=1)


def on_device(
    layer_input,
    skip_input,
    time_embed,
    segment_ids,
    positions,
    valid_mask,
    skip_weight,
    time_weight,
    query_weight,
    key_weight,
    value_weight,
    out_weight,
    up_weight,
    down_weight,
    cotangent,
):
    rows, frames, width = layer_input.shape
    hidden = up_weight.shape[1]
    groups = lax.axis_size("dp")
    me, dp = lax.axis_index("seq"), lax.axis_index("dp")
    local = width // 4
    local_hidden = hidden // 4

    core = me & 1
    hidden_block = hidden // (groups * 4)
    ringed = groups == 8
    first_in, second_in = layer_input.reshape(frames, width), skip_input.reshape(frames, width)
    time_a, time_b = time_weight[:, : 2 * width], time_weight[:, 2 * width :]
    n_skip, n_time = skip_weight.shape[0], time_weight.shape[0]

    def needed():
        triple = [
            jnp.concatenate(
                [
                    w[:, t * local + p * 128 : t * local + (p + 1) * 128]
                    for p in range(2)
                    for w in (query_weight, key_weight, value_weight)
                ],
                axis=1,
            )
            for t in range(4)
        ]
        upper_w = [
            jnp.concatenate(
                [
                    up_weight[:, (g * 4 + t) * hidden_block : (g * 4 + t + 1) * hidden_block]
                    for g in range(groups)
                ],
                axis=1,
            )
            for t in range(4)
        ]
        return triple, upper_w

    triple, upper_w = needed()
    index = None
    marks = jnp.concatenate(spread(jnp.concatenate([segment_ids, positions, valid_mask])), axis=1)
    tables = frame_tables(marks[0], marks[1], marks[2])
    time_value = time_embed.reshape(frames, width).astype(f32)
    time_act = (time_value * jax.nn.sigmoid(time_value)).astype(bf16)
    joined = jnp.concatenate([first_in, second_in], axis=1)
    row_own = jnp.concatenate([first_in, second_in, time_act], axis=1)

    if ringed:
        place = jnp.asarray(PLACE, jnp.int32)[dp]
        order = jnp.asarray(RING, jnp.int32)[(place - jnp.arange(8)) % 8]
        index = jnp.concatenate([order, me[None].astype(jnp.int32)])

        first = Gather(index)
        o_skip, o_time_a = first.out(32 * n_skip, width), first.out(32 * n_time, 2 * width)
        own = jnp.concatenate([skip_weight, time_a[:, :width], time_a[:, width:]], axis=0)
        layout = [
            (0, n_skip, o_skip, 0),
            (n_skip, n_time, o_time_a, 0),
            (n_skip + n_time, n_time, o_time_a, width),
        ]
        n_own = own.shape[0]
        ring_a = RingGather(jnp.concatenate([own, swap(own, 2)], axis=0))
        ring_a.step()
        triple, upper_w, time_b, out_weight = after(
            (triple, upper_w, time_b, out_weight), ring_a.found[0][2]
        )

        def to_core(gather, entries, layout, n_own):
            near = [swap(piece, 1) for _, _, piece in entries]
            for (k, row, piece), other in zip(entries, near):
                for array, flip in ((piece, 0), (other, 1)):
                    for part in range(row // n_own, (row + piece.shape[0]) // n_own):
                        at_row = part * n_own - row
                        gather.add(
                            array,
                            k,
                            [
                                (at_row + at, count, out, (2 * part) ^ flip, 4 * count, count, column, 0)
                                for at, count, out, column in layout
                            ],
                        )
            return near

        rest = []
        for t in range(4):
            sides = [
                w[:, (t & 1) * (w.shape[1] // 2) : ((t & 1) + 1) * (w.shape[1] // 2)]
                for w in (out_weight, time_b)
            ]
            rest.append(jnp.concatenate([triple[t], *sides, upper_w[t]], axis=1))
        rest = by_place(rest, me)
        near = to_core(first, ring_a.found[:1], layout, n_own)
        ring_a.step(*near, *rest)
        near = to_core(first, ring_a.found[1:3], layout, n_own)
        rest = exchange(after(tuple(rest), ring_a.found[1][2]))
        time_far = swap(after(time_act, rest[2]), 2)
        second_far = swap(after(second_in, time_far), 2)
        ring_a.step(*near, *rest)
        near = to_core(first, ring_a.found[3:5], layout, n_own)
        ring_a.step(*near, *tables, time_far)
        rest = jnp.concatenate(by_place(rest, me), axis=0)
        cut = 3 * local + width // 2, 3 * local + 2 * width
        ring_b_own, ring_c_own, ring_d_own = after(
            (
                rest[:, : cut[0]],
                rest[:, cut[0] : cut[1]],
                jnp.concatenate([rest[:, cut[1] :], down_weight], axis=1),
            ),
            *ring_a.found[5][2:],
            *ring_a.found[6][2:],
        )
        ring_b, ring_c, ring_d = (RingGather(v) for v in (ring_b_own, ring_c_own, ring_d_own))
        near = to_core(first, ring_a.found[5:9], layout, n_own)
        ring_b.step()
        skip_full, time_a_full = first.run()
        ring_b.step(skip_full)

        def block_rows(ring, shape):
            gather = Gather(index)
            out = gather.out(*shape)
            for k, row, piece in ring.found:
                gather.add(piece, k, [(0, piece.shape[0], out, 0, width // 8, 0, 0, row)])
            return gather.run()[0]

    else:
        first_far, second_far, time_far = swap(first_in, 2), swap(second_in, 2), swap(time_act, 2)
        skip_full, time_a_full, time_b_full, out_full = (
            lax.all_gather(w, ("dp", "seq"), axis=0, tiled=True)
            for w in (skip_weight, time_a, time_b, out_weight)
        )
        triple_full, up_full = (
            lax.all_gather(
                jnp.concatenate(by_place(exchange(by_place(parts, me)), me), axis=0),
                "dp",
                axis=0,
                tiled=True,
            )
            for parts in (triple, upper_w)
        )
        down_full = lax.all_gather(down_weight, "dp", axis=0, tiled=True)
        out_sides = [half(out_full, core), half(out_full, 1 - core)]
        time_b_sides = [half(time_b_full, core), half(time_b_full, 1 - core)]

    base = dot_nn(joined, skip_full)
    shift_a, scale_a = jnp.split(dot_nn(time_act, time_a_full), 2, axis=1)
    normed_a, inverse_a = norm_rows(base)
    hidden_own = (normed_a * (1.0 + scale_a) + shift_a).astype(bf16)
    if ringed:
        hidden_own = after(hidden_own, second_far)
        ring_c.step(skip_full)
        ring_b.step(hidden_own)
        ring_b.step()
        ring_c.step(*ring_b.found[5][2:])
        ring_c.step(*ring_b.front)
        hidden_a = spread(hidden_own, ring_b.front)
        first_far = swap(after(first_in, hidden_a[2]), 2)
        wide = block_rows(ring_b, (width, cut[0]))
        triple_full = wide[:, : 3 * local]
        out_mine = wide[:, 3 * local :]
        out_sides = [out_mine, swap(after(out_mine, hidden_a[3]), 1)]
        ring_d.step(hidden_a[2])
    else:
        hidden_a = spread(hidden_own)
    qkv = [dot_nn(h, triple_full).astype(bf16) for h in hidden_a]
    att, logsum, query_rot, key_rot = attend(qkv, *tables)
    time_act_b = after(time_act, att)
    if ringed:
        att = after(att, *ring_c.front, *ring_d.front)
    att = after(att, first_far)
    att_parts = [att[j * frames : (j + 1) * frames] for j in range(4)]
    attended = exchange(att_parts)
    if ringed:
        ring_c.step(att)
        mine = block_rows(ring_c, (width, 3 * width // 2))
        time_b_sides = [mine, swap(mine, 1)]
        ring_d.step(*attended)
    shift_b, scale_b, gate_b = jnp.split(
        merge(dot_nn(time_act_b, time_b_sides[0]), dot_nn(time_act_b, time_b_sides[1]), core),
        3,
        axis=1,
    )
    upstream = cotangent.reshape(frames, width).astype(f32)
    ffn_grad = (upstream * gate_b).astype(bf16)
    attended = list(after(tuple(attended), ffn_grad))
    ffn_grad = spread(ffn_grad)
    attended = jnp.concatenate(by_place(attended, me), axis=1)
    middle = base + merge(dot_nn(attended, out_sides[0]), dot_nn(attended, out_sides[1]), core)
    normed_b, inverse_b = norm_rows(middle)

    hidden_own = (normed_b * (1.0 + scale_b) + shift_b).astype(bf16)
    if ringed:
        ring_d.step(hidden_own)
        ring_d.step()
    hidden_b = spread(hidden_own, (), ffn_grad[2])
    if ringed:
        ffn_full = block_rows(ring_d, (width, 2 * local_hidden))
        up_full, down_full = ffn_full[:, :local_hidden], ffn_full[:, local_hidden:]
    row_near = swap(after(row_own, hidden_b[3]), 1)
    row_far = jnp.concatenate([first_far, second_far, time_far], axis=1)
    row_inputs = [row_own, row_near, row_far, swap(after(row_far, hidden_b[3]), 1)]
    hb = [jnp.concatenate(hidden_b[:2]), jnp.concatenate(hidden_b[2:])]
    fg = [jnp.concatenate(ffn_grad[:2]), jnp.concatenate(ffn_grad[2:])]
    upper = dot_nn(hb[1], up_full)
    acted_far = gelu_value(upper).astype(bf16)
    part_far = dot_nn(acted_far, down_full)
    part_low = part_far.astype(bf16)
    fg[1] = after(fg[1], part_low)
    ug_far = (dot_nt(fg[1], down_full) * gelu_slope(upper)).astype(bf16)
    part_sent = (part_far[:frames] + swap(part_low[frames:], 1).astype(f32)).astype(bf16)
    far = dot_nt(after(ug_far, part_sent), up_full)
    far_low = far.astype(bf16)
    hb[0] = after(hb[0], far_low)
    upper = dot_nn(hb[0], up_full)
    sent = (far[:frames] + swap(far_low[frames:], 1).astype(f32)).astype(bf16)
    fg[0] = after(fg[0], sent)
    grad_far = swap(sent, 2)
    acted = [gelu_value(upper).astype(bf16), acted_far]
    ug = [(dot_nt(fg[0], down_full) * gelu_slope(upper)).astype(bf16), ug_far]
    own = dot_nt(ug[0], up_full)
    hidden_b_grad = (
        own[:frames] + swap(own[frames:].astype(bf16), 1).astype(f32) + grad_far.astype(f32)
    )
    acted, fg, ug, hb = after((acted, fg, ug, hb), own, row_near, row_inputs[3])
    part = dot_nn(acted[0], down_full)
    ffn = (
        part[:frames]
        + swap(part[frames:].astype(bf16), 1).astype(f32)
        + swap(after(part_sent, grad_far), 2).astype(f32)
    )
    grad_down = dot_tn(acted[0], fg[0]) + dot_tn(acted[1], fg[1])
    grad_up = dot_tn(hb[0], ug[0]) + dot_tn(hb[1], ug[1])
    grad_ffn = jnp.concatenate([grad_up.astype(bf16), grad_down.astype(bf16)], axis=1)
    hidden_b_grad = after(hidden_b_grad, grad_ffn, part)
    ffn_sum = lax.psum_scatter(grad_ffn, "dp", scatter_dimension=0, tiled=True).astype(f32)

    scale_b_grad = hidden_b_grad * normed_b
    middle_grad = upstream + norm_back(hidden_b_grad * (1.0 + scale_b), normed_b, inverse_b)
    branch_grad = middle_grad.astype(bf16)
    branch_sides = [half(branch_grad, core), half(branch_grad, 1 - core)]
    attended_grad = (
        dot_nt(branch_sides[0], out_sides[0]) + dot_nt(branch_sides[1], out_sides[1])
    ).astype(bf16)
    att_grad_parts = by_place([attended_grad[:, t * local : (t + 1) * local] for t in range(4)], me)
    att_grad = exchange(att_grad_parts)
    def to_columns(grads):
        return [
            jnp.concatenate([g[:, t * local : (t + 1) * local] for g in grads], axis=1) for t in range(4)
        ]

    ffn = after(ffn, *att_grad_parts)
    output = (middle + gate_b * ffn).astype(bf16).reshape(rows, frames, width)
    modul_b_grad = [v.astype(bf16) for v in (hidden_b_grad, scale_b_grad, upstream * ffn)]
    modul_sent = by_place(to_columns(modul_b_grad), me)
    modul_b_parts = exchange(modul_sent)
    grad_out = [dot_tn(attended, side).astype(bf16) for side in branch_sides]
    near_out = swap(grad_out[1], 1)
    att_grad = after(tuple(att_grad), *modul_sent, *grad_out, row_inputs[3])
    triple_grad = attend_back(att_grad, qkv, query_rot, key_rot, att, logsum, *tables)
    triple_grad = after(triple_grad, *modul_b_parts, near_out)
    back = dot_nt(triple_grad, triple_full)
    far_low = back[3 * frames :].astype(bf16)
    triple_grad, modul_b_grad, hidden_a_all = after(
        (triple_grad, tuple(modul_b_grad), jnp.concatenate(hidden_a)), far_low
    )
    sent = (back[2 * frames : 3 * frames] + swap(far_low, 1).astype(f32)).astype(bf16)
    hidden_a_grad = (
        back[:frames]
        + swap(back[frames : 2 * frames].astype(bf16), 1).astype(f32)
        + swap(sent, 2).astype(f32)
    )
    triple_grad, hidden_a_all = after((triple_grad, hidden_a_all), sent)
    grad_triple = dot_tn(hidden_a_all, triple_grad).astype(bf16)
    modul_b_parts = after(tuple(modul_b_parts), sent, grad_triple)
    grad_time_b = sum(dot_tn(v[:, 2 * width :], g) for v, g in zip(row_inputs, modul_b_parts))
    grad_out = (grad_out[0].astype(f32) + near_out.astype(f32)).astype(bf16)
    ring_w = RingSum(
        [by_dp(g, groups) for g in (grad_time_b.astype(bf16), grad_out, grad_triple)], index, ringed
    )
    ring_w.step()
    modul_b_grad = jnp.concatenate(modul_b_grad, axis=1)
    time_back_b = dot_nt(half(modul_b_grad, core), time_b_sides[0]) + dot_nt(
        half(modul_b_grad, 1 - core), time_b_sides[1]
    )
    hidden_a_grad = after(hidden_a_grad, time_back_b)

    scale_a_grad = hidden_a_grad * normed_a
    modul_a_grad = jnp.concatenate([hidden_a_grad, scale_a_grad], axis=1).astype(bf16)
    modul_sent = by_place(to_columns([modul_a_grad[:, :width], modul_a_grad[:, width:]]), me)
    modul_parts = exchange(modul_sent)
    base_grad = (
        middle_grad + norm_back(hidden_a_grad * (1.0 + scale_a), normed_a, inverse_a)
    ).astype(bf16)
    base_sent = by_place([base_grad[:, t * local : (t + 1) * local] for t in range(4)], me)
    base_parts = exchange(base_sent)
    step = ring_w.step(*modul_sent)
    base_grad, modul_a_grad = after((base_grad, modul_a_grad), *base_sent)
    joined_grad = dot_nt(base_grad, skip_full)
    time_back = dot_nt(modul_a_grad, time_a_full) + time_back_b
    time_grad = (time_back * silu_slope(time_value)).reshape(rows, frames, width)
    modul_parts = after(tuple(modul_parts), joined_grad, *step)
    ring_w.step()
    grad_time_a = sum(dot_tn(v[:, 2 * width :], g) for v, g in zip(row_inputs, modul_parts))
    grad_skip = sum(dot_tn(v[:, : 2 * width], g) for v, g in zip(row_inputs, base_parts))
    rows_skip = n_skip // 2
    grad_skip = grad_skip.reshape(groups, 4, 2, rows_skip, local)
    grad_skip = jnp.concatenate([grad_skip[:, :, 0], grad_skip[:, :, 1]], axis=3)
    ring_l = RingSum(
        [
            grad_skip.reshape(groups, 4 * rows_skip, 2 * local).astype(bf16),
            by_dp(grad_time_a.astype(bf16), groups),
        ],
        index,
        ringed,
    )
    ring_l.step()
    ring_w.step(grad_skip)
    ring_l.step()
    wide_sum = ring_w.total()
    ring_l.step(wide_sum)
    parts = finish(jnp.concatenate([ffn_sum[:, :local_hidden], wide_sum], axis=1), me)
    ring_l.step(*parts)
    up_sum = jnp.concatenate(
        [
            p[:, g * hidden_block : (g + 1) * hidden_block]
            for g in range(groups)
            for p in parts
        ],
        axis=1,
    )
    split = local_hidden + 3 * local, local_hidden + 3 * local + width // 2
    by_blocks = lambda parts, start, i: jnp.concatenate(
        [p[:, start + i * local : start + (i + 1) * local] for p in parts], axis=1
    ).astype(f32)
    out_sum = halves_sum([p[:, split[0] : split[1]] for p in parts])
    triples = [
        jnp.concatenate(
            [
                p[:, split[1] + i * 128 + q * 384 : split[1] + (i + 1) * 128 + q * 384]
                for p in parts
                for q in range(2)
            ],
            axis=1,
        ).astype(f32)
        for i in range(3)
    ]
    last = finish(ring_l.total(), me)
    columns = [by_blocks(last, 0, i) for i in range(4)]
    time_b_sum = jnp.concatenate([by_blocks(parts, local_hidden, i) for i in range(3)], axis=1)
    skip_sum = jnp.concatenate(columns[:2], axis=0)
    time_a_sum = jnp.concatenate(columns[2:4], axis=1)
    return (
        output,
        joined_grad[:, :width].reshape(rows, frames, width),
        joined_grad[:, width:].reshape(rows, frames, width),
        time_grad,
        skip_sum,
        jnp.concatenate([time_a_sum, time_b_sum], axis=1),
        *triples,
        out_sum,
        up_sum.astype(f32),
        ffn_sum[:, local_hidden:],
    )


def solution(mesh):
    frames = P("dp", "seq", None)
    marks = P("dp", "seq")
    weight = P(("dp", "seq"), None)
    return jax.shard_map(
        on_device,
        mesh=mesh,
        in_specs=(frames,) * 3 + (marks,) * 3 + (weight,) * 8 + (frames,),
        out_specs=(frames,) * 4 + (weight,) * 8,
        check_vma=False,
    )
```

```python
import functools

import jax
import jax.numpy as jnp
from jax import lax
from jax.experimental import pallas as pl
from jax.experimental.pallas import tpu as pltpu
from jax.sharding import PartitionSpec as P

HD = 64
NEG = 1e30
norm_eps = 1e-06
gelu_coef = 0.7978845608028654
f32, bf16 = jnp.float32, jnp.bfloat16

RING = (0, 2, 4, 6, 7, 5, 3, 1)
PLACE = tuple(RING.index(d) for d in range(8))


def dot_nt(a, b):
    return lax.dot_general(a, b, (((1,), (1,)), ((), ())), preferred_element_type=f32)


def dot_nn(a, b):
    return lax.dot_general(a, b, (((1,), (0,)), ((), ())), preferred_element_type=f32)


def dot_tn(a, b):
    return lax.dot_general(a, b, (((0,), (0,)), ((), ())), preferred_element_type=f32)


def silu_slope(v):
    sig = jax.nn.sigmoid(v)
    return sig * (1.0 + v * (1.0 - sig))


def gelu_value(u):
    return 0.5 * u * (1.0 + jnp.tanh(gelu_coef * (u + 0.044715 * u * u * u)))


def gelu_slope(u):
    inner = jnp.tanh(gelu_coef * (u + 0.044715 * u * u * u))
    return 0.5 * (1.0 + inner) + 0.5 * u * (1.0 - inner * inner) * gelu_coef * (
        1.0 + 3.0 * 0.044715 * u * u
    )


def norm_rows(v):
    mean = jnp.mean(v, axis=-1, keepdims=True)
    centred = v - mean
    inverse = lax.rsqrt(jnp.mean(centred * centred, axis=-1, keepdims=True) + norm_eps)
    return (centred * inverse, inverse)


def norm_back(grad, normed, inverse):
    return inverse * (
        grad
        - jnp.mean(grad, axis=-1, keepdims=True)
        - normed * jnp.mean(grad * normed, axis=-1, keepdims=True)
    )

def lanes_of(shape):
    return lax.broadcasted_iota(jnp.int32, shape, 1)


def swap_halves(v):
    lane = lanes_of(v.shape)
    return jnp.where(lane % HD < HD // 2, pltpu.roll(v, 128 - HD // 2, 1), pltpu.roll(v, HD // 2, 1))


def three_parts(v):
    hi = v.astype(bf16)
    rest = v - hi.astype(f32)
    mid = rest.astype(bf16)
    low = (rest - mid.astype(f32)).astype(bf16)
    return hi, mid, low


def attend_kernel(pieces, block, scale, *refs):
    qkv = refs[:pieces]
    cos_ref, sin_ref, qext_ref, kext_ref = refs[pieces : pieces + 4]
    att_ref, lse_ref, qrot_ref, krot_ref = refs[pieces + 4 : pieces + 8]
    kx, vx = refs[pieces + 8 :]
    step = pl.program_id(1)
    frames = qkv[0].shape[0]
    per_piece = frames // block

    @pl.when(step == 0)
    def _():
        for j in range(pieces):
            rows = pl.ds(j * frames, frames)
            k = qkv[j][:, 128:256].astype(f32)
            k = (k * cos_ref[rows, :] + swap_halves(k) * sin_ref[rows, :]).astype(bf16)
            krot_ref[rows, :] = k
            v = qkv[j][:, 256:384]
            ext = kext_ref[rows, :]
            lane = lanes_of(k.shape)
            one = jnp.where(lane % HD == 0, 1.0, 0.0).astype(bf16)
            low_lane = lane < HD
            kx[0, rows, :] = jnp.where(low_lane, k, ext)
            kx[1, rows, :] = jnp.where(low_lane, ext, k)
            vx[0, rows, :] = jnp.where(low_lane, v, one)
            vx[1, rows, :] = jnp.where(low_lane, one, v)

    rows = pl.ds(pl.multiple_of(step * block, block), block)
    for j in range(pieces):

        @pl.when(step // per_piece == j)
        def _(j=j):
            sub = pl.ds(pl.multiple_of((step - j * per_piece) * block, block), block)
            q = qkv[j][sub, 0:128].astype(f32)
            q = (q * cos_ref[rows, :] + swap_halves(q) * sin_ref[rows, :]).astype(bf16)
            qrot_ref[...] = (q.astype(f32) * scale).astype(bf16)

    q = qrot_ref[...]
    ext = qext_ref[rows, :]
    low_lane = lanes_of(q.shape) < HD
    outs = []
    for h in range(2):
        qx = jnp.where(low_lane, q, ext) if h == 0 else jnp.where(low_lane, ext, q)
        scores = dot_nt(qx, kx[h])
        top = jnp.max(scores, axis=1, keepdims=True)
        expo = jnp.exp(scores - top)
        mixed = dot_nn(expo.astype(bf16), vx[h])
        total = mixed[:, HD : HD + 1] if h == 0 else mixed[:, 0:1]
        outs.append((mixed / total, top + jnp.log(total)))
    low_out = lanes_of((block, 128)) < HD
    att_ref[...] = jnp.where(low_out, outs[0][0], outs[1][0]).astype(bf16)
    lse_ref[...] = jnp.where(low_out, outs[0][1], outs[1][1])


def attend(qkv, cosine, sine, qext, kext, block=384, scale=HD**-0.5):
    pieces = len(qkv)
    frames = qkv[0].shape[0]
    total = pieces * frames
    full = lambda a: pl.BlockSpec(a.shape, lambda p, i: (0, 0))
    tile = pl.BlockSpec((block, 128), lambda p, i: (i, p))
    return pl.pallas_call(
        functools.partial(attend_kernel, pieces, block, scale),
        grid=(2, total // block),
        in_specs=[pl.BlockSpec((frames, 384), lambda p, i: (0, p))] * pieces
        + [full(a) for a in (cosine, sine, qext, kext)],
        out_specs=[tile, tile, tile, pl.BlockSpec((total, 128), lambda p, i: (0, p))],
        out_shape=[jax.ShapeDtypeStruct((total, 256), t) for t in (bf16, f32, bf16, bf16)],
        scratch_shapes=[pltpu.VMEM((2, total, 128), bf16), pltpu.VMEM((2, total, 128), bf16)],
        compiler_params=pltpu.CompilerParams(vmem_limit_bytes=24 * 2**20),
        cost_estimate=pl.CostEstimate(
            flops=21 * 10**9, bytes_accessed=total * 4096, transcendentals=0
        ),
        name="attend",
    )(*qkv, cosine, sine, qext, kext)


def attend_back_kernel(pieces, block, scale, *refs):
    grads = refs[:pieces]
    values = refs[pieces : 2 * pieces]
    qrot_ref, krot_ref, att_ref, lse_ref, cos_ref, sin_ref, qext_ref, kext_ref = refs[2 * pieces : 2 * pieces + 8]
    out_ref = refs[2 * pieces + 8]
    qx, gx, qm, gm, dq = refs[2 * pieces + 9 :]
    step = pl.program_id(1)
    last = pl.num_programs(1) - 1
    frames = grads[0].shape[0]
    per_piece = frames // block

    @pl.when(step == 0)
    def _():
        for j in range(pieces):
            rows = pl.ds(j * frames, frames)
            q = qrot_ref[rows, :]
            g = grads[j][...]
            lane = lanes_of(q.shape)
            low_lane = lane < HD
            spot = lane % HD
            prod = g.astype(f32) * att_ref[rows, :].astype(f32)
            zero = jnp.zeros_like(q)
            lse = lse_ref[rows, :]
            for h in range(2):
                own = low_lane if h == 0 else jnp.logical_not(low_lane)
                lse_h = lse[:, 0:1] if h == 0 else lse[:, HD : HD + 1]
                delta = jnp.sum(jnp.where(own, prod, 0.0), axis=1, keepdims=True)
                a, b, c = (t.astype(f32) for t in three_parts(-lse_h))
                part = jnp.where(spot == 4, a, jnp.where(spot == 5, b, jnp.where(spot == 6, c, qext_ref[rows, :].astype(f32))))
                qx[h, rows, :] = jnp.where(own, q, part.astype(bf16))
                a, b, c = (t.astype(f32) for t in three_parts(-delta))
                part = jnp.where(spot == 0, a, jnp.where(spot == 1, b, jnp.where(spot == 2, c, 0.0)))
                gx[h, rows, :] = jnp.where(own, g, part.astype(bf16))
                qm[h, rows, :] = jnp.where(own, q, zero)
                gm[h, rows, :] = jnp.where(own, g, zero)
        dq[...] = jnp.zeros_like(dq)

    rows = pl.ds(pl.multiple_of(step * block, block), block)
    for j in range(pieces):

        @pl.when(step // per_piece == j)
        def _(j=j):
            sub = pl.ds(pl.multiple_of((step - j * per_piece) * block, block), block)
            k = krot_ref[rows, :]
            v = values[j][sub, 256:384]
            ext = kext_ref[rows, :]
            lane = lanes_of(k.shape)
            low_lane = lane < HD
            three = jnp.where(lane % HD < 3, 1.0, 0.0).astype(bf16)
            zero = jnp.zeros_like(k)
            small = k.astype(f32) * scale
            dk = jnp.zeros((block, 128), f32)
            dv = jnp.zeros((block, 128), f32)
            for h in range(2):
                own = low_lane if h == 0 else jnp.logical_not(low_lane)
                kx = jnp.where(own, k, ext)
                vx = jnp.where(own, v, three)
                probs = jnp.exp(dot_nt(kx, qx[h]))
                grad = (probs * dot_nt(vx, gx[h])).astype(bf16)
                dv = dv + dot_nn(probs.astype(bf16), gm[h])
                dk = dk + dot_nn(grad, qm[h])
                turned = jnp.transpose(jnp.where(own, small, 0.0)).astype(bf16)
                dq[...] += dot_nn(turned, grad)
            dk = dk * cos_ref[rows, :] - swap_halves(dk) * sin_ref[rows, :]
            out_ref[rows, 128:256] = dk.astype(bf16)
            out_ref[rows, 256:384] = dv.astype(bf16)

    @pl.when(step == last)
    def _():
        g = jnp.transpose(dq[...])
        g = g * cos_ref[...] - swap_halves(g) * sin_ref[...]
        out_ref[:, 0:128] = g.astype(bf16)


def attend_back(grads, qkv, qrot, krot, att, lse, cosine, sine, qext, kext, block=384, scale=HD**-0.5):
    pieces = len(grads)
    frames = grads[0].shape[0]
    total = pieces * frames
    full = lambda a: pl.BlockSpec(a.shape, lambda p, i: (0, 0))
    return pl.pallas_call(
        functools.partial(attend_back_kernel, pieces, block, scale),
        grid=(2, total // block),
        in_specs=[pl.BlockSpec((frames, 128), lambda p, i: (0, p))] * pieces
        + [pl.BlockSpec((frames, 384), lambda p, i: (0, p))] * pieces
        + [pl.BlockSpec((total, 128), lambda p, i: (0, p))] * 4
        + [full(a) for a in (cosine, sine, qext, kext)],
        out_specs=pl.BlockSpec((total, 384), lambda p, i: (0, p)),
        out_shape=jax.ShapeDtypeStruct((total, 768), bf16),
        scratch_shapes=[pltpu.VMEM((2, total, 128), bf16)] * 4 + [pltpu.VMEM((128, total), f32)],
        compiler_params=pltpu.CompilerParams(vmem_limit_bytes=34 * 2**20),
        cost_estimate=pl.CostEstimate(
            flops=31 * 10**9, bytes_accessed=total * 8192, transcendentals=0
        ),
        name="attend_back",
    )(*grads, *qkv, qrot, krot, att, lse, cosine, sine, qext, kext)


def frame_tables(seg, pos, valid):
    half = HD // 2
    freq = 10000.0 ** (-jnp.arange(half, dtype=f32) / half)
    angle = pos.astype(f32)[:, None] * freq
    cosine, sine = jnp.cos(angle), jnp.sin(angle)
    cosine = jnp.concatenate([cosine] * 4, axis=1)
    sine = jnp.concatenate([-sine, sine, -sine, sine], axis=1)
    spot = jnp.arange(128)[None, :] % HD
    seg, valid = seg[:, None], valid[:, None] > 0
    qext = jnp.where((spot < 3) & (spot != seg) | (spot == 3), -NEG, 0.0).astype(bf16)
    kext = ((spot == seg) & (spot < 3) | (spot == 3) & ~valid | (spot >= 4) & (spot < 7)).astype(bf16)
    return cosine, sine, qext, kext


def swap(v, mask):
    return lax.ppermute(v, "seq", [(i, i ^ mask) for i in range(4)])


def spread(v, before=(), first=None):
    near = swap(v, 1)
    far = swap(v if first is None else after(v, first), 2)
    return [v, near, far, swap(after(far, *before) if before else far, 1)]


def collect(parts, wait=()):
    low = [part.astype(bf16) for part in parts]
    if wait:
        low = list(after(tuple(low), *wait))
    far_near = swap(low[3], 1)
    near = swap(low[1], 1)
    sent = (low[2].astype(f32) + far_near.astype(f32)).astype(bf16)
    far = swap(sent, 2)
    return parts[0] + near.astype(f32) + far.astype(f32), sent


def exchange(parts):
    return [parts[0], swap(parts[1], 1), swap(parts[2], 2), swap(parts[3], 3)]


def by_place(parts, me):
    odd, high = (me & 1) == 1, (me & 2) == 2
    parts = [jnp.where(odd, parts[t ^ 1], parts[t]) for t in range(4)]
    return [jnp.where(high, parts[t ^ 2], parts[t]) for t in range(4)]


def ring_step(v, step):
    return lax.ppermute(v, "dp", [(RING[i], RING[(i + step) % 8]) for i in range(8)])


class RingGather:
    def __init__(self, v):
        self.found, self.front, self.count = [(0, 0, v)], (v, v), 0

    def step(self, *before):
        one, other = after(self.front, *before) if before else self.front
        self.count += 1
        k = self.count
        if k < 4:
            self.front = ring_step(one, 1), ring_step(other, -1)
            self.found += [(k, 0, self.front[0]), (8 - k, 0, self.front[1])]
        else:
            middle = one.shape[0] // 2
            self.front = ring_step(one[:middle], 1), ring_step(other[middle:], -1)
            self.found += [(4, 0, self.front[0]), (4, middle, self.front[1])]
        return self.front


def ring_add_kernel(k, count, index_ref, *refs):
    plus, minus = refs[:count], refs[count : 2 * count]
    moving = refs[2 * count : -1 if k == 0 else -2]
    outs = refs[-1:] if k == 0 else refs[-2:]
    rows = plus[0].shape[1]
    middle = rows // 2
    upper, lower = slice(0, middle), slice(middle, rows)
    start = 0
    for i in range(count):
        columns = slice(start, start + plus[i].shape[2])
        start += plus[i].shape[2]
        if k == 4:
            outs[0][:, columns] = plus[i][0, upper, :].astype(bf16)
            outs[1][:, columns] = plus[i][0, lower, :].astype(bf16)
            continue
        ahead = plus[i][0].astype(f32)
        if k == 0:
            outs[0][:, columns] = (
                ahead + moving[0][:, columns].astype(f32) + moving[1][:, columns].astype(f32)
            )
            continue
        behind = minus[i][0].astype(f32)
        one, other = moving[0][:, columns].astype(f32), moving[1][:, columns].astype(f32)
        if k == 3:
            outs[0][upper, columns] = (ahead[upper] + one).astype(bf16)
            outs[0][lower, columns] = ahead[lower].astype(bf16)
            outs[1][upper, columns] = behind[upper].astype(bf16)
            outs[1][lower, columns] = (behind[lower] + other).astype(bf16)
        else:
            outs[0][:, columns] = (ahead + one).astype(bf16)
            outs[1][:, columns] = (behind + other).astype(bf16)


def ring_add(index, arrays, moving, k):
    rows, columns = arrays[0].shape[1], sum(a.shape[2] for a in arrays)
    ahead = [pl.BlockSpec((1, rows, a.shape[2]), lambda i, index: (index[(8 - k) % 8], 0, 0)) for a in arrays]
    behind = [pl.BlockSpec((1, rows, a.shape[2]), lambda i, index: (index[k], 0, 0)) for a in arrays]
    whole = lambda shape: pl.BlockSpec(shape, lambda i, index: (0, 0))
    height = rows // 2 if k == 4 else rows
    n_out = 1 if k == 0 else 2
    return pl.pallas_call(
        functools.partial(ring_add_kernel, k, len(arrays)),
        grid_spec=pltpu.PrefetchScalarGridSpec(
            num_scalar_prefetch=1,
            grid=(1,),
            in_specs=ahead + behind + [whole(m.shape) for m in moving],
            out_specs=[whole((height, columns))] * n_out,
        ),
        out_shape=[jax.ShapeDtypeStruct((height, columns), f32 if k == 0 else bf16)] * n_out,
        compiler_params=pltpu.CompilerParams(vmem_limit_bytes=16 * 2**20),
        cost_estimate=pl.CostEstimate(flops=10**9, bytes_accessed=10**6, transcendentals=0),
        name="ring_add",
    )(index, *arrays, *arrays, *moving)


class RingSum:
    def __init__(self, arrays, index, ringed):
        self.arrays, self.index, self.ringed = arrays, index, ringed
        self.front, self.count = (), 4

    def step(self, *before):
        if self.ringed:
            arrays, front = self.arrays, self.front
            if before:
                arrays, front = after((arrays, front), *before)
            moving = ring_add(self.index, arrays, front, self.count)
            self.front = ring_step(moving[0], 1), ring_step(moving[1], -1)
            self.count -= 1
        return self.front

    def total(self):
        if self.ringed:
            return ring_add(self.index, self.arrays, self.front, 0)[0]
        low = jnp.concatenate([a.astype(bf16) for a in self.arrays], axis=2)
        return lax.psum_scatter(low, "dp", scatter_dimension=0).astype(f32)


def after(v, *others):
    return lax.optimization_barrier((v, *others))[0]


def assemble_kernel(copies, n_in, n_out, index_ref, *refs):
    arrays, outs, sems = refs[:n_in], refs[n_in : n_in + n_out], refs[-1]
    moves = []
    me = index_ref[8]
    for number, (a, row, count, out, k, j, per_dp, per_seq, column, more) in enumerate(copies):
        start = index_ref[k] * per_dp + jnp.bitwise_xor(me, j) * per_seq + more
        target = outs[out].at[
            pl.ds(pl.multiple_of(start, count), count), pl.ds(column, arrays[a].shape[1])
        ]
        moves.append(
            pltpu.make_async_copy(arrays[a].at[pl.ds(row, count), :], target, sems.at[number])
        )
    for move in moves:
        move.start()
    for move in moves:
        move.wait()


def assemble(index, arrays, copies, shapes):
    anywhere = pl.BlockSpec(memory_space=pl.ANY)
    return pl.pallas_call(
        functools.partial(assemble_kernel, tuple(copies), len(arrays), len(shapes)),
        grid_spec=pltpu.PrefetchScalarGridSpec(
            num_scalar_prefetch=1,
            grid=(1,),
            in_specs=[anywhere] * len(arrays),
            out_specs=[pl.BlockSpec(shape, lambda i, index: (0, 0)) for shape in shapes],
            scratch_shapes=[pltpu.SemaphoreType.DMA((len(copies),))],
        ),
        out_shape=[jax.ShapeDtypeStruct(shape, bf16) for shape in shapes],
        compiler_params=pltpu.CompilerParams(vmem_limit_bytes=8 * 2**20 + 5 * sum(r * c for r, c in shapes)),
        cost_estimate=pl.CostEstimate(flops=9 * 10**9, bytes_accessed=1024, transcendentals=0),
        name="assemble",
    )(index, *arrays)


class Gather:
    def __init__(self, index):
        self.index, self.arrays, self.copies, self.shapes = index, [], [], []

    def out(self, rows, columns):
        self.shapes.append((rows, columns))
        return len(self.shapes) - 1

    def add(self, piece, k, blocks):
        self.arrays.append(piece)
        for row, count, out, j, per_dp, per_seq, column, more in blocks:
            self.copies.append(
                (len(self.arrays) - 1, row, count, out, k, j, per_dp, per_seq, column, more)
            )

    def run(self):
        return assemble(self.index, self.arrays, self.copies, self.shapes)


def half(v, which):
    middle = v.shape[1] // 2
    return jnp.where(which == 1, v[:, middle:], v[:, :middle])


def merge(mine, other, core):
    return jnp.concatenate(
        [jnp.where(core == 1, other, mine), jnp.where(core == 1, mine, other)], axis=1
    )


def by_dp(grad, groups):
    return grad.reshape(groups, grad.shape[0] // groups, grad.shape[1])


def finish(block, me):
    rows = block.shape[0] // 4
    low = block.astype(bf16)
    parts = by_place([low[t * rows : (t + 1) * rows] for t in range(4)], me)
    return by_place(exchange(parts), me)


def halves_sum(parts):
    total = [parts[c].astype(f32) + parts[2 + c].astype(f32) for c in range(2)]
    return jnp.concatenate(total, axis=1)


def on_device(
    layer_input,
    skip_input,
    time_embed,
    segment_ids,
    positions,
    valid_mask,
    skip_weight,
    time_weight,
    query_weight,
    key_weight,
    value_weight,
    out_weight,
    up_weight,
    down_weight,
    cotangent,
):
    rows, frames, width = layer_input.shape
    hidden = up_weight.shape[1]
    groups = lax.axis_size("dp")
    me, dp = lax.axis_index("seq"), lax.axis_index("dp")
    local = width // 4
    local_hidden = hidden // 4

    core = me & 1
    hidden_block = hidden // (groups * 4)
    ringed = groups == 8
    first_in, second_in = layer_input.reshape(frames, width), skip_input.reshape(frames, width)
    time_a, time_b = time_weight[:, : 2 * width], time_weight[:, 2 * width :]
    n_skip, n_time = skip_weight.shape[0], time_weight.shape[0]

    def needed():
        triple = [
            jnp.concatenate(
                [
                    w[:, t * local + p * 128 : t * local + (p + 1) * 128]
                    for p in range(2)
                    for w in (query_weight, key_weight, value_weight)
                ],
                axis=1,
            )
            for t in range(4)
        ]
        upper_w = [
            jnp.concatenate(
                [
                    up_weight[:, (g * 4 + t) * hidden_block : (g * 4 + t + 1) * hidden_block]
                    for g in range(groups)
                ],
                axis=1,
            )
            for t in range(4)
        ]
        return triple, upper_w

    triple, upper_w = needed()
    index = None
    marks = jnp.concatenate(spread(jnp.concatenate([segment_ids, positions, valid_mask])), axis=1)
    tables = frame_tables(marks[0], marks[1], marks[2])
    time_value = time_embed.reshape(frames, width).astype(f32)
    time_act = (time_value * jax.nn.sigmoid(time_value)).astype(bf16)
    joined = jnp.concatenate([first_in, second_in], axis=1)
    row_own = jnp.concatenate([first_in, second_in, time_act], axis=1)

    if ringed:
        place = jnp.asarray(PLACE, jnp.int32)[dp]
        order = jnp.asarray(RING, jnp.int32)[(place - jnp.arange(8)) % 8]
        index = jnp.concatenate([order, me[None].astype(jnp.int32)])

        first = Gather(index)
        o_skip, o_time_a = first.out(32 * n_skip, width), first.out(32 * n_time, 2 * width)
        own = jnp.concatenate([skip_weight, time_a[:, :width], time_a[:, width:]], axis=0)
        layout = [
            (0, n_skip, o_skip, 0),
            (n_skip, n_time, o_time_a, 0),
            (n_skip + n_time, n_time, o_time_a, width),
        ]
        n_own = own.shape[0]
        ring_a = RingGather(jnp.concatenate([own, swap(own, 2)], axis=0))
        ring_a.step()
        triple, upper_w, time_b, out_weight = after(
            (triple, upper_w, time_b, out_weight), ring_a.found[0][2]
        )

        def to_core(gather, entries, layout, n_own):
            near = [swap(piece, 1) for _, _, piece in entries]
            for (k, row, piece), other in zip(entries, near):
                for array, flip in ((piece, 0), (other, 1)):
                    for part in range(row // n_own, (row + piece.shape[0]) // n_own):
                        at_row = part * n_own - row
                        gather.add(
                            array,
                            k,
                            [
                                (at_row + at, count, out, (2 * part) ^ flip, 4 * count, count, column, 0)
                                for at, count, out, column in layout
                            ],
                        )
            return near

        rest = []
        for t in range(4):
            sides = [
                w[:, (t & 1) * (w.shape[1] // 2) : ((t & 1) + 1) * (w.shape[1] // 2)]
                for w in (out_weight, time_b)
            ]
            rest.append(jnp.concatenate([triple[t], *sides, upper_w[t]], axis=1))
        rest = by_place(rest, me)
        near = to_core(first, ring_a.found[:1], layout, n_own)
        ring_a.step(*near, *rest)
        near = to_core(first, ring_a.found[1:3], layout, n_own)
        rest = exchange(after(tuple(rest), ring_a.found[1][2]))
        time_far = swap(after(time_act, rest[2]), 2)
        second_far = swap(after(second_in, time_far), 2)
        ring_a.step(*near, *rest)
        near = to_core(first, ring_a.found[3:5], layout, n_own)
        ring_a.step(*near, *tables, time_far)
        rest = jnp.concatenate(by_place(rest, me), axis=0)
        cut = 3 * local + width // 2, 3 * local + 2 * width
        ring_b_own, ring_c_own, ring_d_own = after(
            (
                rest[:, : cut[0]],
                rest[:, cut[0] : cut[1]],
                jnp.concatenate([rest[:, cut[1] :], down_weight], axis=1),
            ),
            *ring_a.found[5][2:],
            *ring_a.found[6][2:],
        )
        ring_b, ring_c, ring_d = (RingGather(v) for v in (ring_b_own, ring_c_own, ring_d_own))
        near = to_core(first, ring_a.found[5:9], layout, n_own)
        ring_b.step()
        skip_full, time_a_full = first.run()
        ring_b.step(skip_full)

        def block_rows(ring, shape):
            gather = Gather(index)
            out = gather.out(*shape)
            for k, row, piece in ring.found:
                gather.add(piece, k, [(0, piece.shape[0], out, 0, width // 8, 0, 0, row)])
            return gather.run()[0]

    else:
        first_far, second_far, time_far = swap(first_in, 2), swap(second_in, 2), swap(time_act, 2)
        skip_full, time_a_full, time_b_full, out_full = (
            lax.all_gather(w, ("dp", "seq"), axis=0, tiled=True)
            for w in (skip_weight, time_a, time_b, out_weight)
        )
        triple_full, up_full = (
            lax.all_gather(
                jnp.concatenate(by_place(exchange(by_place(parts, me)), me), axis=0),
                "dp",
                axis=0,
                tiled=True,
            )
            for parts in (triple, upper_w)
        )
        down_full = lax.all_gather(down_weight, "dp", axis=0, tiled=True)
        out_sides = [half(out_full, core), half(out_full, 1 - core)]
        time_b_sides = [half(time_b_full, core), half(time_b_full, 1 - core)]

    base = dot_nn(joined, skip_full)
    shift_a, scale_a = jnp.split(dot_nn(time_act, time_a_full), 2, axis=1)
    normed_a, inverse_a = norm_rows(base)
    hidden_own = (normed_a * (1.0 + scale_a) + shift_a).astype(bf16)
    if ringed:
        hidden_own = after(hidden_own, second_far)
        ring_c.step(skip_full)
        ring_b.step(hidden_own)
        ring_b.step()
        ring_c.step(*ring_b.found[5][2:])
        ring_c.step(*ring_b.front)
        hidden_a = spread(hidden_own, ring_b.front)
        first_far = swap(after(first_in, hidden_a[2]), 2)
        wide = block_rows(ring_b, (width, cut[0]))
        triple_full = wide[:, : 3 * local]
        out_mine = wide[:, 3 * local :]
        out_sides = [out_mine, swap(after(out_mine, hidden_a[3]), 1)]
        ring_d.step(hidden_a[2])
    else:
        hidden_a = spread(hidden_own)
    qkv = [dot_nn(h, triple_full).astype(bf16) for h in hidden_a]
    att, logsum, query_rot, key_rot = attend(qkv, *tables)
    time_act_b = after(time_act, att)
    if ringed:
        att = after(att, *ring_c.front, *ring_d.front)
    att = after(att, first_far)
    att_parts = [att[j * frames : (j + 1) * frames] for j in range(4)]
    attended = exchange(att_parts)
    if ringed:
        ring_c.step(att)
        mine = block_rows(ring_c, (width, 3 * width // 2))
        time_b_sides = [mine, swap(mine, 1)]
        ring_d.step(*attended)
    shift_b, scale_b, gate_b = jnp.split(
        merge(dot_nn(time_act_b, time_b_sides[0]), dot_nn(time_act_b, time_b_sides[1]), core),
        3,
        axis=1,
    )
    upstream = cotangent.reshape(frames, width).astype(f32)
    ffn_grad = (upstream * gate_b).astype(bf16)
    attended = list(after(tuple(attended), ffn_grad))
    ffn_grad = spread(ffn_grad)
    attended = jnp.concatenate(by_place(attended, me), axis=1)
    middle = base + merge(dot_nn(attended, out_sides[0]), dot_nn(attended, out_sides[1]), core)
    normed_b, inverse_b = norm_rows(middle)

    hidden_own = (normed_b * (1.0 + scale_b) + shift_b).astype(bf16)
    if ringed:
        ring_d.step(hidden_own)
        ring_d.step()
    hidden_b = spread(hidden_own, (), ffn_grad[2])
    if ringed:
        ffn_full = block_rows(ring_d, (width, 2 * local_hidden))
        up_full, down_full = ffn_full[:, :local_hidden], ffn_full[:, local_hidden:]
    row_near = swap(after(row_own, hidden_b[3]), 1)
    row_far = jnp.concatenate([first_far, second_far, time_far], axis=1)
    row_inputs = [row_own, row_near, row_far, swap(after(row_far, hidden_b[3]), 1)]
    hb = [jnp.concatenate(hidden_b[:2]), jnp.concatenate(hidden_b[2:])]
    fg = [jnp.concatenate(ffn_grad[:2]), jnp.concatenate(ffn_grad[2:])]
    upper = dot_nn(hb[1], up_full)
    acted_far = gelu_value(upper).astype(bf16)
    part_far = dot_nn(acted_far, down_full)
    part_low = part_far.astype(bf16)
    fg[1] = after(fg[1], part_low)
    ug_far = (dot_nt(fg[1], down_full) * gelu_slope(upper)).astype(bf16)
    part_sent = (part_far[:frames] + swap(part_low[frames:], 1).astype(f32)).astype(bf16)
    far = dot_nt(after(ug_far, part_sent), up_full)
    far_low = far.astype(bf16)
    hb[0] = after(hb[0], far_low)
    upper = dot_nn(hb[0], up_full)
    sent = (far[:frames] + swap(far_low[frames:], 1).astype(f32)).astype(bf16)
    fg[0] = after(fg[0], sent)
    grad_far = swap(sent, 2)
    acted = [gelu_value(upper).astype(bf16), acted_far]
    ug = [(dot_nt(fg[0], down_full) * gelu_slope(upper)).astype(bf16), ug_far]
    own = dot_nt(ug[0], up_full)
    hidden_b_grad = (
        own[:frames] + swap(own[frames:].astype(bf16), 1).astype(f32) + grad_far.astype(f32)
    )
    acted, fg, ug, hb = after((acted, fg, ug, hb), own, row_near, row_inputs[3])
    part = dot_nn(acted[0], down_full)
    ffn = (
        part[:frames]
        + swap(part[frames:].astype(bf16), 1).astype(f32)
        + swap(after(part_sent, grad_far), 2).astype(f32)
    )
    grad_down = dot_tn(acted[0], fg[0]) + dot_tn(acted[1], fg[1])
    grad_up = dot_tn(hb[0], ug[0]) + dot_tn(hb[1], ug[1])
    grad_ffn = jnp.concatenate([grad_up.astype(bf16), grad_down.astype(bf16)], axis=1)
    hidden_b_grad = after(hidden_b_grad, grad_ffn, part)
    ffn_sum = lax.psum_scatter(grad_ffn, "dp", scatter_dimension=0, tiled=True).astype(f32)

    scale_b_grad = hidden_b_grad * normed_b
    middle_grad = upstream + norm_back(hidden_b_grad * (1.0 + scale_b), normed_b, inverse_b)
    branch_grad = middle_grad.astype(bf16)
    branch_sides = [half(branch_grad, core), half(branch_grad, 1 - core)]
    attended_grad = (
        dot_nt(branch_sides[0], out_sides[0]) + dot_nt(branch_sides[1], out_sides[1])
    ).astype(bf16)
    att_grad_parts = by_place([attended_grad[:, t * local : (t + 1) * local] for t in range(4)], me)
    att_grad = exchange(att_grad_parts)
    def to_columns(grads):
        return [
            jnp.concatenate([g[:, t * local : (t + 1) * local] for g in grads], axis=1) for t in range(4)
        ]

    ffn = after(ffn, *att_grad_parts)
    output = (middle + gate_b * ffn).astype(bf16).reshape(rows, frames, width)
    modul_b_grad = [v.astype(bf16) for v in (hidden_b_grad, scale_b_grad, upstream * ffn)]
    modul_sent = by_place(to_columns(modul_b_grad), me)
    modul_b_parts = exchange(modul_sent)
    grad_out = [dot_tn(attended, side).astype(bf16) for side in branch_sides]
    near_out = swap(grad_out[1], 1)
    att_grad = after(tuple(att_grad), *modul_sent, *grad_out, row_inputs[3])
    triple_grad = attend_back(att_grad, qkv, query_rot, key_rot, att, logsum, *tables)
    triple_grad = after(triple_grad, *modul_b_parts, near_out)
    back = dot_nt(triple_grad, triple_full)
    far_low = back[3 * frames :].astype(bf16)
    hidden_a_all = jnp.concatenate(hidden_a)
    sent = (back[2 * frames : 3 * frames] + swap(far_low, 1).astype(f32)).astype(bf16)
    hidden_a_grad = (
        back[:frames]
        + swap(back[frames : 2 * frames].astype(bf16), 1).astype(f32)
        + swap(sent, 2).astype(f32)
    )
    triple_grad, modul_b_grad, hidden_a_all = after(
        (triple_grad, tuple(modul_b_grad), hidden_a_all), sent
    )
    grad_triple = dot_tn(hidden_a_all, triple_grad).astype(bf16)
    modul_b_parts = after(tuple(modul_b_parts), sent, grad_triple)
    grad_time_b = sum(dot_tn(v[:, 2 * width :], g) for v, g in zip(row_inputs, modul_b_parts))
    grad_out = (grad_out[0].astype(f32) + near_out.astype(f32)).astype(bf16)
    ring_w = RingSum(
        [by_dp(g, groups) for g in (grad_time_b.astype(bf16), grad_out, grad_triple)], index, ringed
    )
    ring_w.step()
    modul_b_grad = jnp.concatenate(modul_b_grad, axis=1)
    time_back_b = dot_nt(half(modul_b_grad, core), time_b_sides[0]) + dot_nt(
        half(modul_b_grad, 1 - core), time_b_sides[1]
    )
    hidden_a_grad = after(hidden_a_grad, time_back_b)

    scale_a_grad = hidden_a_grad * normed_a
    modul_a_grad = jnp.concatenate([hidden_a_grad, scale_a_grad], axis=1).astype(bf16)
    modul_sent = by_place(to_columns([modul_a_grad[:, :width], modul_a_grad[:, width:]]), me)
    modul_parts = exchange(modul_sent)
    base_grad = (
        middle_grad + norm_back(hidden_a_grad * (1.0 + scale_a), normed_a, inverse_a)
    ).astype(bf16)
    base_sent = by_place([base_grad[:, t * local : (t + 1) * local] for t in range(4)], me)
    base_parts = exchange(base_sent)
    step = ring_w.step(*modul_sent)
    base_grad, modul_a_grad = after((base_grad, modul_a_grad), *base_sent)
    joined_grad = dot_nt(base_grad, skip_full)
    time_back = dot_nt(modul_a_grad, time_a_full) + time_back_b
    time_grad = (time_back * silu_slope(time_value)).reshape(rows, frames, width)
    modul_parts = after(tuple(modul_parts), joined_grad, *step)
    ring_w.step()
    grad_time_a = sum(dot_tn(v[:, 2 * width :], g) for v, g in zip(row_inputs, modul_parts))
    grad_skip = sum(dot_tn(v[:, : 2 * width], g) for v, g in zip(row_inputs, base_parts))
    rows_skip = n_skip // 2
    grad_skip = grad_skip.reshape(groups, 4, 2, rows_skip, local)
    grad_skip = jnp.concatenate([grad_skip[:, :, 0], grad_skip[:, :, 1]], axis=3)
    ring_l = RingSum(
        [
            grad_skip.reshape(groups, 4 * rows_skip, 2 * local).astype(bf16),
            by_dp(grad_time_a.astype(bf16), groups),
        ],
        index,
        ringed,
    )
    ring_l.step()
    ring_w.step(grad_skip)
    ring_l.step()
    wide_sum = ring_w.total()
    ring_l.step(wide_sum)
    parts = finish(jnp.concatenate([ffn_sum[:, :local_hidden], wide_sum], axis=1), me)
    ring_l.step(*parts)
    up_sum = jnp.concatenate(
        [
            p[:, g * hidden_block : (g + 1) * hidden_block]
            for g in range(groups)
            for p in parts
        ],
        axis=1,
    )
    split = local_hidden + 3 * local, local_hidden + 3 * local + width // 2
    by_blocks = lambda parts, start, i: jnp.concatenate(
        [p[:, start + i * local : start + (i + 1) * local] for p in parts], axis=1
    ).astype(f32)
    out_sum = halves_sum([p[:, split[0] : split[1]] for p in parts])
    triples = [
        jnp.concatenate(
            [
                p[:, split[1] + i * 128 + q * 384 : split[1] + (i + 1) * 128 + q * 384]
                for p in parts
                for q in range(2)
            ],
            axis=1,
        ).astype(f32)
        for i in range(3)
    ]
    last = finish(ring_l.total(), me)
    columns = [by_blocks(last, 0, i) for i in range(4)]
    time_b_sum = jnp.concatenate([by_blocks(parts, local_hidden, i) for i in range(3)], axis=1)
    skip_sum = jnp.concatenate(columns[:2], axis=0)
    time_a_sum = jnp.concatenate(columns[2:4], axis=1)
    return (
        output,
        joined_grad[:, :width].reshape(rows, frames, width),
        joined_grad[:, width:].reshape(rows, frames, width),
        time_grad,
        skip_sum,
        jnp.concatenate([time_a_sum, time_b_sum], axis=1),
        *triples,
        out_sum,
        up_sum.astype(f32),
        ffn_sum[:, local_hidden:],
    )


def solution(mesh):
    frames = P("dp", "seq", None)
    marks = P("dp", "seq")
    weight = P(("dp", "seq"), None)
    return jax.shard_map(
        on_device,
        mesh=mesh,
        in_specs=(frames,) * 3 + (marks,) * 3 + (weight,) * 8 + (frames,),
        out_specs=(frames,) * 4 + (weight,) * 8,
        check_vma=False,
    )
```
